32 devices in a mesh: dp: 8 (over y, x, core), tensor: 4 (over z).
Axes of the slice: x: 2, y: 2, z: 4, core: 2. Of those that a mesh axis runs over, the one named last changes fastest.
Arguments:
- stream_in: bfloat16 [16384, 768], P(('dp', 'tensor')), may hold values from -6 to 6
- patch_size: int32 [16], P('dp'), may hold values from 8 to 10, as said below
- norm_gain: bfloat16 [2, 2, 768], replicated, may hold values from 0.25 to 1.75
- norm_bias: bfloat16 [2, 2, 768], replicated, may hold values from -2 to 2
- input_weight: bfloat16 [2, 3, 768, 768], P(None, None, None, 'tensor'), may hold values from -0.21875 to 0.21875
- input_bias: bfloat16 [2, 2, 768], P(None, None, 'tensor'), may hold values from -3 to 3
- output_weight: bfloat16 [2, 768, 768], P(None, 'tensor'), may hold values from -0.625 to 0.625
- output_bias: bfloat16 [2, 768], replicated, may hold values from -3 to 3
- up_weight: bfloat16 [2, 768, 3072], P(None, None, 'tensor'), may hold values from -0.21875 to 0.21875
- up_bias: bfloat16 [2, 3072], P(None, 'tensor'), may hold values from -3 to 3
- down_weight: bfloat16 [2, 3072, 768], P(None, 'tensor'), may hold values from -0.109375 to 0.109375
- down_bias: bfloat16 [2, 768], replicated, may hold values from -3 to 3
- cotangent: bfloat16 [16384, 768], P(('dp', 'tensor')), may hold values from -6 to 6
Outputs:
- layer_out: bfloat16 [16384, 768], P(('dp', 'tensor'))
- grad_in: float32 [16384, 768], P(('dp', 'tensor'))
- norm_gain_grad: float32 [2, 2, 768], replicated
- norm_bias_grad: float32 [2, 2, 768], replicated
- input_weight_grad: float32 [2, 3, 768, 768], P(None, None, None, 'tensor')
- input_bias_grad: float32 [2, 2, 768], P(None, None, 'tensor')
- output_weight_grad: float32 [2, 768, 768], P(None, 'tensor')
- output_bias_grad: float32 [2, 768], replicated
- up_weight_grad: float32 [2, 768, 3072], P(None, None, 'tensor')
- up_bias_grad: float32 [2, 3072], P(None, 'tensor')
- down_weight_grad: float32 [2, 3072, 768], P(None, 'tensor')
- down_bias_grad: float32 [2, 768], replicated
The draws below stay inside these ranges and needn't reach their ends.
Inputs may be any that keep to these rules, and one draw needn't show every extreme that they name: `patch_size`: every entry is 8 or 10, and both occur in every draw.
All inputs are finite; a program needn't handle non-finite values.
Results may differ from the reference program's by a relative error of at most 0.015.
Values may be sent and summed in bfloat16 or wider, within the bound.
No kernel may reach another device: no remote copies, remote signals or barrier semaphores. Data moves between devices by JAX's collectives and lax.ppermute only.
A program may use at most 192 MiB of HBM per device.

```python
import jax
import jax.numpy as jnp
from jax import lax

D = 768
HEADS = 12
HD = 64
FF = 3072
LAYERS = 2
ROWS = 1024
IMAGE = 240
BUFFERS = 16
TOKENS = 16384


def draw_patch_size(key, part):
    key = jax.random.fold_in(key, 11)
    pick_key, order_key = jax.random.split(key)
    sizes = 8 + 2 * jax.random.randint(pick_key, (BUFFERS,), 0, 2)
    order = jax.random.permutation(order_key, BUFFERS)
    sizes = sizes.at[order[0]].set(8).at[order[1]].set(10)
    return sizes.astype(jnp.int32)


def level_of(rng, shape, pieces, low, top_value):
    def one(dim, parts):
        heights = jax.random.uniform(jax.random.fold_in(jax.random.fold_in(rng, 6), dim), (parts,), jnp.float32, low / len(pieces), top_value / len(pieces))
        return jnp.repeat(jnp.exp(heights), shape[dim] // parts).reshape((-1,) + (1,) * (len(shape) - dim - 1))

    loudness = one(*pieces[0])
    for cut in pieces[1:]:
        loudness = loudness * one(*cut)
    return loudness


def normal_values(key, shape, spread, bound, shards=(), kind=jnp.bfloat16):
    loudness = level_of(key, shape, shards, -0.22, 0.18) if shards else 1.0
    entries = jax.random.normal(key, shape, jnp.float32) * spread * loudness
    return jnp.minimum(jnp.maximum(entries, -bound), bound).astype(kind)


def setup_inputs(seed: int = 0) -> dict:
    key_list = jax.random.split(jax.random.key(seed), 14)
    stream_in = normal_values(key_list[0], (TOKENS, D), 1.0, 6.0, ((0, 32),))
    patch_size = draw_patch_size(jax.random.fold_in(key_list[13], 71), 0)
    norm_gain = jnp.clip(1.0 + 0.15 * jax.random.normal(key_list[2], (LAYERS, 2, D), jnp.float32), 0.25, 1.75).astype(jnp.bfloat16)
    norm_bias = normal_values(key_list[3], (LAYERS, 2, D), 0.3, 2.0)
    input_weight = normal_values(key_list[4], (LAYERS, 3, D, D), D ** -0.5, 0.21875, ((3, 4),))
    input_bias = normal_values(key_list[5], (LAYERS, 2, D), 0.5, 3.0, ((2, 4),))
    output_weight = normal_values(key_list[6], (LAYERS, D, D), (D // 8) ** -0.5, 0.625, ((1, 4),))
    output_bias = normal_values(key_list[7], (LAYERS, D), 0.5, 3.0)
    up_weight = normal_values(key_list[8], (LAYERS, D, FF), D ** -0.5, 0.21875, ((2, 4),))
    up_bias = normal_values(key_list[9], (LAYERS, FF), 0.5, 3.0, ((1, 4),))
    down_weight = normal_values(key_list[10], (LAYERS, FF, D), FF ** -0.5, 0.109375, ((1, 4),))
    down_bias = normal_values(key_list[11], (LAYERS, D), 0.5, 3.0)
    cotangent = normal_values(key_list[12], (TOKENS, D), 1.0, 6.0, ((0, 32),))
    return {"stream_in": stream_in, "patch_size": patch_size, "norm_gain": norm_gain, "norm_bias": norm_bias, "input_weight": input_weight, "input_bias": input_bias, "output_weight": output_weight, "output_bias": output_bias, "up_weight": up_weight, "up_bias": up_bias, "down_weight": down_weight, "down_bias": down_bias, "cotangent": cotangent}


highest = lax.Precision.HIGHEST
epsilon = 1e-06
masked_score = -1e+30

@jax.custom_vjp
def low(v):
    return lax.optimization_barrier(v.astype(jnp.bfloat16)).astype(jnp.float32)

@jax.custom_vjp
def low_back(v):
    return v

def low_keep(v):
    return (low(v), None)

def low_pass(kept, grad):
    return (grad,)

def back_keep(v):
    return (v, None)

def back_low(kept, grad):
    return (low(grad),)
low.defvjp(low_keep, low_pass)
low_back.defvjp(back_keep, back_low)

def matmul(left, right):
    return jnp.dot(left, right, precision=highest, preferred_element_type=jnp.float32)

def normalize(values, gain_row, bias_row):
    average = lax.optimization_barrier(jnp.mean(values, axis=-1, keepdims=True))
    centred = values - average
    variance = lax.optimization_barrier(jnp.mean(centred * centred, axis=-1, keepdims=True))
    return centred * lax.rsqrt(variance + epsilon) * gain_row + bias_row

def attend(queries, keys_in, values_in, valid_count):
    score_scale = HD ** (-0.5)
    scores = jnp.einsum('qhe,khe->hqk', queries, keys_in, precision=highest) * score_scale
    key_index = jnp.arange(ROWS, dtype=jnp.int32)
    scores = jnp.where(key_index[None, None, :] < valid_count, scores, masked_score)
    scores = low_back(scores)
    row_top = lax.optimization_barrier(jnp.max(scores, axis=-1, keepdims=True))
    weights = jnp.exp(scores - row_top)
    softmax_probs = weights / lax.optimization_barrier(jnp.sum(weights, axis=-1, keepdims=True))
    return jnp.einsum('hqk,khe->qhe', low(softmax_probs), values_in, precision=highest)

def residual_block(stream, valid_count, weights_all, layer_idx):
    norm_gain, norm_bias, input_weight, input_bias, output_weight, output_bias, up_weight, up_bias, down_weight, down_bias = weights_all
    normed = low(normalize(stream, norm_gain[layer_idx, 0], norm_bias[layer_idx, 0]))
    queries = low_back(low(matmul(normed, input_weight[layer_idx, 0]) + input_bias[layer_idx, 0]))
    keys_rows = low_back(low(matmul(normed, input_weight[layer_idx, 1])))
    values_rows = low_back(low(matmul(normed, input_weight[layer_idx, 2]) + input_bias[layer_idx, 1]))
    heads_shape = (ROWS, HEADS, HD)
    mixed_rows = attend(queries.reshape(heads_shape), keys_rows.reshape(heads_shape), values_rows.reshape(heads_shape), valid_count).reshape(ROWS, D)
    mixed_rows = low_back(low(mixed_rows))
    middle = stream + low_back(matmul(mixed_rows, output_weight[layer_idx]) + output_bias[layer_idx])
    normed_two = low(normalize(middle, norm_gain[layer_idx, 1], norm_bias[layer_idx, 1]))
    hidden_pre = low_back(matmul(normed_two, up_weight[layer_idx]) + up_bias[layer_idx])
    activated = low(jax.nn.gelu(hidden_pre, approximate=False))
    return middle + low_back(matmul(activated, down_weight[layer_idx]) + down_bias[layer_idx])

def forward(stream_all, weights_all, valid_all):
    buffers = stream_all.reshape(BUFFERS, ROWS, D)

    def one_buffer(buffer_pair):
        stream, valid_count = buffer_pair
        for layer_idx in range(LAYERS):
            stream = residual_block(stream, valid_count, weights_all, layer_idx)
        return stream
    results = lax.map(jax.checkpoint(one_buffer), (buffers, valid_all))
    return results.reshape(TOKENS, D)

def reference(stream_in, patch_size, norm_gain, norm_bias, input_weight, input_bias, output_weight, output_bias, up_weight, up_bias, down_weight, down_bias, cotangent):
    grid_side = IMAGE // patch_size
    valid_all = (grid_side * grid_side).astype(jnp.int32)
    positions = jnp.arange(ROWS, dtype=jnp.int32)
    row_mask = (positions[None, :] < valid_all[:, None]).astype(jnp.float32).reshape(TOKENS, 1)
    weights_all = (norm_gain.astype(jnp.float32), norm_bias.astype(jnp.float32), input_weight.astype(jnp.float32), input_bias.astype(jnp.float32), output_weight.astype(jnp.float32), output_bias.astype(jnp.float32), up_weight.astype(jnp.float32), up_bias.astype(jnp.float32), down_weight.astype(jnp.float32), down_bias.astype(jnp.float32))

    def run_forward(stream, weights):
        return forward(stream, weights, valid_all)
    layer_out, pullback = jax.vjp(run_forward, stream_in.astype(jnp.float32), weights_all)
    grad_in, weight_grads = pullback(cotangent.astype(jnp.float32) * row_mask)
    return (layer_out.astype(jnp.bfloat16), grad_in, weight_grads[0], weight_grads[1], weight_grads[2], weight_grads[3], weight_grads[4], weight_grads[5], weight_grads[6], weight_grads[7], weight_grads[8], weight_grads[9])
```

```python
import functools

import jax
import jax.numpy as jnp
from jax import lax
from jax.experimental import pallas as pl
from jax.experimental.pallas import tpu as pltpu
from jax.sharding import Mesh, PartitionSpec as P

HD = 64
ROWS = 1024
IMAGE = 240

epsilon = 1e-06
masked_score = -1e30
bf16 = jnp.bfloat16
f32 = jnp.float32


def dot(left, right, contract):
    return lax.dot_general(
        left, right, ((contract[:1], contract[1:]), ((), ())), preferred_element_type=f32
    )


def normalize(values, gain_row, bias_row):
    average = jnp.mean(values, axis=-1, keepdims=True)
    centred = values - average
    variance = jnp.mean(centred * centred, axis=-1, keepdims=True)
    return centred * lax.rsqrt(variance + epsilon) * gain_row + bias_row


def gelu_exact(values):
    return jax.nn.gelu(values, approximate=False)


def key_halves(core, own, received):
    first = jnp.where(core == 0, own, received)
    second = jnp.where(core == 0, received, own)
    return first, second


def attend_forward_kernel(info, queries, kv_own, kv_other, mixed, log_total):
    core, valid = info[0], info[1]
    width = queries.shape[0]
    half = kv_own.shape[1]
    key_place = lax.broadcasted_iota(jnp.int32, (half, 1), 0) + half
    key_bias = jnp.where(key_place < valid, 0.0, masked_score).astype(f32)
    for head in range(width // HD):
        rows = slice(head * HD, (head + 1) * HD)
        value_rows = slice(width + head * HD, width + (head + 1) * HD)
        query = queries[rows, :] * jnp.asarray(HD**-0.5, bf16)
        key_one, key_two = key_halves(core, kv_own[rows, :], kv_other[rows, :])
        value_one, value_two = key_halves(core, kv_own[value_rows, :], kv_other[value_rows, :])
        score_one = dot(key_one, query, (0, 0))
        score_two = dot(key_two, query, (0, 0)) + key_bias
        top = jnp.maximum(
            jnp.max(score_one, axis=0, keepdims=True), jnp.max(score_two, axis=0, keepdims=True)
        )
        weight_one = jnp.exp(score_one - top)
        weight_two = jnp.exp(score_two - top)
        total = jnp.sum(weight_one, axis=0, keepdims=True) + jnp.sum(
            weight_two, axis=0, keepdims=True
        )
        out = dot(value_one, weight_one.astype(bf16), (1, 0)) + dot(
            value_two, weight_two.astype(bf16), (1, 0)
        )
        mixed[rows, :] = (out / total).astype(bf16)
        log_total[0, head : head + 1, :] = top + jnp.log(total)


def attend_backward_kernel(
    info, queries, kv_own, kv_other, mixed, log_total, grad_mixed, grad_q, grad_own, grad_other
):
    core, valid = info[0], info[1]
    width = queries.shape[0]
    half = kv_own.shape[1]
    scale = HD**-0.5
    key_place = lax.broadcasted_iota(jnp.int32, (half, 1), 0) + half
    key_bias = jnp.where(key_place < valid, 0.0, masked_score).astype(f32)
    for head in range(width // HD):
        rows = slice(head * HD, (head + 1) * HD)
        value_rows = slice(width + head * HD, width + (head + 1) * HD)
        query = queries[rows, :] * jnp.asarray(scale, bf16)
        grad_out = grad_mixed[rows, :]
        delta = jnp.sum(
            grad_out.astype(f32) * mixed[rows, :].astype(f32), axis=0, keepdims=True
        )
        log_row = log_total[0, head : head + 1, :]
        keys = key_halves(core, kv_own[rows, :], kv_other[rows, :])
        values = key_halves(core, kv_own[value_rows, :], kv_other[value_rows, :])
        grad_query = None
        grad_keys = []
        grad_values = []
        for part in range(2):
            score = dot(keys[part], query, (0, 0))
            if part == 1:
                score = score + key_bias
            probs = jnp.exp(score - log_row)
            grad_values.append(dot(grad_out, probs.astype(bf16), (1, 1)))
            grad_probs = dot(values[part], grad_out, (0, 0))
            grad_score = (probs * (grad_probs - delta)).astype(bf16)
            term = dot(keys[part], grad_score, (1, 0))
            grad_query = term if grad_query is None else grad_query + term
            grad_keys.append(dot(query, grad_score, (1, 1)))
        grad_q[rows, :] = (grad_query * scale).astype(bf16)
        own, other = key_halves(core, *grad_keys)
        grad_own[rows, :] = own
        grad_other[rows, :] = other.astype(bf16)
        own, other = key_halves(core, *grad_values)
        grad_own[value_rows, :] = own
        grad_other[value_rows, :] = other.astype(bf16)


def attention_specs(groups, width, half):
    return dict(
        q=pl.BlockSpec((width, half), lambda g, info: (g, 0)),
        kv=pl.BlockSpec((2 * width, half), lambda g, info: (g, 0)),
        log=pl.BlockSpec((1, 8, half), lambda g, info: (g, 0, 0)),
    )


def attend_forward(info, queries, kv_own, kv_other, groups):
    features, half = queries.shape
    width = features // groups
    specs = attention_specs(groups, width, half)
    return pl.pallas_call(
        attend_forward_kernel,
        grid_spec=pltpu.PrefetchScalarGridSpec(
            num_scalar_prefetch=1,
            grid=(groups,),
            in_specs=[specs["q"], specs["kv"], specs["kv"]],
            out_specs=[specs["q"], specs["log"]],
        ),
        out_shape=[
            jax.ShapeDtypeStruct((features, half), bf16),
            jax.ShapeDtypeStruct((groups, 8, half), f32),
        ],
        compiler_params=pltpu.CompilerParams(vmem_limit_bytes=40 << 20),
        cost_estimate=pl.CostEstimate(
            flops=16 * features * half * 2 * half,
            bytes_accessed=12 * features * half,
            transcendentals=features // HD * half * 2 * half,
        ),
        name="attend_forward",
    )(info, queries, kv_own, kv_other)


def attend_backward(info, queries, kv_own, kv_other, mixed, log_total, grad_mixed, groups):
    features, half = queries.shape
    width = features // groups
    specs = attention_specs(groups, width, half)
    return pl.pallas_call(
        attend_backward_kernel,
        grid_spec=pltpu.PrefetchScalarGridSpec(
            num_scalar_prefetch=1,
            grid=(groups,),
            in_specs=[specs["q"], specs["kv"], specs["kv"], specs["q"], specs["log"], specs["q"]],
            out_specs=[specs["q"], specs["kv"], specs["kv"]],
        ),
        out_shape=[
            jax.ShapeDtypeStruct((features, half), bf16),
            jax.ShapeDtypeStruct((2 * features, half), f32),
            jax.ShapeDtypeStruct((2 * features, half), bf16),
        ],
        compiler_params=pltpu.CompilerParams(vmem_limit_bytes=40 << 20),
        cost_estimate=pl.CostEstimate(
            flops=40 * features * half * 2 * half,
            bytes_accessed=26 * features * half,
            transcendentals=features // HD * half * 2 * half,
        ),
        name="attend_backward",
    )(info, queries, kv_own, kv_other, mixed, log_total, grad_mixed)


flip_pair = [(0, 1), (1, 0)]


def over(axis, array):
    return lax.ppermute(array, axis, flip_pair)


def z_send(array, pairs):
    return lax.ppermute(array, "z", pairs)


inner_pairs = [(1, 2), (2, 1)]
outward_pairs = [(1, 0), (2, 3)]
inward_pairs = [(0, 1), (3, 2)]
near_pairs = [(0, 1), (1, 0), (2, 3), (3, 2)]


def gather_z(block):
    near = z_send(block, near_pairs)
    cross = z_send(block, inner_pairs)
    relay_one = z_send(cross, outward_pairs)
    cross_two = z_send(near, inner_pairs)
    relay_two = z_send(cross_two, outward_pairs)
    at_end = (lax.axis_index("z") == 0) | (lax.axis_index("z") == 3)
    return [
        block,
        near,
        jnp.where(at_end, relay_one, cross_two),
        jnp.where(at_end, relay_two, cross),
    ]


def add_low(kept, received):
    return (kept.astype(f32) + received.astype(f32)).astype(bf16)


def scatter_z(near, far):
    received = z_send(far, inward_pairs)
    far = add_low(far, received[::-1])
    received = z_send(far, inner_pairs)
    near = add_low(near, received[::-1])
    received = z_send(near[1], near_pairs)
    return add_low(near[0], received)


def flip_if(bit, array, axis):
    return jnp.where(bit == 1, jnp.flip(array, axis), array)


def paired(bit, own, received, axis):
    return jnp.stack(
        [jnp.where(bit == 0, own, received), jnp.where(bit == 0, received, own)], axis=axis
    )


def local(
    stream_in,
    patch_size,
    norm_gain,
    norm_bias,
    input_weight,
    input_bias,
    output_weight,
    output_bias,
    up_weight,
    up_bias,
    down_weight,
    down_bias,
    cotangent,
):
    half, width_all = stream_in.shape
    layer_count = input_weight.shape[0]
    shard = input_weight.shape[-1]
    unit_shard = up_weight.shape[-1]
    unit_slice = unit_shard // 8
    groups = lax.axis_size("z")
    outer = lax.axis_size("o")
    core, x_bit, y_bit = lax.axis_index("c"), lax.axis_index("x"), lax.axis_index("y")
    z_place = lax.axis_index("z")
    z_low, z_high = z_place % 2, z_place // 2

    swap = []
    for c in range(2):
        for z in range(groups):
            swap.append((c * groups + z, (z % 2) * groups + (z - z % 2 + c)))

    def swap_rows(array):
        return lax.ppermute(array, ("c", "z"), swap)

    other_patch = over("c", patch_size)
    patch = jnp.where(z_low == core, patch_size, other_patch)
    patch = jnp.where(z_high == 0, patch[0], patch[1])
    grid_side = IMAGE // patch
    valid = grid_side * grid_side
    info = jnp.stack([core, valid]).astype(jnp.int32)

    stream_rows = swap_rows(stream_in)

    up_bias_all = lax.all_gather(up_bias, "z", axis=0)
    input_bias_all = lax.all_gather(input_bias, "z", axis=0)

    def z_order(array):
        pairs = array.reshape((2, 2) + array.shape[1:])
        pairs = flip_if(z_high, flip_if(z_low, pairs, 1), 0)
        return pairs.reshape(array.shape)

    up_bias_all = z_order(up_bias_all).astype(f32)
    input_bias_all = z_order(input_bias_all).astype(f32)

    def unit_order(rows):
        cut = rows.reshape(2, 2, 2, 2, 2, unit_slice)
        cut = flip_if(y_bit, flip_if(x_bit, flip_if(core, cut, 4), 3), 2)
        one = cut[0].transpose(3, 1, 2, 0, 4)
        two = cut[1].transpose(3, 2, 1, 0, 4)
        return jnp.stack([one, two]).reshape(4, unit_shard)

    def unit_order_back(pieces):
        cut = pieces.reshape(2, 2, 2, 2, 2, unit_slice)
        one = cut[0].transpose(3, 1, 2, 0, 4)
        two = cut[1].transpose(3, 2, 1, 0, 4)
        cut = jnp.stack([one, two])
        cut = flip_if(y_bit, flip_if(x_bit, flip_if(core, cut, 4), 3), 2)
        return z_order(cut.reshape(4, unit_shard))

    slice_index = (y_bit * 2 + x_bit) * 2 + core

    def gather_attention(layer_idx):
        kinds = jnp.swapaxes(input_weight[layer_idx], 1, 2)
        kept = jnp.where(
            core == 0,
            jnp.stack([kinds[1], kinds[2]]),
            jnp.stack([kinds[0], output_weight[layer_idx]]),
        )
        blocks = jnp.stack(gather_z(kept))
        received = over("c", blocks)
        kv = jnp.where(core == 0, blocks, received)
        qo = jnp.where(core == 0, received, blocks)
        return (
            kv.reshape(2 * groups * shard, width_all),
            qo[:, 0].reshape(groups * shard, width_all),
            qo[:, 1].reshape(groups * shard, width_all),
        )

    def gather_units(layer_idx):
        up = lax.dynamic_slice_in_dim(
            up_weight[layer_idx], slice_index * unit_slice, unit_slice, axis=1
        )
        down = lax.dynamic_slice_in_dim(
            down_weight[layer_idx], slice_index * unit_slice, unit_slice, axis=0
        )
        blocks = gather_z(jnp.stack([up.T, down]))
        one = jnp.concatenate(blocks[:2], axis=1)
        two = jnp.concatenate(blocks[2:], axis=1)
        one = jnp.concatenate([one, over("x", one)], axis=1)
        two = jnp.concatenate([two, over("y", two)], axis=1)
        one = jnp.concatenate([one, over("y", one)], axis=1)
        two = jnp.concatenate([two, over("x", two)], axis=1)
        pieces = [one, over("c", one), two, over("c", two)]
        return [piece[0] for piece in pieces], [piece[1] for piece in pieces]

    attention_weights = [gather_attention(0)]
    unit_weights = [gather_units(0)]
    for layer_idx in range(1, layer_count):
        attention_weights.append(gather_attention(layer_idx))
        unit_weights.append(gather_units(layer_idx))

    cotangent_rows = swap_rows(cotangent)
    gains = norm_gain.astype(f32)
    shifts = norm_bias.astype(f32)

    stream = stream_rows.astype(f32)
    saved = []
    for layer_idx in range(layer_count):
        weight_kv, weight_q, weight_o = attention_weights[layer_idx]
        up_pieces, down_pieces = unit_weights[layer_idx]
        layer_input = stream
        normed = normalize(stream, gains[layer_idx, 0], shifts[layer_idx, 0]).astype(bf16)
        value_bias = input_bias_all[:, layer_idx, 1]
        kv_bias = jnp.stack([jnp.zeros_like(value_bias), value_bias], axis=1).reshape(-1, 1)
        kv_own = (dot(weight_kv, normed, (1, 1)) + kv_bias).astype(bf16)
        kv_other = over("c", kv_own)
        query_bias = input_bias_all[:, layer_idx, 0].reshape(-1, 1)
        queries = (dot(weight_q, normed, (1, 1)) + query_bias).astype(bf16)
        mixed, log_total = attend_forward(info, queries, kv_own, kv_other, groups)
        middle = stream + (
            dot(mixed, weight_o, (0, 0)) + output_bias[layer_idx].astype(f32)
        )
        normed_two = normalize(middle, gains[layer_idx, 1], shifts[layer_idx, 1]).astype(bf16)
        unit_bias = unit_order(up_bias_all[:, layer_idx])
        hidden = []
        activated = []
        branch = None
        for piece in range(4):
            pre = dot(normed_two, up_pieces[piece], (1, 1)) + unit_bias[piece]
            act = gelu_exact(pre).astype(bf16)
            hidden.append(pre)
            activated.append(act)
            term = dot(act, down_pieces[piece], (1, 0))
            branch = term if branch is None else branch + term
        stream = middle + (branch + down_bias[layer_idx].astype(f32))
        saved.append(
            (
                layer_input,
                middle,
                normed,
                queries,
                kv_own,
                kv_other,
                log_total,
                mixed,
                normed_two,
                hidden,
                activated,
            )
        )
    layer_out = swap_rows(stream.astype(bf16))

    row_place = core * half + jnp.arange(half, dtype=jnp.int32)
    row_mask = (row_place < valid).astype(f32)[:, None]
    grad_stream = cotangent_rows.astype(f32) * row_mask

    def scatter_units(up_grads, down_grads):
        def across(piece):
            sent = jnp.stack([up_grads[piece + 1], down_grads[piece + 1]]).astype(bf16)
            received = over("c", sent).astype(f32)
            return jnp.stack(
                [up_grads[piece] + received[0], down_grads[piece] + received[1]]
            ).astype(bf16)

        def halve(array, axis):
            count = array.shape[1] // 2
            return add_low(array[:, :count], over(axis, array[:, count:]))

        one, two = across(0), across(2)
        one, two = halve(one, "y"), halve(two, "x")
        one, two = halve(one, "x"), halve(two, "y")
        cut = (2, 2, unit_slice, width_all)
        one = jnp.swapaxes(one.reshape(cut), 0, 1)
        two = jnp.swapaxes(two.reshape(cut), 0, 1)
        total = scatter_z(one, two)
        if outer > 1:
            total = lax.psum(total, "o")
        total = paired(x_bit, total, over("x", total), 1)
        total = paired(y_bit, total, over("y", total), 1)
        total = paired(core, total, over("c", total), 3)
        return total.reshape(2, unit_shard, width_all).astype(f32)

    def scatter_attention(grad_kv, grad_q, grad_o):
        kv = grad_kv.reshape(groups, 2, shard, width_all)
        qo = jnp.stack(
            [
                grad_q.reshape(groups, shard, width_all),
                grad_o.reshape(groups, shard, width_all),
            ],
            axis=1,
        )
        sent = jnp.where(core == 0, qo, kv).astype(bf16)
        kept = jnp.where(core == 0, kv, qo)
        total = add_low(kept, over("c", sent))
        total = scatter_z(total[:2], total[2:])
        if outer > 1:
            total = lax.psum(total, "o")
        one, two = total[0], total[1]
        one, two = add_low(one, over("x", one)), add_low(two, over("y", two))
        one, two = add_low(one, over("y", one)), add_low(two, over("x", two))
        total = jnp.stack([one, two])
        total = paired(core, total, over("c", total), 0).astype(f32)
        weight_in = jnp.stack([total[1, 0], total[0, 0], total[0, 1]])
        return jnp.swapaxes(weight_in, 1, 2), total[1, 1]

    layer_grads = [None] * layer_count
    small_rows = [None] * layer_count
    for layer_idx in reversed(range(layer_count)):
        (
            layer_input,
            middle,
            normed,
            queries,
            kv_own,
            kv_other,
            log_total,
            mixed,
            normed_two,
            hidden,
            activated,
        ) = saved[layer_idx]
        weight_kv, weight_q, weight_o = attention_weights[layer_idx]
        up_pieces, down_pieces = unit_weights[layer_idx]
        grad_down = grad_stream.astype(bf16)
        down_bias_grad = jnp.sum(grad_down.astype(f32), axis=0)
        up_grads = [None] * 4
        down_grads = [None] * 4
        up_bias_grads = [None] * 4
        grad_normed_two = None
        for piece in (1, 3, 0, 2):
            down_grads[piece] = dot(activated[piece], grad_down, (0, 0))
            grad_act = dot(grad_down, down_pieces[piece], (1, 1))
            gelu_pull = jax.vjp(gelu_exact, hidden[piece])[1]
            grad_hidden = gelu_pull(grad_act)[0].astype(bf16)
            up_bias_grads[piece] = jnp.sum(grad_hidden.astype(f32), axis=0)
            up_grads[piece] = dot(grad_hidden, normed_two, (0, 0))
            term = dot(grad_hidden, up_pieces[piece], (1, 0))
            grad_normed_two = term if grad_normed_two is None else grad_normed_two + term
        unit_grads = scatter_units(up_grads, down_grads)
        norm_pull = jax.vjp(normalize, middle, gains[layer_idx, 1], shifts[layer_idx, 1])[1]
        grad_from_norm, gain_two_grad, shift_two_grad = norm_pull(grad_normed_two)
        grad_middle = grad_stream + grad_from_norm
        grad_branch = grad_middle.astype(bf16)
        output_bias_grad = jnp.sum(grad_branch.astype(f32), axis=0)
        grad_o = dot(mixed, grad_branch, (1, 0))
        grad_mixed = dot(weight_o, grad_branch, (1, 1)).astype(bf16)
        grad_queries, grad_kv_own, grad_kv_other = attend_backward(
            info, queries, kv_own, kv_other, mixed, log_total, grad_mixed, groups
        )
        grad_kv = add_low(grad_kv_own, over("c", grad_kv_other))
        grad_q = dot(grad_queries, normed, (1, 0))
        grad_kv_weight = dot(grad_kv, normed, (1, 0))
        attention_grads = scatter_attention(grad_kv_weight, grad_q, grad_o)
        query_bias_grad = jnp.sum(grad_queries.astype(f32), axis=1)
        value_bias_grad = jnp.sum(
            grad_kv.reshape(groups, 2, shard, half)[:, 1].astype(f32), axis=-1
        )
        grad_normed = dot(grad_queries, weight_q, (0, 0)) + dot(grad_kv, weight_kv, (0, 0))
        norm_pull = jax.vjp(normalize, layer_input, gains[layer_idx, 0], shifts[layer_idx, 0])[1]
        grad_from_input, gain_one_grad, shift_one_grad = norm_pull(grad_normed)
        grad_stream = grad_middle + grad_from_input
        layer_grads[layer_idx] = (unit_grads, attention_grads)
        small_rows[layer_idx] = jnp.concatenate(
            [
                jnp.stack(
                    [
                        gain_one_grad,
                        gain_two_grad,
                        shift_one_grad,
                        shift_two_grad,
                        output_bias_grad,
                        down_bias_grad,
                    ]
                ),
                unit_order_back(jnp.stack(up_bias_grads)),
                z_order(query_bias_grad.reshape(groups, shard)).reshape(1, -1),
                z_order(value_bias_grad).reshape(1, -1),
            ]
        )
    grad_in = swap_rows(grad_stream)
    small = jnp.stack(small_rows)
    for axis in ("c", "x", "y"):
        small = small + over(axis, small)
    small = small + z_send(small, near_pairs)
    small = small + z_send(small, [(0, 2), (2, 0), (1, 3), (3, 1)])
    if outer > 1:
        small = lax.psum(small, "o")

    def z_part(array, size):
        return lax.dynamic_slice_in_dim(array, z_place * size, size, axis=-1)

    up_bias_all = z_part(small[:, 6:10].reshape(layer_count, -1), unit_shard)
    input_bias_grad = z_part(small[:, 10:12], shard)
    return (
        layer_out,
        grad_in,
        small[:, 0:2],
        small[:, 2:4],
        jnp.stack([grads[1][0] for grads in layer_grads]),
        input_bias_grad,
        jnp.stack([grads[1][1] for grads in layer_grads]),
        small[:, 4],
        jnp.stack([jnp.swapaxes(grads[0][0], 0, 1) for grads in layer_grads]),
        up_bias_all,
        jnp.stack([grads[0][1] for grads in layer_grads]),
        small[:, 5],
    )


def solution(mesh):
    split = mesh.shape["dp"] // 8
    fine = Mesh(
        mesh.devices.reshape(split, 2, 2, 2, mesh.shape["tensor"]), ("o", "y", "x", "c", "z")
    )
    rows = P(("o", "y", "x", "c", "z"), None)
    placed = (
        rows,
        P(("o", "y", "x", "c")),
        P(),
        P(),
        P(None, None, None, "z"),
        P(None, None, "z"),
        P(None, "z", None),
        P(),
        P(None, None, "z"),
        P(None, "z"),
        P(None, "z", None),
        P(),
        rows,
    )
    return jax.shard_map(
        local,
        mesh=fine,
        in_specs=placed,
        out_specs=(rows, rows) + placed[2:12],
        check_vma=False,
    )
```

```python
import functools

import jax
import jax.numpy as jnp
from jax import lax
from jax.experimental import pallas as pl
from jax.experimental.pallas import tpu as pltpu
from jax.sharding import Mesh, PartitionSpec as P

HD = 64
ROWS = 1024
IMAGE = 240

epsilon = 1e-06
masked_score = -1e30
bf16 = jnp.bfloat16
f32 = jnp.float32


def dot(left, right, contract):
    return lax.dot_general(
        left, right, ((contract[:1], contract[1:]), ((), ())), preferred_element_type=f32
    )


def kernel_cost(seconds):
    return pl.CostEstimate(
        flops=int(1.1535e15 * seconds), bytes_accessed=int(3.69e12 * seconds), transcendentals=0
    )


def normalize(values, gain_row, bias_row):
    average = jnp.mean(values, axis=-1, keepdims=True)
    centred = values - average
    variance = jnp.mean(centred * centred, axis=-1, keepdims=True)
    return centred * lax.rsqrt(variance + epsilon) * gain_row + bias_row


def gelu_pair(values):
    size = jnp.abs(values)
    knot = 1.0 / (1.0 + (0.3275911 * 0.5**0.5) * size)
    bell = jnp.exp(values * values * -0.5)
    series = knot * (
        0.127414796
        + knot * (-0.142248368 + knot * (0.7107068705 + knot * (-0.7265760135 + knot * 0.5307027145)))
    )
    tail = series * bell
    normal = jnp.where(values > 0, 1.0 - tail, tail)
    return values * normal, normal + values * bell * 0.3989422804014327


def key_halves(core, own, received):
    first = jnp.where(core == 0, own, received)
    second = jnp.where(core == 0, received, own)
    return first, second


def attend_forward_kernel(info, queries, kv_own, kv_other, mixed, log_total):
    core, valid = info[0], info[1]
    width = queries.shape[0]
    half = kv_own.shape[1]
    key_place = lax.broadcasted_iota(jnp.int32, (half, 1), 0) + half
    key_bias = jnp.where(key_place < valid, 0.0, masked_score).astype(f32)
    for head in range(width // HD):
        rows = slice(head * HD, (head + 1) * HD)
        value_rows = slice(width + head * HD, width + (head + 1) * HD)
        query = queries[rows, :] * jnp.asarray(HD**-0.5, bf16)
        key_one, key_two = key_halves(core, kv_own[rows, :], kv_other[rows, :])
        value_one, value_two = key_halves(core, kv_own[value_rows, :], kv_other[value_rows, :])
        score_one = dot(key_one, query, (0, 0))
        score_two = dot(key_two, query, (0, 0)) + key_bias
        top = jnp.maximum(
            jnp.max(score_one, axis=0, keepdims=True), jnp.max(score_two, axis=0, keepdims=True)
        )
        weight_one = jnp.exp(score_one - top)
        weight_two = jnp.exp(score_two - top)
        total = jnp.sum(weight_one, axis=0, keepdims=True) + jnp.sum(
            weight_two, axis=0, keepdims=True
        )
        out = dot(value_one, weight_one.astype(bf16), (1, 0)) + dot(
            value_two, weight_two.astype(bf16), (1, 0)
        )
        mixed[rows, :] = (out / total).astype(bf16)
        log_total[0, head : head + 1, :] = top + jnp.log(total)


def attend_backward_kernel(
    info, queries, kv_own, kv_other, mixed, log_total, grad_mixed, grad_q, grad_own, grad_other
):
    core, valid = info[0], info[1]
    width = queries.shape[0]
    half = kv_own.shape[1]
    scale = HD**-0.5
    key_place = lax.broadcasted_iota(jnp.int32, (half, 1), 0) + half
    key_bias = jnp.where(key_place < valid, 0.0, masked_score).astype(f32)
    for head in range(width // HD):
        rows = slice(head * HD, (head + 1) * HD)
        value_rows = slice(width + head * HD, width + (head + 1) * HD)
        query = queries[rows, :] * jnp.asarray(scale, bf16)
        grad_out = grad_mixed[rows, :]
        delta = jnp.sum(
            grad_out.astype(f32) * mixed[rows, :].astype(f32), axis=0, keepdims=True
        )
        log_row = log_total[0, head : head + 1, :]
        keys = key_halves(core, kv_own[rows, :], kv_other[rows, :])
        values = key_halves(core, kv_own[value_rows, :], kv_other[value_rows, :])
        grad_query = None
        grad_keys = []
        grad_values = []
        for part in range(2):
            score = dot(keys[part], query, (0, 0))
            if part == 1:
                score = score + key_bias
            probs = jnp.exp(score - log_row)
            grad_values.append(dot(grad_out, probs.astype(bf16), (1, 1)))
            grad_probs = dot(values[part], grad_out, (0, 0))
            grad_score = (probs * (grad_probs - delta)).astype(bf16)
            term = dot(keys[part], grad_score, (1, 0))
            grad_query = term if grad_query is None else grad_query + term
            grad_keys.append(dot(query, grad_score, (1, 1)))
        grad_q[rows, :] = (grad_query * scale).astype(bf16)
        own, other = key_halves(core, *grad_keys)
        grad_own[rows, :] = own
        grad_other[rows, :] = other.astype(bf16)
        own, other = key_halves(core, *grad_values)
        grad_own[value_rows, :] = own
        grad_other[value_rows, :] = other.astype(bf16)


def attention_specs(groups, width, half):
    return dict(
        q=pl.BlockSpec((width, half), lambda g, info: (g, 0)),
        kv=pl.BlockSpec((2 * width, half), lambda g, info: (g, 0)),
        log=pl.BlockSpec((1, 8, half), lambda g, info: (g, 0, 0)),
    )


def attend_forward(info, queries, kv_own, kv_other, groups):
    features, half = queries.shape
    width = features // groups
    specs = attention_specs(groups, width, half)
    return pl.pallas_call(
        attend_forward_kernel,
        grid_spec=pltpu.PrefetchScalarGridSpec(
            num_scalar_prefetch=1,
            grid=(groups,),
            in_specs=[specs["q"], specs["kv"], specs["kv"]],
            out_specs=[specs["q"], specs["log"]],
        ),
        out_shape=[
            jax.ShapeDtypeStruct((features, half), bf16),
            jax.ShapeDtypeStruct((groups, 8, half), f32),
        ],
        compiler_params=pltpu.CompilerParams(vmem_limit_bytes=40 << 20),
        cost_estimate=kernel_cost(14e-6),
        name="attend_forward",
    )(info, queries, kv_own, kv_other)


def attend_backward(info, queries, kv_own, kv_other, mixed, log_total, grad_mixed, groups):
    features, half = queries.shape
    width = features // groups
    specs = attention_specs(groups, width, half)
    return pl.pallas_call(
        attend_backward_kernel,
        grid_spec=pltpu.PrefetchScalarGridSpec(
            num_scalar_prefetch=1,
            grid=(groups,),
            in_specs=[specs["q"], specs["kv"], specs["kv"], specs["q"], specs["log"], specs["q"]],
            out_specs=[specs["q"], specs["kv"], specs["kv"]],
        ),
        out_shape=[
            jax.ShapeDtypeStruct((features, half), bf16),
            jax.ShapeDtypeStruct((2 * features, half), f32),
            jax.ShapeDtypeStruct((2 * features, half), bf16),
        ],
        compiler_params=pltpu.CompilerParams(vmem_limit_bytes=40 << 20),
        cost_estimate=kernel_cost(21e-6),
        name="attend_backward",
    )(info, queries, kv_own, kv_other, mixed, log_total, grad_mixed)


def stream_pieces(pieces, buffer, arrived):
    step = pl.program_id(0)
    rows = buffer.shape[1]

    def copy(index):
        source, offset = pieces[index]
        return pltpu.make_async_copy(
            source.at[pl.ds(offset, rows), :], buffer.at[index % 2], arrived.at[index % 2]
        )

    @pl.when(step == 0)
    def _():
        copy(0).start()

    for index in range(len(pieces) - 1):

        @pl.when(step == index)
        def _(index=index):
            copy(index + 1).start()

    for index in range(len(pieces)):

        @pl.when(step == index)
        def _(index=index):
            copy(index).wait()

    return lax.rem(step, 2)


def list_pieces(refs, rows):
    return [(ref, start) for ref in refs for start in range(0, ref.shape[0], rows)]


def units_forward_kernel(count, rows, normed, middle, unit_bias, down_bias, *refs):
    weights = refs[:count]
    activated, slopes, result, buffer, arrived = refs[count:]
    slot = stream_pieces(list_pieces(weights, rows), buffer, arrived)
    width = normed.shape[1]
    pre = dot(normed[...], buffer[slot, :, :width], (1, 1)) + unit_bias[0]
    act, slope = gelu_pair(pre)
    act = act.astype(bf16)
    activated[...] = act
    slopes[...] = slope.astype(bf16)

    @pl.when(pl.program_id(0) == 0)
    def _():
        result[...] = middle[...] + down_bias[...]

    result[...] += dot(act, buffer[slot, :, width:], (1, 0))


def units_forward(normed, middle, unit_bias, down_bias, weights):
    tokens, width = normed.shape
    rows = unit_bias.shape[1]
    steps = unit_bias.shape[0]
    units = rows * steps
    whole = pl.BlockSpec((tokens, width), lambda i: (0, 0))
    block = pl.BlockSpec((tokens, rows), lambda i: (0, i))
    return pl.pallas_call(
        functools.partial(units_forward_kernel, len(weights), rows),
        grid=(steps,),
        in_specs=[
            whole,
            whole,
            pl.BlockSpec((1, 1, rows), lambda i: (i, 0, 0)),
            pl.BlockSpec((1, width), lambda i: (0, 0)),
        ]
        + [pl.BlockSpec(memory_space=pl.ANY)] * len(weights),
        out_specs=[block, block, whole],
        out_shape=[
            jax.ShapeDtypeStruct((tokens, units), bf16),
            jax.ShapeDtypeStruct((tokens, units), bf16),
            jax.ShapeDtypeStruct((tokens, width), f32),
        ],
        scratch_shapes=[
            pltpu.VMEM((2, rows, 2 * width), bf16),
            pltpu.SemaphoreType.DMA((2,)),
        ],
        compiler_params=pltpu.CompilerParams(vmem_limit_bytes=40 << 20),
        cost_estimate=kernel_cost(17e-6),
        name="units_forward",
    )(normed, middle, unit_bias[:, None, :], down_bias, *weights)


def stream_blocks(place, source, buffer, arrived):
    step = pl.program_id(0)
    rows = buffer.shape[1]

    def copy(index):
        offset = pl.multiple_of(place[index] * rows, rows)
        slot = lax.rem(index, 2)
        return pltpu.make_async_copy(
            source.at[pl.ds(offset, rows), :], buffer.at[slot], arrived.at[slot]
        )

    @pl.when(step == 0)
    def _():
        copy(0).start()

    @pl.when(step + 1 < pl.num_programs(0))
    def _():
        copy(step + 1).start()

    copy(step).wait()
    return lax.rem(step, 2)


def units_backward_kernel(count, rows, place, grad_down, normed, activated, slopes, *refs):
    weights = refs[:count]
    sent, kept, grad_normed, bias_grad, buffer, arrived = refs[count:]
    step = pl.program_id(0)
    if count == 1:
        slot = stream_blocks(place, weights[0], buffer, arrived)
    else:
        slot = stream_pieces(list_pieces(weights, rows), buffer, arrived)
    width = normed.shape[1]
    grad_act = dot(grad_down[...], buffer[slot, :, width:], (1, 1))
    grad_hidden = grad_act * slopes[...].astype(f32)
    bias_grad[0] = jnp.sum(grad_hidden, axis=0, keepdims=True)
    grad_hidden = grad_hidden.astype(bf16)

    @pl.when(step == 0)
    def _():
        grad_normed[...] = jnp.zeros_like(grad_normed)

    grad_normed[...] += dot(grad_hidden, buffer[slot, :, :width], (1, 0))
    up = dot(grad_hidden, normed[...], (0, 0)).astype(bf16)
    down = dot(activated[...], grad_down[...], (0, 0)).astype(bf16)

    def store(target):
        target[:, :width] = up
        target[:, width:] = down

    half = pl.num_programs(0) // 2
    pl.when(step < half)(lambda: store(sent))
    pl.when(step >= half)(lambda: store(kept))


def units_backward(place, grad_down, normed, activated, slopes, weights, rows):
    tokens, width = normed.shape
    units = activated.shape[1]
    steps = units // rows
    half = steps // 2
    whole = pl.BlockSpec((tokens, width), lambda i, place: (0, 0))
    block = pl.BlockSpec((tokens, rows), lambda i, place: (0, place[i]))
    return pl.pallas_call(
        functools.partial(units_backward_kernel, len(weights), rows),
        grid_spec=pltpu.PrefetchScalarGridSpec(
            num_scalar_prefetch=1,
            grid=(steps,),
            in_specs=[whole, whole, block, block]
            + [pl.BlockSpec(memory_space=pl.ANY)] * len(weights),
            out_specs=[
                pl.BlockSpec((rows, 2 * width), lambda i, place: (jnp.minimum(i, half - 1), 0)),
                pl.BlockSpec((rows, 2 * width), lambda i, place: (jnp.maximum(i - half, 0), 0)),
                whole,
                pl.BlockSpec((1, 1, rows), lambda i, place: (place[i], 0, 0)),
            ],
            scratch_shapes=[
                pltpu.VMEM((2, rows, 2 * width), bf16),
                pltpu.SemaphoreType.DMA((2,)),
            ],
        ),
        out_shape=[jax.ShapeDtypeStruct((units // 2, 2 * width), bf16)] * 2
        + [
            jax.ShapeDtypeStruct((tokens, width), f32),
            jax.ShapeDtypeStruct((steps, 1, rows), f32),
        ],
        compiler_params=pltpu.CompilerParams(vmem_limit_bytes=40 << 20),
        cost_estimate=kernel_cost(20e-6),
        name="units_backward",
    )(place, grad_down, normed, activated, slopes, *weights)


def norm_backward_kernel(last, values, grad, kept, gain, *refs):
    if last:
        earlier, others, result, packed, sums = refs[:3], refs[3], *refs[4:]
    else:
        result, low, sums = refs
    step = pl.program_id(0)
    block = values[...]
    average = jnp.mean(block, axis=-1, keepdims=True)
    centred = block - average
    scale = lax.rsqrt(jnp.mean(centred * centred, axis=-1, keepdims=True) + epsilon)
    unit = centred * scale
    down = grad[...]
    inner = down * gain[...]
    total = kept[...] + scale * (
        inner
        - jnp.mean(inner, axis=-1, keepdims=True)
        - unit * jnp.mean(inner * unit, axis=-1, keepdims=True)
    )
    result[...] = total

    @pl.when(step == 0)
    def _():
        sums[...] = jnp.zeros_like(sums)

    sums[0:1, :] += jnp.sum(down * unit, axis=0, keepdims=True)
    sums[1:2, :] += jnp.sum(down, axis=0, keepdims=True)
    if not last:
        rounded = total.astype(bf16)
        low[...] = rounded
        sums[2:3, :] += jnp.sum(rounded.astype(f32), axis=0, keepdims=True)
    else:

        @pl.when(step == pl.num_programs(0) - 1)
        def _():
            rows = jnp.concatenate(
                [ref[0:3, :] for ref in earlier] + [sums[0:2, :], others[...]]
            )
            high = rows.astype(bf16)
            packed[0 : rows.shape[0], :] = high
            packed[rows.shape[0] :, :] = (rows - high.astype(f32)).astype(bf16)


def norm_backward(values, grad, kept, gain, *rows):
    tokens, width = values.shape
    steps = 4
    block = pl.BlockSpec((tokens // steps, width), lambda i: (i, 0))

    def whole(count):
        return pl.BlockSpec((count, width), lambda i: (0, 0))

    last = bool(rows)
    if last:
        count = 2 * (11 + rows[-1].shape[0])
        out_specs = [block, whole(count)]
        out_shape = [
            jax.ShapeDtypeStruct((tokens, width), f32),
            jax.ShapeDtypeStruct((count, width), bf16),
        ]
        scratch = [pltpu.VMEM((8, width), f32)]
    else:
        out_specs = [block, block, whole(8)]
        out_shape = [
            jax.ShapeDtypeStruct((tokens, width), f32),
            jax.ShapeDtypeStruct((tokens, width), bf16),
            jax.ShapeDtypeStruct((8, width), f32),
        ]
        scratch = []
    return pl.pallas_call(
        functools.partial(norm_backward_kernel, last),
        grid=(steps,),
        in_specs=[block, block, block, whole(1)] + [whole(row.shape[0]) for row in rows],
        out_specs=out_specs,
        out_shape=out_shape,
        scratch_shapes=scratch,
        compiler_params=pltpu.CompilerParams(vmem_limit_bytes=24 << 20),
        cost_estimate=kernel_cost(3e-6),
        name="norm_backward",
    )(values, grad, kept, gain, *rows)


def unit_results_kernel(own, even, up, down):
    width = down.shape[2]
    for layer, grads in enumerate((own, even)):
        up[layer] = grads[:, :width].astype(f32).T
        down[layer] = grads[:, width:].astype(f32)


def unit_results(own, even):
    units, double = own.shape
    width = double // 2
    steps = 3
    block = pl.BlockSpec((units // steps, double), lambda i: (i, 0))
    return pl.pallas_call(
        unit_results_kernel,
        grid=(steps,),
        in_specs=[block, block],
        out_specs=[
            pl.BlockSpec((2, width, units // steps), lambda i: (0, 0, i)),
            pl.BlockSpec((2, units // steps, width), lambda i: (0, i, 0)),
        ],
        out_shape=[
            jax.ShapeDtypeStruct((2, width, units), f32),
            jax.ShapeDtypeStruct((2, units, width), f32),
        ],
        compiler_params=pltpu.CompilerParams(vmem_limit_bytes=24 << 20),
        cost_estimate=kernel_cost(5e-6),
        name="unit_results",
    )(own, even)


flip_pair = [(0, 1), (1, 0)]


def over(axis, array):
    return lax.ppermute(array, axis, flip_pair)


def z_send(array, pairs):
    return lax.ppermute(array, "z", pairs)


def z_pairs(step):
    return [(z, z ^ step) for z in range(4)]


def z_three(blocks):
    return [lax.ppermute(block, "z", z_pairs(step + 1)) for step, block in enumerate(blocks)]


def yx_three(blocks):
    across = [(place, 3 - place) for place in range(4)]
    return [
        over("x", blocks[0]),
        over("y", blocks[1]),
        lax.ppermute(blocks[2], ("y", "x"), across),
    ]


def add_low(*terms):
    total = terms[0].astype(f32)
    for term in terms[1:]:
        total = total + term.astype(f32)
    return total.astype(bf16)


def together(*arrays):
    return lax.optimization_barrier(arrays)


def tie(array, *after):
    return lax.optimization_barrier((array, after))[0]


def flip_if(bit, array, axis):
    return jnp.where(bit == 1, jnp.flip(array, axis), array)


def paired(bit, own, received, axis):
    return jnp.stack(
        [jnp.where(bit == 0, own, received), jnp.where(bit == 0, received, own)], axis=axis
    )


def local(
    stream_in,
    patch_size,
    norm_gain,
    norm_bias,
    input_weight,
    input_bias,
    output_weight,
    output_bias,
    up_weight,
    up_bias,
    down_weight,
    down_bias,
    cotangent,
):
    half, width_all = stream_in.shape
    layer_count = input_weight.shape[0]
    shard = input_weight.shape[-1]
    unit_shard = up_weight.shape[-1]
    unit_slice = unit_shard // 8
    groups = lax.axis_size("z")
    outer = lax.axis_size("o")
    core, x_bit, y_bit = lax.axis_index("c"), lax.axis_index("x"), lax.axis_index("y")
    z_place = lax.axis_index("z")
    z_low, z_high = z_place % 2, z_place // 2

    swap = []
    for c in range(2):
        for z in range(groups):
            if c != z % 2:
                swap.append((c * groups + z, (z % 2) * groups + (z - z % 2 + c)))

    def swap_rows(array):
        return jnp.where(z_low == core, array, lax.ppermute(array, ("c", "z"), swap))

    other_patch = over("c", patch_size)
    patch = jnp.where(z_low == core, patch_size, other_patch)
    patch = jnp.where(z_high == 0, patch[0], patch[1])
    grid_side = IMAGE // patch
    valid = grid_side * grid_side
    info = jnp.stack([core, valid]).astype(jnp.int32)

    stream_rows = swap_rows(stream_in)

    def z_order(array):
        pairs = array.reshape((2, 2) + array.shape[1:])
        pairs = flip_if(z_high, flip_if(z_low, pairs, 1), 0)
        return pairs.reshape(array.shape)

    def unit_flip(cut):
        cut = flip_if(z_high, flip_if(z_low, cut, 1), 0)
        return flip_if(y_bit, flip_if(x_bit, flip_if(core, cut, 4), 3), 2)

    def own_order(rows):
        cut = unit_flip(rows.reshape(2, 2, 2, 2, 2, unit_slice))
        cut = jnp.stack([cut[0].transpose(3, 1, 2, 0, 4), cut[1].transpose(3, 2, 1, 0, 4)], axis=1)
        return cut[::-1].reshape(8, unit_shard // 2)

    def own_order_back(pieces):
        cut = pieces.reshape(2, 2, 2, 2, 2, unit_slice)[::-1]
        cut = jnp.stack([cut[:, 0].transpose(3, 1, 2, 0, 4), cut[:, 1].transpose(3, 2, 1, 0, 4)])
        return unit_flip(cut).reshape(groups, unit_shard)

    def even_order(rows):
        cut = rows.reshape(groups, 8, unit_slice).transpose(1, 0, 2)
        return cut.reshape(8, unit_shard // 2)

    def even_order_back(pieces):
        cut = pieces.reshape(8, groups, unit_slice).transpose(1, 0, 2)
        return cut.reshape(groups, unit_shard)

    slice_index = (y_bit * 2 + x_bit) * 2 + core

    part = shard // 2

    def attention_slice(layer_idx):
        first = jnp.where(core == 0, input_weight[layer_idx, 1], input_weight[layer_idx, 0]).T
        second = jnp.where(core == 0, input_weight[layer_idx, 2].T, output_weight[layer_idx])
        return jnp.concatenate(
            [
                lax.dynamic_slice_in_dim(first, x_bit * part, part, axis=0),
                lax.dynamic_slice_in_dim(second, y_bit * part, part, axis=0),
            ]
        )

    def attention_halves(blocks):
        return (
            jnp.stack([block[:part] for block in blocks]),
            jnp.stack([block[part : 2 * part] for block in blocks]),
        )

    def attention_own(first, second, received):
        first = paired(x_bit, first, received[0], 1).reshape(groups, shard, width_all)
        second = paired(y_bit, second, received[1], 1).reshape(groups, shard, width_all)
        return jnp.stack([first, second], axis=1)

    def attention_whole(own):
        received = over("c", own)
        kv = jnp.where(core == 0, own, received)
        qo = jnp.where(core == 0, received, own)
        return (
            kv.reshape(2 * groups * shard, width_all),
            qo[:, 0].reshape(groups * shard, width_all),
            qo[:, 1].reshape(groups * shard, width_all),
        )

    def unit_block(layer_idx):
        up = lax.dynamic_slice_in_dim(
            up_weight[layer_idx], slice_index * unit_slice, unit_slice, axis=1
        )
        down = lax.dynamic_slice_in_dim(
            down_weight[layer_idx], slice_index * unit_slice, unit_slice, axis=0
        )
        return jnp.concatenate([up.T, down], axis=1)

    small_bias = input_bias.reshape(-1, unit_shard)
    bias_count = layer_count + small_bias.shape[0]
    bias_rows = jnp.pad(up_bias, ((0, 16 - layer_count), (0, 0))) + jnp.pad(
        small_bias, ((layer_count, 16 - bias_count), (0, 0))
    )
    everyone = ("y", "x", "c", "z")
    block = jnp.concatenate([attention_slice(0), bias_rows])
    first_blocks = z_three([block] * 3)
    blocks = [block] + first_blocks
    biases = jnp.stack([block[2 * part :] for block in blocks]).astype(f32)
    first, second = attention_halves(blocks)
    own_attention = attention_own(first, second, [over("x", first), over("y", second)])
    block = tie(unit_block(0), first, second)
    unit_blocks = z_three([block] * 3)
    first_weights = attention_whole(own_attention)
    one = tie(jnp.concatenate([block, unit_blocks[0]]), first_weights[0])
    two = tie(jnp.concatenate(unit_blocks[1:]), first_weights[0])
    one = jnp.concatenate([one, over("x", one)])
    two = jnp.concatenate([two, over("y", two)])
    near_units = [over("y", one), over("x", two)]
    even_units = lax.all_gather(
        tie(unit_block(1), *first_blocks), everyone, axis=0, tiled=True
    )
    attention_weights = [first_weights, None]
    unit_weights = [None, [even_units]]
    up_bias_all = z_order(biases[:, :layer_count])
    input_bias_all = biases[:, layer_count : layer_count + input_bias.size // unit_shard].reshape(
        groups, layer_count, 2, shard
    )
    gains = norm_gain.astype(f32)
    shifts = norm_bias.astype(f32)

    stream = stream_rows.astype(f32)
    saved = []
    for layer_idx in range(layer_count):
        if layer_idx == 1:
            attention_weights[1] = attention_whole(own_attention)
            cotangent_rows = swap_rows(tie(cotangent, own_attention))
        weight_kv, weight_q, weight_o = attention_weights[layer_idx]
        layer_input = stream
        normed = normalize(stream, gains[layer_idx, 0], shifts[layer_idx, 0]).astype(bf16)
        value_bias = input_bias_all[:, layer_idx, 1]
        kv_bias = jnp.stack([jnp.zeros_like(value_bias), value_bias], axis=1).reshape(-1, 1)
        kv_own = (dot(weight_kv, normed, (1, 1)) + kv_bias).astype(bf16)
        if layer_idx == 0:
            later_block = tie(attention_slice(1), kv_own)
            later_blocks = z_three([later_block] * 3)
        kv_other = over("c", kv_own)
        query_bias = input_bias_all[:, layer_idx, 0].reshape(-1, 1)
        queries = (dot(weight_q, normed, (1, 1)) + query_bias).astype(bf16)
        mixed, log_total = attend_forward(info, queries, kv_own, kv_other, groups)
        if layer_idx == 0:
            mixed, log_total, near_units, later_blocks = together(
                mixed, log_total, near_units, later_blocks
            )
            pieces = [one, near_units[0], two, near_units[1]]
            unit_weights[0] = [over("c", piece) for piece in pieces] + pieces
            first, second = attention_halves([later_block, *later_blocks])
        middle = stream + (
            dot(mixed, weight_o, (0, 0)) + output_bias[layer_idx].astype(f32)
        )
        normed_two = normalize(middle, gains[layer_idx, 1], shifts[layer_idx, 1]).astype(bf16)
        order = own_order if layer_idx == 0 else even_order
        if layer_idx == 0:
            unit_weights[0], normed_two, first, second = together(
                unit_weights[0], normed_two, first, second
            )
            received = [over("x", first), over("y", second)]
        activated, slopes, stream = units_forward(
            normed_two,
            middle,
            order(up_bias_all[:, layer_idx]),
            down_bias[layer_idx].astype(f32)[None, :],
            unit_weights[layer_idx],
        )
        if layer_idx == 0:
            activated, slopes, stream, received = together(activated, slopes, stream, received)
            own_attention = attention_own(first, second, received)
        saved.append(
            (
                layer_input,
                middle,
                normed,
                queries,
                kv_own,
                kv_other,
                log_total,
                mixed,
                normed_two,
                slopes,
                activated,
            )
        )
    layer_rows = stream.astype(bf16)

    row_place = core * half + jnp.arange(half, dtype=jnp.int32)
    row_mask = (row_place < valid).astype(f32)[:, None]
    grad_stream = cotangent_rows.astype(f32) * row_mask

    slab = (4, unit_shard // 2, 2 * width_all)
    strip = unit_shard // 4
    thin = (2, unit_slice, 2 * width_all)

    def own_first(kept, received):
        kept, received = kept.reshape(slab), received.reshape(slab)
        parts = [add_low(kept[k], received[k]) for k in range(4)]
        return [parts[0], parts[2]], [parts[1], parts[3]]

    def even_first(kept, received):
        kept, received = kept.reshape(slab), received.reshape(slab)

        def part(rows, blocks):
            return add_low(
                jnp.concatenate([kept[k, rows] for k in blocks]),
                jnp.concatenate([received[k, rows] for k in blocks]),
            )

        one, two = slice(0, strip), slice(strip, 2 * strip)
        return [part(one, (0, 1)), part(two, (0, 2))], [part(one, (2, 3)), part(two, (1, 3))]

    def unit_second(parts, received):
        kept, sent = [], []
        for part, other in zip(parts, received):
            kept.append(add_low(part[:strip], other[:strip]).reshape(thin))
            sent.append(add_low(part[strip:], other[strip:]).reshape(thin))
        return kept, sent

    def own_third(parts, received):
        one, two = [add_low(*pair) for pair in zip(parts, received)]
        return [one[0], one[1], two[0], two[1]]

    def even_third(parts, received):
        total = jnp.concatenate([add_low(*pair) for pair in zip(parts, received)])
        return [
            lax.dynamic_index_in_dim(total, z_place ^ step, axis=0, keepdims=False)
            for step in range(4)
        ]

    def over_outer(total):
        return lax.psum(total, "o") if outer > 1 else total

    def gather_shard(total):
        return lax.all_gather(total, everyone[:3], axis=0, tiled=True)

    def attention_parts(grad_kv, grad_q, grad_o):
        kv = grad_kv.reshape(groups, 2, shard, width_all)
        qo = jnp.stack(
            [
                grad_q.reshape(groups, shard, width_all),
                grad_o.reshape(groups, shard, width_all),
            ],
            axis=1,
        )
        sent = jnp.where(core == 0, qo, kv)
        kept = jnp.where(core == 0, kv, qo)
        return sent, kept

    quarter = shard // 4
    rest = 2 * quarter

    def attention_first(total):
        cut = total.reshape(groups, 2, 2, 2, quarter, width_all)
        one, two = cut[:, 0], cut[:, 1]

        def pick(array, index, axis):
            return lax.dynamic_index_in_dim(array, index, axis, keepdims=False)

        kept = [pick(one, y_bit, 1), pick(two, x_bit, 2)]
        return kept, [pick(one, 1 - y_bit, 1), pick(two, 1 - x_bit, 2)]

    def attention_second(parts, received):
        kept, sent = [], []
        for part, other, bit in zip(parts, received, (x_bit, y_bit)):
            total = add_low(part, other)
            kept.append(lax.dynamic_index_in_dim(total, bit, 1, keepdims=False))
            sent.append(lax.dynamic_index_in_dim(total, 1 - bit, 1, keepdims=False))
        return kept, sent

    def attention_third(parts, received):
        total = jnp.concatenate([add_low(*pair) for pair in zip(parts, received)], axis=1)
        return [total[step] for step in range(4)]

    def attention_gathered(rows):
        cut = rows.reshape(4, 2, 2, quarter, width_all).transpose(1, 2, 0, 3, 4).astype(f32)
        cut = cut.reshape(2, 2, shard, width_all)
        weight_in = jnp.stack([cut[1, 0], cut[0, 0], cut[0, 1]])
        return jnp.swapaxes(weight_in, 1, 2), cut[1, 1]

    def attention_out(whole, received):
        cut = (2, shard, width_all)
        total = paired(core, whole.reshape(cut), received.reshape(cut), 0).astype(f32)
        weight_in = jnp.stack([total[1, 0], total[0, 0], total[0, 1]])
        return jnp.swapaxes(weight_in, 1, 2), total[1, 1]

    def attention_cuts(kept, received):
        place = y_bit * 2 + x_bit

        def cut(array, step):
            return lax.dynamic_slice_in_dim(array, (place ^ step) * quarter, quarter, axis=2)

        return [add_low(cut(kept, step), cut(received, step)) for step in range(4)]

    def attention_sum(cuts, received):
        return add_low(cuts[0], *received).reshape(4, rest, width_all)

    def attention_join(blocks):
        whole = jnp.stack(blocks).reshape(2, 2, 2, quarter, width_all)
        whole = flip_if(y_bit, flip_if(x_bit, whole, 1), 0)
        return whole.transpose(2, 0, 1, 3, 4).reshape(2 * shard, width_all)

    def pack(rows):
        high = rows.astype(bf16)
        low = (rows - lax.optimization_barrier(high).astype(f32)).astype(bf16)
        return lax.optimization_barrier(jnp.concatenate([high, low]))

    def unpack(rows):
        count = rows.shape[0] // 2
        return rows[:count].astype(f32) + rows[count:].astype(f32)

    def four(own, received):
        one, two, three = received
        return (unpack(own) + unpack(one)) + (unpack(two) + unpack(three))

    grad_down = grad_stream.astype(bf16)
    other_rows = [jnp.sum(grad_down.astype(f32), axis=0, keepdims=True)]
    sum_rows = []
    for layer_idx in reversed(range(layer_count)):
        (
            layer_input,
            middle,
            normed,
            queries,
            kv_own,
            kv_other,
            log_total,
            mixed,
            normed_two,
            slopes,
            activated,
        ) = saved[layer_idx]
        weight_kv, weight_q, weight_o = attention_weights[layer_idx]
        first = layer_idx == 0
        steps = jnp.arange(8, dtype=jnp.int32)
        if first:
            place = steps
            later, later_sent = attention_first(add_low(attention_kept, attention_received))
            even_cuts = even_third(unit_parts, unit_received)
            grad_down, later, later_sent, even_cuts = together(
                grad_down, later, later_sent, even_cuts
            )
            later_received = [over("y", later_sent[0]), over("x", later_sent[1])]
            even_received = z_three(even_cuts[1:])
        else:
            place = slice_index ^ ((steps % 4) * 2 + (1 - steps // 4))
        grads = units_backward(
            place,
            grad_down,
            normed_two,
            activated,
            slopes,
            unit_weights[layer_idx],
            unit_shard // 2,
        )
        if first:
            grads, later_received, even_received = together(grads, later_received, even_received)
            later, later_sent = attention_second(later, later_received)
            even_total = over_outer(add_low(even_cuts[0], *even_received))
            grads, later, later_sent, even_total = together(grads, later, later_sent, even_total)
            later_received = [over("x", later_sent[0]), over("y", later_sent[1])]
            even_grads = gather_shard(even_total)
        unit_sent, unit_kept, grad_normed_two, up_bias_grad = grads
        unit_received = over("c", unit_sent)
        order_back = own_order_back if first else even_order_back
        other_rows.append(order_back(up_bias_grad))
        grad_middle, grad_branch, rows = norm_backward(
            middle, grad_normed_two, grad_stream, gains[layer_idx, 1][None, :]
        )
        sum_rows.append(rows)
        grad_o = dot(mixed, grad_branch, (1, 0)).astype(bf16)
        grad_mixed = dot(weight_o, grad_branch, (1, 1)).astype(bf16)
        grad_mixed, grad_o, unit_received = together(grad_mixed, grad_o, unit_received)
        unit_parts, unit_sent = (own_first if first else even_first)(unit_kept, unit_received)
        if first:
            later_received = tie(later_received, grad_mixed)
            later_cuts = attention_third(later, later_received)
            grad_mixed, unit_parts, unit_sent, later_cuts = together(
                grad_mixed, unit_parts, unit_sent, later_cuts
            )
            later_received = z_three(later_cuts[1:])
        else:
            grad_mixed, unit_parts, unit_sent, layer_rows = together(
                grad_mixed, unit_parts, unit_sent, layer_rows
            )
            layer_out = swap_rows(layer_rows)
        unit_received = [over("y", unit_sent[0]), over("x", unit_sent[1])]
        outs = attend_backward(
            info, queries, kv_own, kv_other, mixed, log_total, grad_mixed, groups
        )
        outs, unit_received = together(outs, unit_received)
        unit_parts, unit_sent = unit_second(unit_parts, unit_received)
        if first:
            later_received = tie(later_received, outs[0])
            later_total = over_outer(add_low(later_cuts[0], *later_received))
            outs, unit_parts, unit_sent, later_total = together(
                outs, unit_parts, unit_sent, later_total
            )
            later_grads = gather_shard(later_total)
        else:
            outs, unit_parts, unit_sent, layer_out = together(
                outs, unit_parts, unit_sent, layer_out
            )
        unit_received = [over("x", unit_sent[0]), over("y", unit_sent[1])]
        grad_queries, grad_kv_own, grad_kv_other = outs
        grad_kv = add_low(grad_kv_own, over("c", grad_kv_other))
        grad_q = dot(grad_queries, normed, (1, 0)).astype(bf16)
        grad_kv_weight = dot(grad_kv, normed, (1, 0)).astype(bf16)
        attention_sent, attention_kept = attention_parts(grad_kv_weight, grad_q, grad_o)
        attention_received = over("c", attention_sent)
        query_bias_grad = jnp.sum(grad_queries.astype(f32), axis=1)
        value_bias_grad = jnp.sum(
            grad_kv.reshape(groups, 2, shard, half)[:, 1].astype(f32), axis=-1
        )
        other_rows.append(z_order(query_bias_grad.reshape(groups, shard)).reshape(1, -1))
        other_rows.append(z_order(value_bias_grad).reshape(1, -1))
        grad_normed = dot(grad_queries, weight_q, (0, 0)) + dot(grad_kv, weight_kv, (0, 0))
        if first:
            other_rows = jnp.concatenate(other_rows)
            grad_normed, attention_received, unit_received, other_rows = together(
                grad_normed, attention_received, unit_received, other_rows
            )
            cuts = attention_cuts(attention_kept, attention_received)
            unit_cuts = own_third(unit_parts, unit_received)
            grad_normed, cuts, unit_cuts = together(grad_normed, cuts, unit_cuts)
            received = yx_three(cuts[1:])
            unit_received = z_three(unit_cuts[1:])
            grad_stream, small = norm_backward(
                layer_input,
                grad_normed,
                grad_middle,
                gains[layer_idx, 0][None, :],
                *sum_rows,
                other_rows,
            )
        else:
            grad_stream, grad_down, rows = norm_backward(
                layer_input, grad_normed, grad_middle, gains[layer_idx, 0][None, :]
            )
            sum_rows.append(rows)
            grad_stream, grad_down, attention_received, unit_received = together(
                grad_stream, grad_down, attention_received, unit_received
            )
    width = width_all
    grad_stream, small, received, unit_received = together(
        grad_stream, small, received, unit_received
    )
    last = attention_sum(cuts, received)
    unit_total = over_outer(add_low(unit_cuts[0], *unit_received))
    sent = [jnp.concatenate([last[k], small]) for k in (1, 2, 3)]
    sent, last, unit_total, grad_stream, even_grads, later_grads = together(
        sent, last, unit_total, grad_stream, even_grads, later_grads
    )
    received = z_three(sent)
    own_grads = gather_shard(unit_total)
    grad_in = swap_rows(grad_stream)
    later_grads = attention_gathered(later_grads)
    received, later_grads = together(received, later_grads)
    last = over_outer(add_low(last[0], *[block[:rest] for block in received]))
    small = pack(over_outer(four(small, [block[rest:] for block in received])))
    sent = jnp.concatenate([last, small])
    received = yx_three([sent] * 3)
    up_grads, down_grads = unit_results(own_grads, even_grads)
    received, up_grads, down_grads, grad_in = together(received, up_grads, down_grads, grad_in)
    small = pack(four(small, [block[rest:] for block in received]))
    last = attention_join([last] + [block[:rest] for block in received])
    received = over("c", jnp.concatenate([last, small]))
    small = unpack(small) + unpack(received[2 * shard :])
    first_grads = attention_out(last, received[: 2 * shard])

    def two_layers(one, two):
        return jnp.stack([one, two])

    gain_grads = two_layers(jnp.stack([small[9], small[6]]), jnp.stack([small[3], small[0]]))
    shift_grads = two_layers(jnp.stack([small[10], small[7]]), jnp.stack([small[4], small[1]]))
    output_bias_grads = two_layers(small[8], small[2])
    down_bias_grads = two_layers(small[5], small[11])
    up_bias_rows = two_layers(small[18:22], small[12:16])
    input_bias_rows = two_layers(small[22:24], small[16:18])

    def z_part(array, size):
        return lax.dynamic_slice_in_dim(array, z_place * size, size, axis=-1)

    return (
        layer_out,
        grad_in,
        gain_grads,
        shift_grads,
        jnp.stack([first_grads[0], later_grads[0]]),
        z_part(input_bias_rows, shard),
        jnp.stack([first_grads[1], later_grads[1]]),
        output_bias_grads,
        up_grads,
        z_part(up_bias_rows.reshape(layer_count, -1), unit_shard),
        down_grads,
        down_bias_grads,
    )


def solution(mesh):
    split = mesh.shape["dp"] // 8
    fine = Mesh(
        mesh.devices.reshape(split, 2, 2, 2, mesh.shape["tensor"]), ("o", "y", "x", "c", "z")
    )
    rows = P(("o", "y", "x", "c", "z"), None)
    placed = (
        rows,
        P(("o", "y", "x", "c")),
        P(),
        P(),
        P(None, None, None, "z"),
        P(None, None, "z"),
        P(None, "z", None),
        P(),
        P(None, None, "z"),
        P(None, "z"),
        P(None, "z", None),
        P(),
        rows,
    )
    return jax.shard_map(
        local,
        mesh=fine,
        in_specs=placed,
        out_specs=(rows, rows) + placed[2:12],
        check_vma=False,
    )
```

```python
import functools

import jax
import jax.numpy as jnp
from jax import lax
from jax.experimental import pallas as pl
from jax.experimental.pallas import tpu as pltpu
from jax.sharding import Mesh, PartitionSpec as P

HD = 64
ROWS = 1024
IMAGE = 240

epsilon = 1e-06
masked_score = -1e30
bf16 = jnp.bfloat16
f32 = jnp.float32


def dot(left, right, contract):
    return lax.dot_general(
        left, right, ((contract[:1], contract[1:]), ((), ())), preferred_element_type=f32
    )


def kernel_cost(seconds):
    return pl.CostEstimate(
        flops=int(1.1535e15 * seconds), bytes_accessed=int(3.69e12 * seconds), transcendentals=0
    )


def normalize(values, gain_row, bias_row):
    average = jnp.mean(values, axis=-1, keepdims=True)
    centred = values - average
    variance = jnp.mean(centred * centred, axis=-1, keepdims=True)
    return centred * lax.rsqrt(variance + epsilon) * gain_row + bias_row


def gelu_pair(values):
    size = jnp.abs(values)
    knot = 1.0 / (1.0 + (0.3275911 * 0.5**0.5) * size)
    bell = jnp.exp(values * values * -0.5)
    series = knot * (
        0.127414796
        + knot * (-0.142248368 + knot * (0.7107068705 + knot * (-0.7265760135 + knot * 0.5307027145)))
    )
    tail = series * bell
    normal = jnp.where(values > 0, 1.0 - tail, tail)
    return values * normal, normal + values * bell * 0.3989422804014327


def key_halves(core, own, received):
    first = jnp.where(core == 0, own, received)
    second = jnp.where(core == 0, received, own)
    return first, second


def attend_forward_kernel(info, queries, kv_own, kv_other, mixed, log_total):
    core, valid = info[0], info[1]
    width = queries.shape[0]
    half = kv_own.shape[1]
    key_place = lax.broadcasted_iota(jnp.int32, (half, 1), 0) + half
    key_bias = jnp.where(key_place < valid, 0.0, masked_score).astype(f32)
    for head in range(width // HD):
        rows = slice(head * HD, (head + 1) * HD)
        value_rows = slice(width + head * HD, width + (head + 1) * HD)
        query = queries[rows, :] * jnp.asarray(HD**-0.5, bf16)
        key_one, key_two = key_halves(core, kv_own[rows, :], kv_other[rows, :])
        value_one, value_two = key_halves(core, kv_own[value_rows, :], kv_other[value_rows, :])
        score_one = dot(key_one, query, (0, 0))
        score_two = dot(key_two, query, (0, 0)) + key_bias
        top = jnp.maximum(
            jnp.max(score_one, axis=0, keepdims=True), jnp.max(score_two, axis=0, keepdims=True)
        )
        weight_one = jnp.exp(score_one - top)
        weight_two = jnp.exp(score_two - top)
        total = jnp.sum(weight_one, axis=0, keepdims=True) + jnp.sum(
            weight_two, axis=0, keepdims=True
        )
        out = dot(value_one, weight_one.astype(bf16), (1, 0)) + dot(
            value_two, weight_two.astype(bf16), (1, 0)
        )
        mixed[rows, :] = (out / total).astype(bf16)
        log_total[0, head : head + 1, :] = top + jnp.log(total)


def attend_backward_kernel(
    info, queries, kv_own, kv_other, mixed, log_total, grad_mixed, grad_q, grad_own, grad_other
):
    core, valid = info[0], info[1]
    width = queries.shape[0]
    half = kv_own.shape[1]
    scale = HD**-0.5
    key_place = lax.broadcasted_iota(jnp.int32, (half, 1), 0) + half
    key_bias = jnp.where(key_place < valid, 0.0, masked_score).astype(f32)
    for head in range(width // HD):
        rows = slice(head * HD, (head + 1) * HD)
        value_rows = slice(width + head * HD, width + (head + 1) * HD)
        query = queries[rows, :] * jnp.asarray(scale, bf16)
        grad_out = grad_mixed[rows, :]
        delta = jnp.sum(
            grad_out.astype(f32) * mixed[rows, :].astype(f32), axis=0, keepdims=True
        )
        log_row = log_total[0, head : head + 1, :]
        keys = key_halves(core, kv_own[rows, :], kv_other[rows, :])
        values = key_halves(core, kv_own[value_rows, :], kv_other[value_rows, :])
        grad_query = None
        grad_keys = []
        grad_values = []
        for part in range(2):
            score = dot(keys[part], query, (0, 0))
            if part == 1:
                score = score + key_bias
            probs = jnp.exp(score - log_row)
            grad_values.append(dot(grad_out, probs.astype(bf16), (1, 1)))
            grad_probs = dot(values[part], grad_out, (0, 0))
            grad_score = (probs * (grad_probs - delta)).astype(bf16)
            term = dot(keys[part], grad_score, (1, 0))
            grad_query = term if grad_query is None else grad_query + term
            grad_keys.append(dot(query, grad_score, (1, 1)))
        grad_q[rows, :] = (grad_query * scale).astype(bf16)
        own, other = key_halves(core, *grad_keys)
        grad_own[rows, :] = own
        grad_other[rows, :] = other.astype(bf16)
        own, other = key_halves(core, *grad_values)
        grad_own[value_rows, :] = own
        grad_other[value_rows, :] = other.astype(bf16)


def attention_specs(groups, width, half):
    return dict(
        q=pl.BlockSpec((width, half), lambda g, info: (g, 0)),
        kv=pl.BlockSpec((2 * width, half), lambda g, info: (g, 0)),
        log=pl.BlockSpec((1, 8, half), lambda g, info: (g, 0, 0)),
    )


def attend_forward(info, queries, kv_own, kv_other, groups):
    features, half = queries.shape
    width = features // groups
    specs = attention_specs(groups, width, half)
    return pl.pallas_call(
        attend_forward_kernel,
        grid_spec=pltpu.PrefetchScalarGridSpec(
            num_scalar_prefetch=1,
            grid=(groups,),
            in_specs=[specs["q"], specs["kv"], specs["kv"]],
            out_specs=[specs["q"], specs["log"]],
        ),
        out_shape=[
            jax.ShapeDtypeStruct((features, half), bf16),
            jax.ShapeDtypeStruct((groups, 8, half), f32),
        ],
        compiler_params=pltpu.CompilerParams(vmem_limit_bytes=40 << 20),
        cost_estimate=kernel_cost(14e-6),
        name="attend_forward",
    )(info, queries, kv_own, kv_other)


def attend_backward(info, queries, kv_own, kv_other, mixed, log_total, grad_mixed, groups):
    features, half = queries.shape
    width = features // groups
    specs = attention_specs(groups, width, half)
    return pl.pallas_call(
        attend_backward_kernel,
        grid_spec=pltpu.PrefetchScalarGridSpec(
            num_scalar_prefetch=1,
            grid=(groups,),
            in_specs=[specs["q"], specs["kv"], specs["kv"], specs["q"], specs["log"], specs["q"]],
            out_specs=[specs["q"], specs["kv"], specs["kv"]],
        ),
        out_shape=[
            jax.ShapeDtypeStruct((features, half), bf16),
            jax.ShapeDtypeStruct((2 * features, half), f32),
            jax.ShapeDtypeStruct((2 * features, half), bf16),
        ],
        compiler_params=pltpu.CompilerParams(vmem_limit_bytes=40 << 20),
        cost_estimate=kernel_cost(21e-6),
        name="attend_backward",
    )(info, queries, kv_own, kv_other, mixed, log_total, grad_mixed)


def stream_pieces(pieces, buffer, arrived):
    step = pl.program_id(0)
    rows = buffer.shape[1]

    def copy(index):
        source, offset = pieces[index]
        return pltpu.make_async_copy(
            source.at[pl.ds(offset, rows), :], buffer.at[index % 2], arrived.at[index % 2]
        )

    @pl.when(step == 0)
    def _():
        copy(0).start()

    for index in range(len(pieces) - 1):

        @pl.when(step == index)
        def _(index=index):
            copy(index + 1).start()

    for index in range(len(pieces)):

        @pl.when(step == index)
        def _(index=index):
            copy(index).wait()

    return lax.rem(step, 2)


def list_pieces(refs, rows):
    return [(ref, start) for ref in refs for start in range(0, ref.shape[0], rows)]


def units_forward_kernel(count, rows, normed, middle, unit_bias, down_bias, *refs):
    weights = refs[:count]
    activated, slopes, result, buffer, arrived = refs[count:]
    slot = stream_pieces(list_pieces(weights, rows), buffer, arrived)
    width = normed.shape[1]

    @pl.when(pl.program_id(0) == 0)
    def _():
        result[...] = middle[...] + down_bias[...]

    size = normed.shape[0] // 2
    for start in range(0, 2 * size, size):
        part = slice(start, start + size)
        pre = dot(normed[part, :], buffer[slot, :, :width], (1, 1)) + unit_bias[0]
        act, slope = gelu_pair(pre)
        act = act.astype(bf16)
        activated[part, :] = act
        slopes[part, :] = slope.astype(bf16)
        result[part, :] += dot(act, buffer[slot, :, width:], (1, 0))


def units_forward(normed, middle, unit_bias, down_bias, weights):
    tokens, width = normed.shape
    rows = unit_bias.shape[1]
    steps = unit_bias.shape[0]
    units = rows * steps
    whole = pl.BlockSpec((tokens, width), lambda i: (0, 0))
    block = pl.BlockSpec((tokens, rows), lambda i: (0, i))
    return pl.pallas_call(
        functools.partial(units_forward_kernel, len(weights), rows),
        grid=(steps,),
        in_specs=[
            whole,
            whole,
            pl.BlockSpec((1, 1, rows), lambda i: (i, 0, 0)),
            pl.BlockSpec((1, width), lambda i: (0, 0)),
        ]
        + [pl.BlockSpec(memory_space=pl.ANY)] * len(weights),
        out_specs=[block, block, whole],
        out_shape=[
            jax.ShapeDtypeStruct((tokens, units), bf16),
            jax.ShapeDtypeStruct((tokens, units), bf16),
            jax.ShapeDtypeStruct((tokens, width), f32),
        ],
        scratch_shapes=[
            pltpu.VMEM((2, rows, 2 * width), bf16),
            pltpu.SemaphoreType.DMA((2,)),
        ],
        compiler_params=pltpu.CompilerParams(vmem_limit_bytes=40 << 20),
        cost_estimate=kernel_cost(17e-6),
        name="units_forward",
    )(normed, middle, unit_bias[:, None, :], down_bias, *weights)


def stream_blocks(place, source, buffer, arrived):
    step = pl.program_id(0)
    rows = buffer.shape[1]

    def copy(index):
        offset = pl.multiple_of(place[index] * rows, rows)
        slot = lax.rem(index, 2)
        return pltpu.make_async_copy(
            source.at[pl.ds(offset, rows), :], buffer.at[slot], arrived.at[slot]
        )

    @pl.when(step == 0)
    def _():
        copy(0).start()

    @pl.when(step + 1 < pl.num_programs(0))
    def _():
        copy(step + 1).start()

    copy(step).wait()
    return lax.rem(step, 2)


def units_backward_kernel(count, rows, place, grad_down, normed, activated, slopes, *refs):
    weights = refs[:count]
    sent, kept, grad_normed, bias_grad, buffer, arrived = refs[count:]
    step = pl.program_id(0)
    if count == 1:
        slot = stream_blocks(place, weights[0], buffer, arrived)
    else:
        slot = stream_pieces(list_pieces(weights, rows), buffer, arrived)
    width = normed.shape[1]
    grad_act = dot(grad_down[...], buffer[slot, :, width:], (1, 1))
    grad_hidden = grad_act * slopes[...].astype(f32)
    bias_grad[0] = jnp.sum(grad_hidden, axis=0, keepdims=True)
    grad_hidden = grad_hidden.astype(bf16)

    @pl.when(step == 0)
    def _():
        grad_normed[...] = jnp.zeros_like(grad_normed)

    grad_normed[...] += dot(grad_hidden, buffer[slot, :, :width], (1, 0))
    up = dot(grad_hidden, normed[...], (0, 0)).astype(bf16)
    down = dot(activated[...], grad_down[...], (0, 0)).astype(bf16)

    def store(target):
        target[:, :width] = up
        target[:, width:] = down

    half = pl.num_programs(0) // 2
    pl.when(step < half)(lambda: store(sent))
    pl.when(step >= half)(lambda: store(kept))


def units_backward(place, grad_down, normed, activated, slopes, weights, rows):
    tokens, width = normed.shape
    units = activated.shape[1]
    steps = units // rows
    half = steps // 2
    whole = pl.BlockSpec((tokens, width), lambda i, place: (0, 0))
    block = pl.BlockSpec((tokens, rows), lambda i, place: (0, place[i]))
    return pl.pallas_call(
        functools.partial(units_backward_kernel, len(weights), rows),
        grid_spec=pltpu.PrefetchScalarGridSpec(
            num_scalar_prefetch=1,
            grid=(steps,),
            in_specs=[whole, whole, block, block]
            + [pl.BlockSpec(memory_space=pl.ANY)] * len(weights),
            out_specs=[
                pl.BlockSpec((rows, 2 * width), lambda i, place: (jnp.minimum(i, half - 1), 0)),
                pl.BlockSpec((rows, 2 * width), lambda i, place: (jnp.maximum(i - half, 0), 0)),
                whole,
                pl.BlockSpec((1, 1, rows), lambda i, place: (place[i], 0, 0)),
            ],
            scratch_shapes=[
                pltpu.VMEM((2, rows, 2 * width), bf16),
                pltpu.SemaphoreType.DMA((2,)),
            ],
        ),
        out_shape=[jax.ShapeDtypeStruct((units // 2, 2 * width), bf16)] * 2
        + [
            jax.ShapeDtypeStruct((tokens, width), f32),
            jax.ShapeDtypeStruct((steps, 1, rows), f32),
        ],
        compiler_params=pltpu.CompilerParams(vmem_limit_bytes=40 << 20),
        cost_estimate=kernel_cost(20e-6),
        name="units_backward",
    )(place, grad_down, normed, activated, slopes, *weights)


def norm_backward_kernel(last, values, grad, kept, gain, *refs):
    if last:
        earlier, others, result, packed, sums = refs[:3], refs[3], *refs[4:]
    else:
        result, low, sums = refs
    step = pl.program_id(0)
    block = values[...]
    average = jnp.mean(block, axis=-1, keepdims=True)
    centred = block - average
    scale = lax.rsqrt(jnp.mean(centred * centred, axis=-1, keepdims=True) + epsilon)
    unit = centred * scale
    down = grad[...]
    inner = down * gain[...]
    total = kept[...] + scale * (
        inner
        - jnp.mean(inner, axis=-1, keepdims=True)
        - unit * jnp.mean(inner * unit, axis=-1, keepdims=True)
    )
    result[...] = total

    @pl.when(step == 0)
    def _():
        sums[...] = jnp.zeros_like(sums)

    sums[0:1, :] += jnp.sum(down * unit, axis=0, keepdims=True)
    sums[1:2, :] += jnp.sum(down, axis=0, keepdims=True)
    if not last:
        rounded = total.astype(bf16)
        low[...] = rounded
        sums[2:3, :] += jnp.sum(rounded.astype(f32), axis=0, keepdims=True)
    else:

        @pl.when(step == pl.num_programs(0) - 1)
        def _():
            rows = [sums[0:1, :], earlier[2][0:1, :], earlier[1][0:1, :], earlier[0][0:1, :]]
            rows += [sums[1:2, :], earlier[2][1:2, :], earlier[1][1:2, :], earlier[0][1:2, :]]
            rows += [earlier[2][2:3, :], earlier[0][2:3, :], earlier[1][2:3, :]]
            rows += [others[0:1, :], others[7:11, :], others[1:5, :]]
            rows = jnp.concatenate(rows + [others[11:13, :], others[5:7, :]])
            high = rows.astype(bf16)
            packed[0 : rows.shape[0], :] = high
            packed[rows.shape[0] :, :] = (rows - high.astype(f32)).astype(bf16)


def norm_backward(values, grad, kept, gain, *rows):
    tokens, width = values.shape
    steps = 4
    block = pl.BlockSpec((tokens // steps, width), lambda i: (i, 0))

    def whole(count):
        return pl.BlockSpec((count, width), lambda i: (0, 0))

    last = bool(rows)
    if last:
        count = 2 * (11 + rows[-1].shape[0])
        out_specs = [block, whole(count)]
        out_shape = [
            jax.ShapeDtypeStruct((tokens, width), f32),
            jax.ShapeDtypeStruct((count, width), bf16),
        ]
        scratch = [pltpu.VMEM((8, width), f32)]
    else:
        out_specs = [block, block, whole(8)]
        out_shape = [
            jax.ShapeDtypeStruct((tokens, width), f32),
            jax.ShapeDtypeStruct((tokens, width), bf16),
            jax.ShapeDtypeStruct((8, width), f32),
        ]
        scratch = []
    return pl.pallas_call(
        functools.partial(norm_backward_kernel, last),
        grid=(steps,),
        in_specs=[block, block, block, whole(1)] + [whole(row.shape[0]) for row in rows],
        out_specs=out_specs,
        out_shape=out_shape,
        scratch_shapes=scratch,
        compiler_params=pltpu.CompilerParams(vmem_limit_bytes=24 << 20),
        cost_estimate=kernel_cost(3e-6),
        name="norm_backward",
    )(values, grad, kept, gain, *rows)


def unit_results_kernel(own, even, up, down):
    width = down.shape[2]
    for layer, grads in enumerate((own, even)):
        up[layer] = grads[:, :width].astype(f32).T
        down[layer] = grads[:, width:].astype(f32)


def unit_results(own, even):
    units, double = own.shape
    width = double // 2
    steps = 3
    block = pl.BlockSpec((units // steps, double), lambda i: (i, 0))
    return pl.pallas_call(
        unit_results_kernel,
        grid=(steps,),
        in_specs=[block, block],
        out_specs=[
            pl.BlockSpec((2, width, units // steps), lambda i: (0, 0, i)),
            pl.BlockSpec((2, units // steps, width), lambda i: (0, i, 0)),
        ],
        out_shape=[
            jax.ShapeDtypeStruct((2, width, units), f32),
            jax.ShapeDtypeStruct((2, units, width), f32),
        ],
        compiler_params=pltpu.CompilerParams(vmem_limit_bytes=24 << 20),
        cost_estimate=kernel_cost(5e-6),
        name="unit_results",
    )(own, even)


flip_pair = [(0, 1), (1, 0)]


def over(axis, array):
    return lax.ppermute(array, axis, flip_pair)


def z_send(array, pairs):
    return lax.ppermute(array, "z", pairs)


def z_pairs(step):
    return [(z, z ^ step) for z in range(4)]


def z_three(blocks):
    return [lax.ppermute(block, "z", z_pairs(step + 1)) for step, block in enumerate(blocks)]


def yx_three(blocks):
    across = [(place, 3 - place) for place in range(4)]
    return [
        over("x", blocks[0]),
        over("y", blocks[1]),
        lax.ppermute(blocks[2], ("y", "x"), across),
    ]


def add_low(*terms):
    total = terms[0].astype(f32)
    for term in terms[1:]:
        total = total + term.astype(f32)
    return total.astype(bf16)


def together(*arrays):
    return lax.optimization_barrier(arrays)


def tie(array, *after):
    return lax.optimization_barrier((array, after))[0]


def flip_if(bit, array, axis):
    return jnp.where(bit == 1, jnp.flip(array, axis), array)


def paired(bit, own, received, axis):
    return jnp.stack(
        [jnp.where(bit == 0, own, received), jnp.where(bit == 0, received, own)], axis=axis
    )


def local(
    stream_in,
    patch_size,
    norm_gain,
    norm_bias,
    input_weight,
    input_bias,
    output_weight,
    output_bias,
    up_weight,
    up_bias,
    down_weight,
    down_bias,
    cotangent,
):
    half, width_all = stream_in.shape
    layer_count = input_weight.shape[0]
    shard = input_weight.shape[-1]
    unit_shard = up_weight.shape[-1]
    unit_slice = unit_shard // 8
    groups = lax.axis_size("z")
    outer = lax.axis_size("o")
    core, x_bit, y_bit = lax.axis_index("c"), lax.axis_index("x"), lax.axis_index("y")
    z_place = lax.axis_index("z")
    z_low, z_high = z_place % 2, z_place // 2

    swap = []
    for c in range(2):
        for z in range(groups):
            if c != z % 2:
                swap.append((c * groups + z, (z % 2) * groups + (z - z % 2 + c)))

    def swap_rows(array):
        return jnp.where(z_low == core, array, lax.ppermute(array, ("c", "z"), swap))

    other_patch = over("c", patch_size)
    patch = jnp.where(z_low == core, patch_size, other_patch)
    patch = jnp.where(z_high == 0, patch[0], patch[1])
    grid_side = IMAGE // patch
    valid = grid_side * grid_side
    info = jnp.stack([core, valid]).astype(jnp.int32)

    stream_rows = swap_rows(stream_in)

    def z_order(array):
        pairs = array.reshape((2, 2) + array.shape[1:])
        pairs = flip_if(z_high, flip_if(z_low, pairs, 1), 0)
        return pairs.reshape(array.shape)

    def unit_flip(cut):
        cut = flip_if(z_high, flip_if(z_low, cut, 1), 0)
        return flip_if(y_bit, flip_if(x_bit, flip_if(core, cut, 4), 3), 2)

    def own_order(rows):
        cut = unit_flip(rows.reshape(2, 2, 2, 2, 2, unit_slice))
        cut = jnp.stack([cut[0].transpose(3, 1, 2, 0, 4), cut[1].transpose(3, 2, 1, 0, 4)], axis=1)
        return cut[::-1].reshape(8, unit_shard // 2)

    def own_order_back(pieces):
        cut = pieces.reshape(2, 2, 2, 2, 2, unit_slice)[::-1]
        cut = jnp.stack([cut[:, 0].transpose(3, 1, 2, 0, 4), cut[:, 1].transpose(3, 2, 1, 0, 4)])
        return unit_flip(cut).reshape(groups, unit_shard)

    def even_order(rows):
        cut = rows.reshape(groups, 8, unit_slice).transpose(1, 0, 2)
        return cut.reshape(8, unit_shard // 2)

    def even_order_back(pieces):
        cut = pieces.reshape(8, groups, unit_slice).transpose(1, 0, 2)
        return cut.reshape(groups, unit_shard)

    slice_index = (y_bit * 2 + x_bit) * 2 + core

    part = shard // 2

    def attention_slice(layer_idx):
        first = jnp.where(core == 0, input_weight[layer_idx, 1], input_weight[layer_idx, 0]).T
        second = jnp.where(core == 0, input_weight[layer_idx, 2].T, output_weight[layer_idx])
        return jnp.concatenate(
            [
                lax.dynamic_slice_in_dim(first, x_bit * part, part, axis=0),
                lax.dynamic_slice_in_dim(second, y_bit * part, part, axis=0),
            ]
        )

    def attention_halves(blocks):
        return (
            jnp.stack([block[:part] for block in blocks]),
            jnp.stack([block[part : 2 * part] for block in blocks]),
        )

    def attention_own(first, second, received):
        first = paired(x_bit, first, received[0], 1).reshape(groups, shard, width_all)
        second = paired(y_bit, second, received[1], 1).reshape(groups, shard, width_all)
        return jnp.stack([first, second], axis=1)

    def attention_whole(own):
        received = over("c", own)
        kv = jnp.where(core == 0, own, received)
        qo = jnp.where(core == 0, received, own)
        return (
            kv.reshape(2 * groups * shard, width_all),
            qo[:, 0].reshape(groups * shard, width_all),
            qo[:, 1].reshape(groups * shard, width_all),
        )

    def unit_block(layer_idx):
        up = lax.dynamic_slice_in_dim(
            up_weight[layer_idx], slice_index * unit_slice, unit_slice, axis=1
        )
        down = lax.dynamic_slice_in_dim(
            down_weight[layer_idx], slice_index * unit_slice, unit_slice, axis=0
        )
        return jnp.concatenate([up.T, down], axis=1)

    small_bias = input_bias.reshape(-1, unit_shard)
    bias_count = layer_count + small_bias.shape[0]
    bias_rows = jnp.pad(up_bias, ((0, 16 - layer_count), (0, 0))) + jnp.pad(
        small_bias, ((layer_count, 16 - bias_count), (0, 0))
    )
    everyone = ("y", "x", "c", "z")
    block = jnp.concatenate([attention_slice(0), bias_rows])
    first_blocks = z_three([block] * 3)
    blocks = [block] + first_blocks
    biases = jnp.stack([block[2 * part :] for block in blocks]).astype(f32)
    first, second = attention_halves(blocks)
    own_attention = attention_own(first, second, [over("x", first), over("y", second)])
    block = tie(unit_block(0), first, second)
    unit_blocks = z_three([block] * 3)
    first_weights = attention_whole(own_attention)
    one = tie(jnp.concatenate([block, unit_blocks[0]]), first_weights[0])
    two = tie(jnp.concatenate(unit_blocks[1:]), first_weights[0])
    one = jnp.concatenate([one, over("x", one)])
    two = jnp.concatenate([two, over("y", two)])
    near_units = [over("y", one), over("x", two)]
    even_units = lax.all_gather(
        tie(unit_block(1), *first_blocks), everyone, axis=0, tiled=True
    )
    attention_weights = [first_weights, None]
    unit_weights = [None, [even_units]]
    up_bias_all = z_order(biases[:, :layer_count])
    input_bias_all = biases[:, layer_count : layer_count + input_bias.size // unit_shard].reshape(
        groups, layer_count, 2, shard
    )
    gains = norm_gain.astype(f32)
    shifts = norm_bias.astype(f32)

    stream = stream_rows.astype(f32)
    saved = []
    for layer_idx in range(layer_count):
        if layer_idx == 1:
            attention_weights[1] = attention_whole(own_attention)
            cotangent_rows = swap_rows(tie(cotangent, own_attention))
        weight_kv, weight_q, weight_o = attention_weights[layer_idx]
        layer_input = stream
        normed = normalize(stream, gains[layer_idx, 0], shifts[layer_idx, 0]).astype(bf16)
        value_bias = input_bias_all[:, layer_idx, 1]
        kv_bias = jnp.stack([jnp.zeros_like(value_bias), value_bias], axis=1).reshape(-1, 1)
        kv_own = (dot(weight_kv, normed, (1, 1)) + kv_bias).astype(bf16)
        if layer_idx == 0:
            later_block = tie(attention_slice(1), kv_own)
            later_blocks = z_three([later_block] * 3)
        kv_other = over("c", kv_own)
        query_bias = input_bias_all[:, layer_idx, 0].reshape(-1, 1)
        queries = (dot(weight_q, normed, (1, 1)) + query_bias).astype(bf16)
        mixed, log_total = attend_forward(info, queries, kv_own, kv_other, groups)
        if layer_idx == 0:
            mixed, log_total, near_units, later_blocks = together(
                mixed, log_total, near_units, later_blocks
            )
            pieces = [one, near_units[0], two, near_units[1]]
            unit_weights[0] = [over("c", piece) for piece in pieces] + pieces
            first, second = attention_halves([later_block, *later_blocks])
        middle = stream + (
            dot(mixed, weight_o, (0, 0)) + output_bias[layer_idx].astype(f32)
        )
        normed_two = normalize(middle, gains[layer_idx, 1], shifts[layer_idx, 1]).astype(bf16)
        order = own_order if layer_idx == 0 else even_order
        if layer_idx == 0:
            unit_weights[0], normed_two, first, second = together(
                unit_weights[0], normed_two, first, second
            )
            received = [over("x", first), over("y", second)]
        activated, slopes, stream = units_forward(
            normed_two,
            middle,
            order(up_bias_all[:, layer_idx]),
            down_bias[layer_idx].astype(f32)[None, :],
            unit_weights[layer_idx],
        )
        if layer_idx == 0:
            activated, slopes, stream, received = together(activated, slopes, stream, received)
            own_attention = attention_own(first, second, received)
        saved.append(
            (
                layer_input,
                middle,
                normed,
                queries,
                kv_own,
                kv_other,
                log_total,
                mixed,
                normed_two,
                slopes,
                activated,
            )
        )
    layer_rows = stream.astype(bf16)

    row_place = core * half + jnp.arange(half, dtype=jnp.int32)
    row_mask = (row_place < valid).astype(f32)[:, None]
    grad_stream = cotangent_rows.astype(f32) * row_mask

    slab = (4, unit_shard // 2, 2 * width_all)
    strip = unit_shard // 4
    thin = (2, unit_slice, 2 * width_all)

    def own_first(kept, received):
        kept, received = kept.reshape(slab), received.reshape(slab)
        parts = [add_low(kept[k], received[k]) for k in range(4)]
        return [parts[0], parts[2]], [parts[1], parts[3]]

    def even_first(kept, received):
        kept, received = kept.reshape(slab), received.reshape(slab)

        def part(rows, blocks):
            return add_low(
                jnp.concatenate([kept[k, rows] for k in blocks]),
                jnp.concatenate([received[k, rows] for k in blocks]),
            )

        one, two = slice(0, strip), slice(strip, 2 * strip)
        return [part(one, (0, 1)), part(two, (0, 2))], [part(one, (2, 3)), part(two, (1, 3))]

    def unit_second(parts, received):
        kept, sent = [], []
        for part, other in zip(parts, received):
            kept.append(add_low(part[:strip], other[:strip]).reshape(thin))
            sent.append(add_low(part[strip:], other[strip:]).reshape(thin))
        return kept, sent

    def own_third(parts, received):
        one, two = [add_low(*pair) for pair in zip(parts, received)]
        return [one[0], one[1], two[0], two[1]]

    def even_third(parts, received):
        total = jnp.concatenate([add_low(*pair) for pair in zip(parts, received)])
        return [
            lax.dynamic_index_in_dim(total, z_place ^ step, axis=0, keepdims=False)
            for step in range(4)
        ]

    def over_outer(total):
        return lax.psum(total, "o") if outer > 1 else total

    def gather_shard(total):
        return lax.all_gather(total, everyone[:3], axis=0, tiled=True)

    def attention_parts(grad_kv, grad_q, grad_o):
        kv = grad_kv.reshape(groups, 2, shard, width_all)
        qo = jnp.stack(
            [
                grad_q.reshape(groups, shard, width_all),
                grad_o.reshape(groups, shard, width_all),
            ],
            axis=1,
        )
        sent = jnp.where(core == 0, qo, kv)
        kept = jnp.where(core == 0, kv, qo)
        return sent, kept

    quarter = shard // 4
    rest = 2 * quarter

    def attention_first(total):
        cut = total.reshape(groups, 2, 2, 2, quarter, width_all)
        one, two = cut[:, 0], cut[:, 1]

        def pick(array, index, axis):
            return lax.dynamic_index_in_dim(array, index, axis, keepdims=False)

        kept = [pick(one, y_bit, 1), pick(two, x_bit, 2)]
        return kept, [pick(one, 1 - y_bit, 1), pick(two, 1 - x_bit, 2)]

    def attention_second(parts, received):
        kept, sent = [], []
        for part, other, bit in zip(parts, received, (x_bit, y_bit)):
            total = add_low(part, other)
            kept.append(lax.dynamic_index_in_dim(total, bit, 1, keepdims=False))
            sent.append(lax.dynamic_index_in_dim(total, 1 - bit, 1, keepdims=False))
        return kept, sent

    def attention_third(parts, received):
        total = jnp.concatenate([add_low(*pair) for pair in zip(parts, received)], axis=1)
        return [total[step] for step in range(4)]

    def attention_gathered(rows):
        cut = rows.reshape(4, 2, 2, quarter, width_all).transpose(1, 2, 0, 3, 4).astype(f32)
        cut = cut.reshape(2, 2, shard, width_all)
        weight_in = jnp.stack([cut[1, 0], cut[0, 0], cut[0, 1]])
        return jnp.swapaxes(weight_in, 1, 2), cut[1, 1]

    def attention_out(whole, received):
        cut = (2, shard, width_all)
        total = paired(core, whole.reshape(cut), received.reshape(cut), 0).astype(f32)
        weight_in = jnp.stack([total[1, 0], total[0, 0], total[0, 1]])
        return jnp.swapaxes(weight_in, 1, 2), total[1, 1]

    def attention_cuts(kept, received):
        place = y_bit * 2 + x_bit

        def cut(array, step):
            return lax.dynamic_slice_in_dim(array, (place ^ step) * quarter, quarter, axis=2)

        return [add_low(cut(kept, step), cut(received, step)) for step in range(4)]

    def attention_sum(cuts, received):
        return add_low(cuts[0], *received).reshape(4, rest, width_all)

    def attention_join(blocks):
        whole = jnp.stack(blocks).reshape(2, 2, 2, quarter, width_all)
        whole = flip_if(y_bit, flip_if(x_bit, whole, 1), 0)
        return whole.transpose(2, 0, 1, 3, 4).reshape(2 * shard, width_all)

    def pack(rows):
        high = rows.astype(bf16)
        low = (rows - lax.optimization_barrier(high).astype(f32)).astype(bf16)
        return lax.optimization_barrier(jnp.concatenate([high, low]))

    def unpack(rows):
        count = rows.shape[0] // 2
        return rows[:count].astype(f32) + rows[count:].astype(f32)

    def four(own, received):
        one, two, three = received
        return (unpack(own) + unpack(one)) + (unpack(two) + unpack(three))

    grad_down = grad_stream.astype(bf16)
    other_rows = [jnp.sum(grad_down.astype(f32), axis=0, keepdims=True)]
    sum_rows = []
    for layer_idx in reversed(range(layer_count)):
        (
            layer_input,
            middle,
            normed,
            queries,
            kv_own,
            kv_other,
            log_total,
            mixed,
            normed_two,
            slopes,
            activated,
        ) = saved[layer_idx]
        weight_kv, weight_q, weight_o = attention_weights[layer_idx]
        first = layer_idx == 0
        steps = jnp.arange(8, dtype=jnp.int32)
        if first:
            place = steps
            later, later_sent = attention_first(add_low(attention_kept, attention_received))
            even_cuts = even_third(unit_parts, unit_received)
            grad_down, later, later_sent, even_cuts = together(
                grad_down, later, later_sent, even_cuts
            )
            later_received = [over("y", later_sent[0]), over("x", later_sent[1])]
            even_received = z_three(even_cuts[1:])
        else:
            place = slice_index ^ ((steps % 4) * 2 + (1 - steps // 4))
        grads = units_backward(
            place,
            grad_down,
            normed_two,
            activated,
            slopes,
            unit_weights[layer_idx],
            unit_shard // 2,
        )
        if first:
            grads, later_received, even_received = together(grads, later_received, even_received)
            later, later_sent = attention_second(later, later_received)
            even_total = over_outer(add_low(even_cuts[0], *even_received))
            grads, later, later_sent, even_total = together(grads, later, later_sent, even_total)
            later_received = [over("x", later_sent[0]), over("y", later_sent[1])]
            even_grads = gather_shard(even_total)
        unit_sent, unit_kept, grad_normed_two, up_bias_grad = grads
        unit_received = over("c", unit_sent)
        order_back = own_order_back if first else even_order_back
        other_rows.append(order_back(up_bias_grad))
        grad_middle, grad_branch, rows = norm_backward(
            middle, grad_normed_two, grad_stream, gains[layer_idx, 1][None, :]
        )
        sum_rows.append(rows)
        grad_o = dot(mixed, grad_branch, (1, 0)).astype(bf16)
        grad_mixed = dot(weight_o, grad_branch, (1, 1)).astype(bf16)
        grad_mixed, grad_o, unit_received = together(grad_mixed, grad_o, unit_received)
        unit_parts, unit_sent = (own_first if first else even_first)(unit_kept, unit_received)
        if first:
            later_received = tie(later_received, grad_mixed)
            later_cuts = attention_third(later, later_received)
            grad_mixed, unit_parts, unit_sent, later_cuts = together(
                grad_mixed, unit_parts, unit_sent, later_cuts
            )
            later_received = z_three(later_cuts[1:])
        else:
            grad_mixed, unit_parts, unit_sent, layer_rows = together(
                grad_mixed, unit_parts, unit_sent, layer_rows
            )
            layer_out = swap_rows(layer_rows)
        unit_received = [over("y", unit_sent[0]), over("x", unit_sent[1])]
        outs = attend_backward(
            info, queries, kv_own, kv_other, mixed, log_total, grad_mixed, groups
        )
        kv_received = over("c", outs[2])
        outs, unit_received = together(outs[:2], unit_received)
        unit_parts, unit_sent = unit_second(unit_parts, unit_received)
        if first:
            later_received = tie(later_received, outs[0])
            later_total = over_outer(add_low(later_cuts[0], *later_received))
            outs, unit_parts, unit_sent, later_total = together(
                outs, unit_parts, unit_sent, later_total
            )
            later_grads = gather_shard(later_total)
        else:
            outs, unit_parts, unit_sent, layer_out = together(
                outs, unit_parts, unit_sent, layer_out
            )
        unit_received = [over("x", unit_sent[0]), over("y", unit_sent[1])]
        grad_queries, grad_kv_own = outs
        grad_kv = add_low(grad_kv_own, kv_received)
        grad_q = dot(grad_queries, normed, (1, 0)).astype(bf16)
        grad_kv_weight = dot(grad_kv, normed, (1, 0)).astype(bf16)
        attention_sent, attention_kept = attention_parts(grad_kv_weight, grad_q, grad_o)
        attention_received = over("c", attention_sent)
        query_bias_grad = jnp.sum(grad_queries.astype(f32), axis=1)
        value_bias_grad = jnp.sum(
            grad_kv.reshape(groups, 2, shard, half)[:, 1].astype(f32), axis=-1
        )
        other_rows.append(z_order(query_bias_grad.reshape(groups, shard)).reshape(1, -1))
        other_rows.append(z_order(value_bias_grad).reshape(1, -1))
        grad_normed = dot(grad_queries, weight_q, (0, 0)) + dot(grad_kv, weight_kv, (0, 0))
        if first:
            other_rows = jnp.concatenate(other_rows)
            grad_normed, attention_received, unit_received, other_rows = together(
                grad_normed, attention_received, unit_received, other_rows
            )
            cuts = attention_cuts(attention_kept, attention_received)
            unit_cuts = own_third(unit_parts, unit_received)
            grad_normed, cuts, unit_cuts = together(grad_normed, cuts, unit_cuts)
            received = yx_three(cuts[1:])
            unit_received = z_three(unit_cuts[1:])
            grad_stream, small = norm_backward(
                layer_input,
                grad_normed,
                grad_middle,
                gains[layer_idx, 0][None, :],
                *sum_rows,
                other_rows,
            )
        else:
            grad_stream, grad_down, rows = norm_backward(
                layer_input, grad_normed, grad_middle, gains[layer_idx, 0][None, :]
            )
            sum_rows.append(rows)
            grad_stream, grad_down, attention_received, unit_received = together(
                grad_stream, grad_down, attention_received, unit_received
            )
    width = width_all
    grad_stream, small, received, unit_received = together(
        grad_stream, small, received, unit_received
    )
    last = attention_sum(cuts, received)
    unit_total = over_outer(add_low(unit_cuts[0], *unit_received))
    sent = [jnp.concatenate([last[k], small]) for k in (1, 2, 3)]
    sent, last, unit_total, grad_stream, even_grads, later_grads = together(
        sent, last, unit_total, grad_stream, even_grads, later_grads
    )
    received = z_three(sent)
    own_grads = gather_shard(unit_total)
    grad_in = swap_rows(grad_stream)
    later_grads = attention_gathered(later_grads)
    received, later_grads = together(received, later_grads)
    last = over_outer(add_low(last[0], *[block[:rest] for block in received]))
    small = pack(over_outer(four(small, [block[rest:] for block in received])))
    sent = jnp.concatenate([last, small])
    received = yx_three([sent] * 3)
    received, grad_in = together(received, grad_in)
    small = pack(four(small, [block[rest:] for block in received]))
    last = attention_join([last] + [block[:rest] for block in received])
    sent = jnp.concatenate([last, small])
    sent, own_grads, even_grads = together(sent, own_grads, even_grads)
    received = over("c", sent)
    up_grads, down_grads = unit_results(own_grads, even_grads)
    received, up_grads, down_grads = together(received, up_grads, down_grads)
    small = unpack(small) + unpack(received[2 * shard :])
    first_grads = attention_out(last, received[: 2 * shard])

    gain_grads = small[0:4].reshape(layer_count, 2, width)
    shift_grads = small[4:8].reshape(layer_count, 2, width)
    output_bias_grads, down_bias_grads = small[8:10], small[10:12]
    up_bias_rows = small[12:20].reshape(layer_count, -1)
    input_bias_rows = small[20:24].reshape(layer_count, 2, width)

    def z_part(array, size):
        return lax.dynamic_slice_in_dim(array, z_place * size, size, axis=-1)

    return (
        layer_out,
        grad_in,
        gain_grads,
        shift_grads,
        jnp.stack([first_grads[0], later_grads[0]]),
        z_part(input_bias_rows, shard),
        jnp.stack([first_grads[1], later_grads[1]]),
        output_bias_grads,
        up_grads,
        z_part(up_bias_rows, unit_shard),
        down_grads,
        down_bias_grads,
    )


def solution(mesh):
    split = mesh.shape["dp"] // 8
    fine = Mesh(
        mesh.devices.reshape(split, 2, 2, 2, mesh.shape["tensor"]), ("o", "y", "x", "c", "z")
    )
    rows = P(("o", "y", "x", "c", "z"), None)
    placed = (
        rows,
        P(("o", "y", "x", "c")),
        P(),
        P(),
        P(None, None, None, "z"),
        P(None, None, "z"),
        P(None, "z", None),
        P(),
        P(None, None, "z"),
        P(None, "z"),
        P(None, "z", None),
        P(),
        rows,
    )
    return jax.shard_map(
        local,
        mesh=fine,
        in_specs=placed,
        out_specs=(rows, rows) + placed[2:12],
        check_vma=False,
    )
```

```python
import functools

import jax
import jax.numpy as jnp
from jax import lax
from jax.experimental import pallas as pl
from jax.experimental.pallas import tpu as pltpu
from jax.sharding import Mesh, PartitionSpec as P

HD = 64
ROWS = 1024
IMAGE = 240

epsilon = 1e-06
masked_score = -1e30
bf16 = jnp.bfloat16
f32 = jnp.float32


def dot(left, right, contract):
    return lax.dot_general(
        left, right, ((contract[:1], contract[1:]), ((), ())), preferred_element_type=f32
    )


def kernel_cost(seconds):
    return pl.CostEstimate(
        flops=int(1.1535e15 * seconds), bytes_accessed=int(3.69e12 * seconds), transcendentals=0
    )


def normalize(values, gain_row, bias_row):
    average = jnp.mean(values, axis=-1, keepdims=True)
    centred = values - average
    variance = jnp.mean(centred * centred, axis=-1, keepdims=True)
    return centred * lax.rsqrt(variance + epsilon) * gain_row + bias_row


def gelu_pair(values):
    size = jnp.abs(values)
    knot = 1.0 / (1.0 + (0.3275911 * 0.5**0.5) * size)
    bell = jnp.exp(values * values * -0.5)
    series = knot * (
        0.127414796
        + knot * (-0.142248368 + knot * (0.7107068705 + knot * (-0.7265760135 + knot * 0.5307027145)))
    )
    tail = series * bell
    normal = jnp.where(values > 0, 1.0 - tail, tail)
    return values * normal, normal + values * bell * 0.3989422804014327


def key_halves(core, own, received):
    first = jnp.where(core == 0, own, received)
    second = jnp.where(core == 0, received, own)
    return first, second


def attend_forward_kernel(info, queries, kv_own, kv_other, mixed, log_total):
    core, valid = info[0], info[1]
    width = queries.shape[0]
    half = kv_own.shape[1]
    key_place = lax.broadcasted_iota(jnp.int32, (half, 1), 0) + half
    key_bias = jnp.where(key_place < valid, 0.0, masked_score).astype(f32)
    for head in range(width // HD):
        rows = slice(head * HD, (head + 1) * HD)
        value_rows = slice(width + head * HD, width + (head + 1) * HD)
        query = queries[rows, :] * jnp.asarray(HD**-0.5, bf16)
        key_one, key_two = key_halves(core, kv_own[rows, :], kv_other[rows, :])
        value_one, value_two = key_halves(core, kv_own[value_rows, :], kv_other[value_rows, :])
        score_one = dot(key_one, query, (0, 0))
        score_two = dot(key_two, query, (0, 0)) + key_bias
        top = jnp.maximum(
            jnp.max(score_one, axis=0, keepdims=True), jnp.max(score_two, axis=0, keepdims=True)
        )
        weight_one = jnp.exp(score_one - top)
        weight_two = jnp.exp(score_two - top)
        total = jnp.sum(weight_one, axis=0, keepdims=True) + jnp.sum(
            weight_two, axis=0, keepdims=True
        )
        out = dot(value_one, weight_one.astype(bf16), (1, 0)) + dot(
            value_two, weight_two.astype(bf16), (1, 0)
        )
        mixed[rows, :] = (out / total).astype(bf16)
        log_total[0, head : head + 1, :] = top + jnp.log(total)


def attend_backward_kernel(
    info, queries, kv_own, kv_other, mixed, log_total, grad_mixed, grad_q, grad_own, grad_other
):
    core, valid = info[0], info[1]
    width = queries.shape[0]
    half = kv_own.shape[1]
    scale = HD**-0.5
    key_place = lax.broadcasted_iota(jnp.int32, (half, 1), 0) + half
    key_bias = jnp.where(key_place < valid, 0.0, masked_score).astype(f32)
    for head in range(width // HD):
        rows = slice(head * HD, (head + 1) * HD)
        value_rows = slice(width + head * HD, width + (head + 1) * HD)
        query = queries[rows, :] * jnp.asarray(scale, bf16)
        grad_out = grad_mixed[rows, :]
        delta = jnp.sum(
            grad_out.astype(f32) * mixed[rows, :].astype(f32), axis=0, keepdims=True
        )
        log_row = log_total[0, head : head + 1, :]
        keys = key_halves(core, kv_own[rows, :], kv_other[rows, :])
        values = key_halves(core, kv_own[value_rows, :], kv_other[value_rows, :])
        grad_query = None
        grad_keys = []
        grad_values = []
        for part in range(2):
            score = dot(keys[part], query, (0, 0))
            if part == 1:
                score = score + key_bias
            probs = jnp.exp(score - log_row)
            grad_values.append(dot(grad_out, probs.astype(bf16), (1, 1)))
            grad_probs = dot(values[part], grad_out, (0, 0))
            grad_score = (probs * (grad_probs - delta)).astype(bf16)
            term = dot(keys[part], grad_score, (1, 0))
            grad_query = term if grad_query is None else grad_query + term
            grad_keys.append(dot(query, grad_score, (1, 1)))
        grad_q[rows, :] = (grad_query * scale).astype(bf16)
        own, other = key_halves(core, *grad_keys)
        grad_own[rows, :] = own
        grad_other[rows, :] = other.astype(bf16)
        own, other = key_halves(core, *grad_values)
        grad_own[value_rows, :] = own
        grad_other[value_rows, :] = other.astype(bf16)


def attention_specs(groups, width, half):
    return dict(
        q=pl.BlockSpec((width, half), lambda g, info: (g, 0)),
        kv=pl.BlockSpec((2 * width, half), lambda g, info: (g, 0)),
        log=pl.BlockSpec((1, 8, half), lambda g, info: (g, 0, 0)),
    )


def attend_forward(info, queries, kv_own, kv_other, groups):
    features, half = queries.shape
    width = features // groups
    specs = attention_specs(groups, width, half)
    return pl.pallas_call(
        attend_forward_kernel,
        grid_spec=pltpu.PrefetchScalarGridSpec(
            num_scalar_prefetch=1,
            grid=(groups,),
            in_specs=[specs["q"], specs["kv"], specs["kv"]],
            out_specs=[specs["q"], specs["log"]],
        ),
        out_shape=[
            jax.ShapeDtypeStruct((features, half), bf16),
            jax.ShapeDtypeStruct((groups, 8, half), f32),
        ],
        compiler_params=pltpu.CompilerParams(vmem_limit_bytes=40 << 20),
        cost_estimate=kernel_cost(14e-6),
        name="attend_forward",
    )(info, queries, kv_own, kv_other)


def attend_backward(info, queries, kv_own, kv_other, mixed, log_total, grad_mixed, groups):
    features, half = queries.shape
    width = features // groups
    specs = attention_specs(groups, width, half)
    return pl.pallas_call(
        attend_backward_kernel,
        grid_spec=pltpu.PrefetchScalarGridSpec(
            num_scalar_prefetch=1,
            grid=(groups,),
            in_specs=[specs["q"], specs["kv"], specs["kv"], specs["q"], specs["log"], specs["q"]],
            out_specs=[specs["q"], specs["kv"], specs["kv"]],
        ),
        out_shape=[
            jax.ShapeDtypeStruct((features, half), bf16),
            jax.ShapeDtypeStruct((2 * features, half), f32),
            jax.ShapeDtypeStruct((2 * features, half), bf16),
        ],
        compiler_params=pltpu.CompilerParams(vmem_limit_bytes=40 << 20),
        cost_estimate=kernel_cost(21e-6),
        name="attend_backward",
    )(info, queries, kv_own, kv_other, mixed, log_total, grad_mixed)


def stream_pieces(pieces, buffer, arrived):
    step = pl.program_id(0)
    rows = buffer.shape[1]

    def copy(index):
        source, offset = pieces[index]
        return pltpu.make_async_copy(
            source.at[pl.ds(offset, rows), :], buffer.at[index % 2], arrived.at[index % 2]
        )

    @pl.when(step == 0)
    def _():
        copy(0).start()

    for index in range(len(pieces) - 1):

        @pl.when(step == index)
        def _(index=index):
            copy(index + 1).start()

    for index in range(len(pieces)):

        @pl.when(step == index)
        def _(index=index):
            copy(index).wait()

    return lax.rem(step, 2)


def list_pieces(refs, rows):
    return [(ref, start) for ref in refs for start in range(0, ref.shape[0], rows)]


def units_forward_kernel(count, rows, normed, middle, unit_bias, down_bias, *refs):
    weights = refs[:count]
    activated, slopes, result, buffer, arrived = refs[count:]
    slot = stream_pieces(list_pieces(weights, rows), buffer, arrived)
    width = normed.shape[1]

    @pl.when(pl.program_id(0) == 0)
    def _():
        result[...] = middle[...] + down_bias[...]

    size = normed.shape[0] // 2
    for start in range(0, 2 * size, size):
        part = slice(start, start + size)
        pre = dot(normed[part, :], buffer[slot, :, :width], (1, 1)) + unit_bias[0]
        act, slope = gelu_pair(pre)
        act = act.astype(bf16)
        activated[part, :] = act
        slopes[part, :] = slope.astype(bf16)
        result[part, :] += dot(act, buffer[slot, :, width:], (1, 0))


def units_forward(normed, middle, unit_bias, down_bias, weights):
    tokens, width = normed.shape
    rows = unit_bias.shape[1]
    steps = unit_bias.shape[0]
    units = rows * steps
    whole = pl.BlockSpec((tokens, width), lambda i: (0, 0))
    block = pl.BlockSpec((tokens, rows), lambda i: (0, i))
    return pl.pallas_call(
        functools.partial(units_forward_kernel, len(weights), rows),
        grid=(steps,),
        in_specs=[
            whole,
            whole,
            pl.BlockSpec((1, 1, rows), lambda i: (i, 0, 0)),
            pl.BlockSpec((1, width), lambda i: (0, 0)),
        ]
        + [pl.BlockSpec(memory_space=pl.ANY)] * len(weights),
        out_specs=[block, block, whole],
        out_shape=[
            jax.ShapeDtypeStruct((tokens, units), bf16),
            jax.ShapeDtypeStruct((tokens, units), bf16),
            jax.ShapeDtypeStruct((tokens, width), f32),
        ],
        scratch_shapes=[
            pltpu.VMEM((2, rows, 2 * width), bf16),
            pltpu.SemaphoreType.DMA((2,)),
        ],
        compiler_params=pltpu.CompilerParams(vmem_limit_bytes=40 << 20),
        cost_estimate=kernel_cost(17e-6),
        name="units_forward",
    )(normed, middle, unit_bias[:, None, :], down_bias, *weights)


def stream_blocks(place, source, buffer, arrived):
    step = pl.program_id(0)
    rows = buffer.shape[1]

    def copy(index):
        offset = pl.multiple_of(place[index] * rows, rows)
        slot = lax.rem(index, 2)
        return pltpu.make_async_copy(
            source.at[pl.ds(offset, rows), :], buffer.at[slot], arrived.at[slot]
        )

    @pl.when(step == 0)
    def _():
        copy(0).start()

    @pl.when(step + 1 < pl.num_programs(0))
    def _():
        copy(step + 1).start()

    copy(step).wait()
    return lax.rem(step, 2)


def units_backward_kernel(count, rows, place, grad_down, normed, activated, slopes, *refs):
    weights = refs[:count]
    sent, kept, grad_normed, bias_grad, buffer, arrived = refs[count:]
    step = pl.program_id(0)
    if count == 1:
        slot = stream_blocks(place, weights[0], buffer, arrived)
    else:
        slot = stream_pieces(list_pieces(weights, rows), buffer, arrived)
    width = normed.shape[1]
    grad_act = dot(grad_down[...], buffer[slot, :, width:], (1, 1))
    grad_hidden = grad_act * slopes[...].astype(f32)
    bias_grad[0] = jnp.sum(grad_hidden, axis=0, keepdims=True)
    grad_hidden = grad_hidden.astype(bf16)

    @pl.when(step == 0)
    def _():
        grad_normed[...] = jnp.zeros_like(grad_normed)

    grad_normed[...] += dot(grad_hidden, buffer[slot, :, :width], (1, 0))
    up = dot(grad_hidden, normed[...], (0, 0)).astype(bf16)
    down = dot(activated[...], grad_down[...], (0, 0)).astype(bf16)

    def store(target):
        target[:, :width] = up
        target[:, width:] = down

    half = pl.num_programs(0) // 2
    pl.when(step < half)(lambda: store(sent))
    pl.when(step >= half)(lambda: store(kept))


def units_backward(place, grad_down, normed, activated, slopes, weights, rows):
    tokens, width = normed.shape
    units = activated.shape[1]
    steps = units // rows
    half = steps // 2
    whole = pl.BlockSpec((tokens, width), lambda i, place: (0, 0))
    block = pl.BlockSpec((tokens, rows), lambda i, place: (0, place[i]))
    return pl.pallas_call(
        functools.partial(units_backward_kernel, len(weights), rows),
        grid_spec=pltpu.PrefetchScalarGridSpec(
            num_scalar_prefetch=1,
            grid=(steps,),
            in_specs=[whole, whole, block, block]
            + [pl.BlockSpec(memory_space=pl.ANY)] * len(weights),
            out_specs=[
                pl.BlockSpec((rows, 2 * width), lambda i, place: (jnp.minimum(i, half - 1), 0)),
                pl.BlockSpec((rows, 2 * width), lambda i, place: (jnp.maximum(i - half, 0), 0)),
                whole,
                pl.BlockSpec((1, 1, rows), lambda i, place: (place[i], 0, 0)),
            ],
            scratch_shapes=[
                pltpu.VMEM((2, rows, 2 * width), bf16),
                pltpu.SemaphoreType.DMA((2,)),
            ],
        ),
        out_shape=[jax.ShapeDtypeStruct((units // 2, 2 * width), bf16)] * 2
        + [
            jax.ShapeDtypeStruct((tokens, width), f32),
            jax.ShapeDtypeStruct((steps, 1, rows), f32),
        ],
        compiler_params=pltpu.CompilerParams(vmem_limit_bytes=40 << 20),
        cost_estimate=kernel_cost(20e-6),
        name="units_backward",
    )(place, grad_down, normed, activated, slopes, *weights)


def norm_backward_kernel(last, values, grad, kept, gain, *refs):
    if last:
        earlier, others, result, packed, sums = refs[:3], refs[3], *refs[4:]
    else:
        result, low, sums = refs
    step = pl.program_id(0)
    block = values[...]
    average = jnp.mean(block, axis=-1, keepdims=True)
    centred = block - average
    scale = lax.rsqrt(jnp.mean(centred * centred, axis=-1, keepdims=True) + epsilon)
    unit = centred * scale
    down = grad[...]
    inner = down * gain[...]
    total = kept[...] + scale * (
        inner
        - jnp.mean(inner, axis=-1, keepdims=True)
        - unit * jnp.mean(inner * unit, axis=-1, keepdims=True)
    )
    result[...] = total

    @pl.when(step == 0)
    def _():
        sums[...] = jnp.zeros_like(sums)

    sums[0:1, :] += jnp.sum(down * unit, axis=0, keepdims=True)
    sums[1:2, :] += jnp.sum(down, axis=0, keepdims=True)
    if not last:
        rounded = total.astype(bf16)
        low[...] = rounded
        sums[2:3, :] += jnp.sum(rounded.astype(f32), axis=0, keepdims=True)
    else:

        @pl.when(step == pl.num_programs(0) - 1)
        def _():
            rows = [sums[0:1, :], earlier[2][0:1, :], earlier[1][0:1, :], earlier[0][0:1, :]]
            rows += [sums[1:2, :], earlier[2][1:2, :], earlier[1][1:2, :], earlier[0][1:2, :]]
            rows += [earlier[2][2:3, :], earlier[0][2:3, :], earlier[1][2:3, :]]
            rows += [others[0:1, :], others[7:11, :], others[1:5, :]]
            rows = jnp.concatenate(rows + [others[11:13, :], others[5:7, :]])
            high = rows.astype(bf16)
            packed[0 : rows.shape[0], :] = high
            packed[rows.shape[0] :, :] = (rows - high.astype(f32)).astype(bf16)


def norm_backward(values, grad, kept, gain, *rows):
    tokens, width = values.shape
    steps = 4
    block = pl.BlockSpec((tokens // steps, width), lambda i: (i, 0))

    def whole(count):
        return pl.BlockSpec((count, width), lambda i: (0, 0))

    last = bool(rows)
    if last:
        count = 2 * (11 + rows[-1].shape[0])
        out_specs = [block, whole(count)]
        out_shape = [
            jax.ShapeDtypeStruct((tokens, width), f32),
            jax.ShapeDtypeStruct((count, width), bf16),
        ]
        scratch = [pltpu.VMEM((8, width), f32)]
    else:
        out_specs = [block, block, whole(8)]
        out_shape = [
            jax.ShapeDtypeStruct((tokens, width), f32),
            jax.ShapeDtypeStruct((tokens, width), bf16),
            jax.ShapeDtypeStruct((8, width), f32),
        ]
        scratch = []
    return pl.pallas_call(
        functools.partial(norm_backward_kernel, last),
        grid=(steps,),
        in_specs=[block, block, block, whole(1)] + [whole(row.shape[0]) for row in rows],
        out_specs=out_specs,
        out_shape=out_shape,
        scratch_shapes=scratch,
        compiler_params=pltpu.CompilerParams(vmem_limit_bytes=24 << 20),
        cost_estimate=kernel_cost(3e-6),
        name="norm_backward",
    )(values, grad, kept, gain, *rows)


def unit_results_kernel(own, even, up, down):
    width = down.shape[2]
    for layer, grads in enumerate((own, even)):
        up[layer] = grads[:, :width].astype(f32).T
        down[layer] = grads[:, width:].astype(f32)


def unit_results(own, even):
    units, double = own.shape
    width = double // 2
    steps = 3
    block = pl.BlockSpec((units // steps, double), lambda i: (i, 0))
    return pl.pallas_call(
        unit_results_kernel,
        grid=(steps,),
        in_specs=[block, block],
        out_specs=[
            pl.BlockSpec((2, width, units // steps), lambda i: (0, 0, i)),
            pl.BlockSpec((2, units // steps, width), lambda i: (0, i, 0)),
        ],
        out_shape=[
            jax.ShapeDtypeStruct((2, width, units), f32),
            jax.ShapeDtypeStruct((2, units, width), f32),
        ],
        compiler_params=pltpu.CompilerParams(vmem_limit_bytes=24 << 20),
        cost_estimate=kernel_cost(5e-6),
        name="unit_results",
    )(own, even)


flip_pair = [(0, 1), (1, 0)]


def over(axis, array):
    return lax.ppermute(array, axis, flip_pair)


def z_send(array, pairs):
    return lax.ppermute(array, "z", pairs)


def z_pairs(step):
    return [(z, z ^ step) for z in range(4)]


def z_three(blocks):
    return [lax.ppermute(block, "z", z_pairs(step + 1)) for step, block in enumerate(blocks)]


def yx_three(blocks):
    across = [(place, 3 - place) for place in range(4)]
    return [
        over("x", blocks[0]),
        over("y", blocks[1]),
        lax.ppermute(blocks[2], ("y", "x"), across),
    ]


def add_low(*terms):
    total = terms[0].astype(f32)
    for term in terms[1:]:
        total = total + term.astype(f32)
    return total.astype(bf16)


def together(*arrays):
    return lax.optimization_barrier(arrays)


def tie(array, *after):
    return lax.optimization_barrier((array, after))[0]


def flip_if(bit, array, axis):
    return jnp.where(bit == 1, jnp.flip(array, axis), array)


def paired(bit, own, received, axis):
    return jnp.stack(
        [jnp.where(bit == 0, own, received), jnp.where(bit == 0, received, own)], axis=axis
    )


def local(
    stream_in,
    patch_size,
    norm_gain,
    norm_bias,
    input_weight,
    input_bias,
    output_weight,
    output_bias,
    up_weight,
    up_bias,
    down_weight,
    down_bias,
    cotangent,
):
    half, width_all = stream_in.shape
    layer_count = input_weight.shape[0]
    shard = input_weight.shape[-1]
    unit_shard = up_weight.shape[-1]
    unit_slice = unit_shard // 8
    groups = lax.axis_size("z")
    outer = lax.axis_size("o")
    core, x_bit, y_bit = lax.axis_index("c"), lax.axis_index("x"), lax.axis_index("y")
    z_place = lax.axis_index("z")
    z_low, z_high = z_place % 2, z_place // 2

    swap = []
    for c in range(2):
        for z in range(groups):
            if c != z % 2:
                swap.append((c * groups + z, (z % 2) * groups + (z - z % 2 + c)))

    def swap_rows(array):
        return jnp.where(z_low == core, array, lax.ppermute(array, ("c", "z"), swap))

    other_patch = over("c", patch_size)
    patch = jnp.where(z_low == core, patch_size, other_patch)
    patch = jnp.where(z_high == 0, patch[0], patch[1])
    grid_side = IMAGE // patch
    valid = grid_side * grid_side
    info = jnp.stack([core, valid]).astype(jnp.int32)

    stream_rows = swap_rows(stream_in)

    def z_order(array):
        pairs = array.reshape((2, 2) + array.shape[1:])
        pairs = flip_if(z_high, flip_if(z_low, pairs, 1), 0)
        return pairs.reshape(array.shape)

    def unit_flip(cut):
        cut = flip_if(z_high, flip_if(z_low, cut, 1), 0)
        return flip_if(y_bit, flip_if(x_bit, flip_if(core, cut, 4), 3), 2)

    def own_order(rows):
        cut = unit_flip(rows.reshape(2, 2, 2, 2, 2, unit_slice))
        cut = jnp.stack([cut[0].transpose(3, 1, 2, 0, 4), cut[1].transpose(3, 2, 1, 0, 4)], axis=1)
        return cut[::-1].reshape(8, unit_shard // 2)

    def own_order_back(pieces):
        cut = pieces.reshape(2, 2, 2, 2, 2, unit_slice)[::-1]
        cut = jnp.stack([cut[:, 0].transpose(3, 1, 2, 0, 4), cut[:, 1].transpose(3, 2, 1, 0, 4)])
        return unit_flip(cut).reshape(groups, unit_shard)

    def even_order(rows):
        cut = rows.reshape(groups, 8, unit_slice).transpose(1, 0, 2)
        return cut.reshape(8, unit_shard // 2)

    def even_order_back(pieces):
        cut = pieces.reshape(8, groups, unit_slice).transpose(1, 0, 2)
        return cut.reshape(groups, unit_shard)

    slice_index = (y_bit * 2 + x_bit) * 2 + core

    part = shard // 2

    def attention_slice(layer_idx):
        first = jnp.where(core == 0, input_weight[layer_idx, 1], input_weight[layer_idx, 0]).T
        second = jnp.where(core == 0, input_weight[layer_idx, 2].T, output_weight[layer_idx])
        return jnp.concatenate(
            [
                lax.dynamic_slice_in_dim(first, x_bit * part, part, axis=0),
                lax.dynamic_slice_in_dim(second, y_bit * part, part, axis=0),
            ]
        )

    def attention_halves(blocks):
        return (
            jnp.stack([block[:part] for block in blocks]),
            jnp.stack([block[part : 2 * part] for block in blocks]),
        )

    def attention_own(first, second, received):
        first = paired(x_bit, first, received[0], 1).reshape(groups, shard, width_all)
        second = paired(y_bit, second, received[1], 1).reshape(groups, shard, width_all)
        return jnp.stack([first, second], axis=1)

    def attention_whole(own):
        received = over("c", own)
        kv = jnp.where(core == 0, own, received)
        qo = jnp.where(core == 0, received, own)
        return (
            kv.reshape(2 * groups * shard, width_all),
            qo[:, 0].reshape(groups * shard, width_all),
            qo[:, 1].reshape(groups * shard, width_all),
        )

    def unit_block(layer_idx):
        up = lax.dynamic_slice_in_dim(
            up_weight[layer_idx], slice_index * unit_slice, unit_slice, axis=1
        )
        down = lax.dynamic_slice_in_dim(
            down_weight[layer_idx], slice_index * unit_slice, unit_slice, axis=0
        )
        return jnp.concatenate([up.T, down], axis=1)

    small_bias = input_bias.reshape(-1, unit_shard)
    bias_count = layer_count + small_bias.shape[0]
    bias_rows = jnp.pad(up_bias, ((0, 16 - layer_count), (0, 0))) + jnp.pad(
        small_bias, ((layer_count, 16 - bias_count), (0, 0))
    )
    everyone = ("y", "x", "c", "z")
    block = jnp.concatenate([attention_slice(0), bias_rows])
    first_blocks = z_three([block] * 3)
    blocks = [block] + first_blocks
    biases = jnp.stack([block[2 * part :] for block in blocks]).astype(f32)
    first, second = attention_halves(blocks)
    own_attention = attention_own(first, second, [over("x", first), over("y", second)])
    block = tie(unit_block(0), first, second)
    unit_blocks = z_three([block] * 3)
    first_weights = attention_whole(own_attention)
    one = tie(jnp.concatenate([block, unit_blocks[0]]), first_weights[0])
    two = tie(jnp.concatenate(unit_blocks[1:]), first_weights[0])
    one = jnp.concatenate([one, over("x", one)])
    two = jnp.concatenate([two, over("y", two)])
    near_units = [over("y", one), over("x", two)]
    even_units = lax.all_gather(
        tie(unit_block(1), *first_blocks), everyone, axis=0, tiled=True
    )
    attention_weights = [first_weights, None]
    unit_weights = [None, [even_units]]
    up_bias_all = z_order(biases[:, :layer_count])
    input_bias_all = biases[:, layer_count : layer_count + input_bias.size // unit_shard].reshape(
        groups, layer_count, 2, shard
    )
    gains = norm_gain.astype(f32)
    shifts = norm_bias.astype(f32)

    stream = stream_rows.astype(f32)
    saved = []
    for layer_idx in range(layer_count):
        if layer_idx == 1:
            attention_weights[1] = attention_whole(own_attention)
        weight_kv, weight_q, weight_o = attention_weights[layer_idx]
        layer_input = stream
        normed = normalize(stream, gains[layer_idx, 0], shifts[layer_idx, 0]).astype(bf16)
        value_bias = input_bias_all[:, layer_idx, 1]
        kv_bias = jnp.stack([jnp.zeros_like(value_bias), value_bias], axis=1).reshape(-1, 1)
        kv_own = (dot(weight_kv, normed, (1, 1)) + kv_bias).astype(bf16)
        if layer_idx == 0:
            later_block = tie(attention_slice(1), kv_own)
            later_blocks = z_three([later_block] * 3)
        kv_other = over("c", kv_own)
        query_bias = input_bias_all[:, layer_idx, 0].reshape(-1, 1)
        queries = (dot(weight_q, normed, (1, 1)) + query_bias).astype(bf16)
        mixed, log_total = attend_forward(info, queries, kv_own, kv_other, groups)
        if layer_idx == 0:
            mixed, log_total, near_units, later_blocks = together(
                mixed, log_total, near_units, later_blocks
            )
            pieces = [one, near_units[0], two, near_units[1]]
            unit_weights[0] = [over("c", piece) for piece in pieces] + pieces
            first, second = attention_halves([later_block, *later_blocks])
        middle = stream + (
            dot(mixed, weight_o, (0, 0)) + output_bias[layer_idx].astype(f32)
        )
        normed_two = normalize(middle, gains[layer_idx, 1], shifts[layer_idx, 1]).astype(bf16)
        order = own_order if layer_idx == 0 else even_order
        if layer_idx == 0:
            unit_weights[0], normed_two, first, second = together(
                unit_weights[0], normed_two, first, second
            )
            received = [over("x", first), over("y", second)]
            cotangent_rows = swap_rows(tie(cotangent, first, second))
        activated, slopes, stream = units_forward(
            normed_two,
            middle,
            order(up_bias_all[:, layer_idx]),
            down_bias[layer_idx].astype(f32)[None, :],
            unit_weights[layer_idx],
        )
        if layer_idx == 0:
            activated, slopes, stream, received, cotangent_rows = together(
                activated, slopes, stream, received, cotangent_rows
            )
            own_attention = attention_own(first, second, received)
        saved.append(
            (
                layer_input,
                middle,
                normed,
                queries,
                kv_own,
                kv_other,
                log_total,
                mixed,
                normed_two,
                slopes,
                activated,
            )
        )
    layer_rows = stream.astype(bf16)

    row_place = core * half + jnp.arange(half, dtype=jnp.int32)
    row_mask = (row_place < valid).astype(f32)[:, None]
    grad_stream = cotangent_rows.astype(f32) * row_mask

    slab = (4, unit_shard // 2, 2 * width_all)
    strip = unit_shard // 4
    thin = (2, unit_slice, 2 * width_all)

    def own_first(kept, received):
        kept, received = kept.reshape(slab), received.reshape(slab)
        parts = [add_low(kept[k], received[k]) for k in range(4)]
        return [parts[0], parts[2]], [parts[1], parts[3]]

    def even_first(kept, received):
        kept, received = kept.reshape(slab), received.reshape(slab)

        def part(rows, blocks):
            return add_low(
                jnp.concatenate([kept[k, rows] for k in blocks]),
                jnp.concatenate([received[k, rows] for k in blocks]),
            )

        one, two = slice(0, strip), slice(strip, 2 * strip)
        return [part(one, (0, 1)), part(two, (0, 2))], [part(one, (2, 3)), part(two, (1, 3))]

    def unit_second(parts, received):
        kept, sent = [], []
        for part, other in zip(parts, received):
            kept.append(add_low(part[:strip], other[:strip]).reshape(thin))
            sent.append(add_low(part[strip:], other[strip:]).reshape(thin))
        return kept, sent

    def own_third(parts, received):
        one, two = [add_low(*pair) for pair in zip(parts, received)]
        return [one[0], one[1], two[0], two[1]]

    def even_third(parts, received):
        total = jnp.concatenate([add_low(*pair) for pair in zip(parts, received)])
        return [
            lax.dynamic_index_in_dim(total, z_place ^ step, axis=0, keepdims=False)
            for step in range(4)
        ]

    def over_outer(total):
        return lax.psum(total, "o") if outer > 1 else total

    def gather_shard(total):
        return lax.all_gather(total, everyone[:3], axis=0, tiled=True)

    def attention_parts(grad_kv, grad_q, grad_o):
        kv = grad_kv.reshape(groups, 2, shard, width_all)
        qo = jnp.stack(
            [
                grad_q.reshape(groups, shard, width_all),
                grad_o.reshape(groups, shard, width_all),
            ],
            axis=1,
        )
        sent = jnp.where(core == 0, qo, kv)
        kept = jnp.where(core == 0, kv, qo)
        return sent, kept

    quarter = shard // 4
    rest = 2 * quarter

    def attention_first(total):
        cut = total.reshape(groups, 2, 2, 2, quarter, width_all)
        one, two = cut[:, 0], cut[:, 1]

        def pick(array, index, axis):
            return lax.dynamic_index_in_dim(array, index, axis, keepdims=False)

        kept = [pick(one, y_bit, 1), pick(two, x_bit, 2)]
        return kept, [pick(one, 1 - y_bit, 1), pick(two, 1 - x_bit, 2)]

    def attention_second(parts, received):
        kept, sent = [], []
        for part, other, bit in zip(parts, received, (x_bit, y_bit)):
            total = add_low(part, other)
            kept.append(lax.dynamic_index_in_dim(total, bit, 1, keepdims=False))
            sent.append(lax.dynamic_index_in_dim(total, 1 - bit, 1, keepdims=False))
        return kept, sent

    def attention_third(parts, received):
        total = jnp.concatenate([add_low(*pair) for pair in zip(parts, received)], axis=1)
        return [total[step] for step in range(4)]

    def attention_gathered(rows):
        cut = rows.reshape(4, 2, 2, quarter, width_all).transpose(1, 2, 0, 3, 4).astype(f32)
        cut = cut.reshape(2, 2, shard, width_all)
        weight_in = jnp.stack([cut[1, 0], cut[0, 0], cut[0, 1]])
        return jnp.swapaxes(weight_in, 1, 2), cut[1, 1]

    def attention_out(whole, received):
        cut = (2, shard, width_all)
        total = paired(core, whole.reshape(cut), received.reshape(cut), 0).astype(f32)
        weight_in = jnp.stack([total[1, 0], total[0, 0], total[0, 1]])
        return jnp.swapaxes(weight_in, 1, 2), total[1, 1]

    def attention_cuts(kept, received):
        place = y_bit * 2 + x_bit

        def cut(array, step):
            return lax.dynamic_slice_in_dim(array, (place ^ step) * quarter, quarter, axis=2)

        return [add_low(cut(kept, step), cut(received, step)) for step in range(4)]

    def attention_sum(cuts, received):
        return add_low(cuts[0], *received).reshape(4, rest, width_all)

    def attention_join(blocks):
        whole = jnp.stack(blocks).reshape(2, 2, 2, quarter, width_all)
        whole = flip_if(y_bit, flip_if(x_bit, whole, 1), 0)
        return whole.transpose(2, 0, 1, 3, 4).reshape(2 * shard, width_all)

    def pack(rows):
        high = rows.astype(bf16)
        low = (rows - lax.optimization_barrier(high).astype(f32)).astype(bf16)
        return lax.optimization_barrier(jnp.concatenate([high, low]))

    def unpack(rows):
        count = rows.shape[0] // 2
        return rows[:count].astype(f32) + rows[count:].astype(f32)

    def four(own, received):
        one, two, three = received
        return (unpack(own) + unpack(one)) + (unpack(two) + unpack(three))

    grad_down = grad_stream.astype(bf16)
    other_rows = [jnp.sum(grad_down.astype(f32), axis=0, keepdims=True)]
    sum_rows = []
    for layer_idx in reversed(range(layer_count)):
        (
            layer_input,
            middle,
            normed,
            queries,
            kv_own,
            kv_other,
            log_total,
            mixed,
            normed_two,
            slopes,
            activated,
        ) = saved[layer_idx]
        weight_kv, weight_q, weight_o = attention_weights[layer_idx]
        first = layer_idx == 0
        steps = jnp.arange(8, dtype=jnp.int32)
        if first:
            place = steps
            later, later_sent = attention_first(add_low(attention_kept, attention_received))
            even_cuts = even_third(unit_parts, unit_received)
            grad_down, later, later_sent, even_cuts = together(
                grad_down, later, later_sent, even_cuts
            )
            later_received = [over("y", later_sent[0]), over("x", later_sent[1])]
            even_received = z_three(even_cuts[1:])
        else:
            place = slice_index ^ ((steps % 4) * 2 + (1 - steps // 4))
        grads = units_backward(
            place,
            grad_down,
            normed_two,
            activated,
            slopes,
            unit_weights[layer_idx],
            unit_shard // 2,
        )
        if first:
            grads, later_received, even_received = together(grads, later_received, even_received)
            later, later_sent = attention_second(later, later_received)
            even_total = over_outer(add_low(even_cuts[0], *even_received))
            grads, later, later_sent, even_total = together(grads, later, later_sent, even_total)
            later_received = [over("x", later_sent[0]), over("y", later_sent[1])]
            even_grads = gather_shard(even_total)
        unit_sent, unit_kept, grad_normed_two, up_bias_grad = grads
        unit_received = over("c", unit_sent)
        order_back = own_order_back if first else even_order_back
        other_rows.append(order_back(up_bias_grad))
        grad_middle, grad_branch, rows = norm_backward(
            middle, grad_normed_two, grad_stream, gains[layer_idx, 1][None, :]
        )
        sum_rows.append(rows)
        grad_o = dot(mixed, grad_branch, (1, 0)).astype(bf16)
        grad_mixed = dot(weight_o, grad_branch, (1, 1)).astype(bf16)
        grad_mixed, grad_o, unit_received = together(grad_mixed, grad_o, unit_received)
        unit_parts, unit_sent = (own_first if first else even_first)(unit_kept, unit_received)
        if first:
            later_received = tie(later_received, grad_mixed)
            later_cuts = attention_third(later, later_received)
            grad_mixed, unit_parts, unit_sent, later_cuts = together(
                grad_mixed, unit_parts, unit_sent, later_cuts
            )
            later_received = z_three(later_cuts[1:])
        else:
            grad_mixed, unit_parts, unit_sent, layer_rows = together(
                grad_mixed, unit_parts, unit_sent, layer_rows
            )
            layer_out = swap_rows(layer_rows)
        unit_received = [over("y", unit_sent[0]), over("x", unit_sent[1])]
        outs = attend_backward(
            info, queries, kv_own, kv_other, mixed, log_total, grad_mixed, groups
        )
        kv_received = over("c", outs[2])
        outs, unit_received = together(outs[:2], unit_received)
        unit_parts, unit_sent = unit_second(unit_parts, unit_received)
        if first:
            later_received = tie(later_received, outs[0])
            later_total = over_outer(add_low(later_cuts[0], *later_received))
            outs, unit_parts, unit_sent, later_total = together(
                outs, unit_parts, unit_sent, later_total
            )
            later_grads = gather_shard(later_total)
        else:
            outs, unit_parts, unit_sent, layer_out = together(
                outs, unit_parts, unit_sent, layer_out
            )
        unit_received = [over("x", unit_sent[0]), over("y", unit_sent[1])]
        grad_queries, grad_kv_own = outs
        grad_kv = add_low(grad_kv_own, kv_received)
        grad_q = dot(grad_queries, normed, (1, 0)).astype(bf16)
        grad_kv_weight = dot(grad_kv, normed, (1, 0)).astype(bf16)
        attention_sent, attention_kept = attention_parts(grad_kv_weight, grad_q, grad_o)
        attention_received = over("c", attention_sent)
        query_bias_grad = jnp.sum(grad_queries.astype(f32), axis=1)
        value_bias_grad = jnp.sum(
            grad_kv.reshape(groups, 2, shard, half)[:, 1].astype(f32), axis=-1
        )
        other_rows.append(z_order(query_bias_grad.reshape(groups, shard)).reshape(1, -1))
        other_rows.append(z_order(value_bias_grad).reshape(1, -1))
        grad_normed = dot(grad_queries, weight_q, (0, 0)) + dot(grad_kv, weight_kv, (0, 0))
        if first:
            other_rows = jnp.concatenate(other_rows)
            grad_normed, attention_received, unit_received, other_rows = together(
                grad_normed, attention_received, unit_received, other_rows
            )
            cuts = attention_cuts(attention_kept, attention_received)
            unit_cuts = own_third(unit_parts, unit_received)
            grad_normed, cuts, unit_cuts = together(grad_normed, cuts, unit_cuts)
            received = yx_three(cuts[1:])
            unit_received = z_three(unit_cuts[1:])
            grad_stream, small = norm_backward(
                layer_input,
                grad_normed,
                grad_middle,
                gains[layer_idx, 0][None, :],
                *sum_rows,
                other_rows,
            )
        else:
            grad_stream, grad_down, rows = norm_backward(
                layer_input, grad_normed, grad_middle, gains[layer_idx, 0][None, :]
            )
            sum_rows.append(rows)
            grad_stream, grad_down, attention_received, unit_received = together(
                grad_stream, grad_down, attention_received, unit_received
            )
    width = width_all
    grad_stream, small, received, unit_received = together(
        grad_stream, small, received, unit_received
    )
    last = attention_sum(cuts, received)
    unit_total = over_outer(add_low(unit_cuts[0], *unit_received))
    sent = [jnp.concatenate([last[k], small]) for k in (1, 2, 3)]
    sent, last, unit_total, grad_stream, even_grads, later_grads = together(
        sent, last, unit_total, grad_stream, even_grads, later_grads
    )
    received = z_three(sent)
    own_grads = gather_shard(unit_total)
    grad_in = swap_rows(grad_stream)
    later_grads = attention_gathered(later_grads)
    received, later_grads = together(received, later_grads)
    last = over_outer(add_low(last[0], *[block[:rest] for block in received]))
    small = pack(over_outer(four(small, [block[rest:] for block in received])))
    sent = jnp.concatenate([last, small])
    received = yx_three([sent] * 3)
    received, grad_in = together(received, grad_in)
    small = pack(four(small, [block[rest:] for block in received]))
    last = attention_join([last] + [block[:rest] for block in received])
    sent = jnp.concatenate([last, small])
    sent, own_grads, even_grads = together(sent, own_grads, even_grads)
    received = over("c", sent)
    up_grads, down_grads = unit_results(own_grads, even_grads)
    received, up_grads, down_grads = together(received, up_grads, down_grads)
    small = unpack(small) + unpack(received[2 * shard :])
    first_grads = attention_out(last, received[: 2 * shard])

    gain_grads = small[0:4].reshape(layer_count, 2, width)
    shift_grads = small[4:8].reshape(layer_count, 2, width)
    output_bias_grads, down_bias_grads = small[8:10], small[10:12]
    up_bias_rows = small[12:20].reshape(layer_count, -1)
    input_bias_rows = small[20:24].reshape(layer_count, 2, width)

    def z_part(array, size):
        return lax.dynamic_slice_in_dim(array, z_place * size, size, axis=-1)

    return (
        layer_out,
        grad_in,
        gain_grads,
        shift_grads,
        jnp.stack([first_grads[0], later_grads[0]]),
        z_part(input_bias_rows, shard),
        jnp.stack([first_grads[1], later_grads[1]]),
        output_bias_grads,
        up_grads,
        z_part(up_bias_rows, unit_shard),
        down_grads,
        down_bias_grads,
    )


def solution(mesh):
    split = mesh.shape["dp"] // 8
    fine = Mesh(
        mesh.devices.reshape(split, 2, 2, 2, mesh.shape["tensor"]), ("o", "y", "x", "c", "z")
    )
    rows = P(("o", "y", "x", "c", "z"), None)
    placed = (
        rows,
        P(("o", "y", "x", "c")),
        P(),
        P(),
        P(None, None, None, "z"),
        P(None, None, "z"),
        P(None, "z", None),
        P(),
        P(None, None, "z"),
        P(None, "z"),
        P(None, "z", None),
        P(),
        rows,
    )
    return jax.shard_map(
        local,
        mesh=fine,
        in_specs=placed,
        out_specs=(rows, rows) + placed[2:12],
        check_vma=False,
    )
```

```python
import functools

import jax
import jax.numpy as jnp
from jax import lax
from jax.experimental import pallas as pl
from jax.experimental.pallas import tpu as pltpu
from jax.sharding import Mesh, PartitionSpec as P

HD = 64
ROWS = 1024
IMAGE = 240

epsilon = 1e-06
masked_score = -1e30
bf16 = jnp.bfloat16
f32 = jnp.float32


def dot(left, right, contract):
    return lax.dot_general(
        left, right, ((contract[:1], contract[1:]), ((), ())), preferred_element_type=f32
    )


def kernel_cost(seconds):
    return pl.CostEstimate(
        flops=int(1.1535e15 * seconds), bytes_accessed=int(3.69e12 * seconds), transcendentals=0
    )


def normalize(values, gain_row, bias_row):
    average = jnp.mean(values, axis=-1, keepdims=True)
    centred = values - average
    variance = jnp.mean(centred * centred, axis=-1, keepdims=True)
    return centred * lax.rsqrt(variance + epsilon) * gain_row + bias_row


def gelu_pair(values):
    size = jnp.abs(values)
    knot = 1.0 / (1.0 + (0.3275911 * 0.5**0.5) * size)
    bell = jnp.exp(values * values * -0.5)
    series = knot * (
        0.127414796
        + knot * (-0.142248368 + knot * (0.7107068705 + knot * (-0.7265760135 + knot * 0.5307027145)))
    )
    tail = series * bell
    normal = jnp.where(values > 0, 1.0 - tail, tail)
    return values * normal, normal + values * bell * 0.3989422804014327


def key_halves(core, own, received):
    first = jnp.where(core == 0, own, received)
    second = jnp.where(core == 0, received, own)
    return first, second


def attend_forward_kernel(info, queries, kv_own, kv_other, mixed, log_total):
    core, valid = info[0], info[1]
    width = queries.shape[0]
    half = kv_own.shape[1]
    key_place = lax.broadcasted_iota(jnp.int32, (half, 1), 0) + half
    key_bias = jnp.where(key_place < valid, 0.0, masked_score).astype(f32)
    for head in range(width // HD):
        rows = slice(head * HD, (head + 1) * HD)
        value_rows = slice(width + head * HD, width + (head + 1) * HD)
        query = queries[rows, :] * jnp.asarray(HD**-0.5, bf16)
        key_one, key_two = key_halves(core, kv_own[rows, :], kv_other[rows, :])
        value_one, value_two = key_halves(core, kv_own[value_rows, :], kv_other[value_rows, :])
        score_one = dot(key_one, query, (0, 0))
        score_two = dot(key_two, query, (0, 0)) + key_bias
        top = jnp.maximum(
            jnp.max(score_one, axis=0, keepdims=True), jnp.max(score_two, axis=0, keepdims=True)
        )
        weight_one = jnp.exp(score_one - top)
        weight_two = jnp.exp(score_two - top)
        total = jnp.sum(weight_one, axis=0, keepdims=True) + jnp.sum(
            weight_two, axis=0, keepdims=True
        )
        out = dot(value_one, weight_one.astype(bf16), (1, 0)) + dot(
            value_two, weight_two.astype(bf16), (1, 0)
        )
        mixed[rows, :] = (out / total).astype(bf16)
        log_total[0, head : head + 1, :] = top + jnp.log(total)


def attend_backward_kernel(
    info, queries, kv_own, kv_other, mixed, log_total, grad_mixed, grad_q, grad_own, grad_other
):
    core, valid = info[0], info[1]
    width = queries.shape[0]
    half = kv_own.shape[1]
    scale = HD**-0.5
    key_place = lax.broadcasted_iota(jnp.int32, (half, 1), 0) + half
    key_bias = jnp.where(key_place < valid, 0.0, masked_score).astype(f32)
    for head in range(width // HD):
        rows = slice(head * HD, (head + 1) * HD)
        value_rows = slice(width + head * HD, width + (head + 1) * HD)
        query = queries[rows, :] * jnp.asarray(scale, bf16)
        grad_out = grad_mixed[rows, :]
        delta = jnp.sum(
            grad_out.astype(f32) * mixed[rows, :].astype(f32), axis=0, keepdims=True
        )
        log_row = log_total[0, head : head + 1, :]
        keys = key_halves(core, kv_own[rows, :], kv_other[rows, :])
        values = key_halves(core, kv_own[value_rows, :], kv_other[value_rows, :])
        grad_query = None
        grad_keys = []
        grad_values = []
        for part in range(2):
            score = dot(keys[part], query, (0, 0))
            if part == 1:
                score = score + key_bias
            probs = jnp.exp(score - log_row)
            grad_values.append(dot(grad_out, probs.astype(bf16), (1, 1)))
            grad_probs = dot(values[part], grad_out, (0, 0))
            grad_score = (probs * (grad_probs - delta)).astype(bf16)
            term = dot(keys[part], grad_score, (1, 0))
            grad_query = term if grad_query is None else grad_query + term
            grad_keys.append(dot(query, grad_score, (1, 1)))
        grad_q[rows, :] = (grad_query * scale).astype(bf16)
        own, other = key_halves(core, *grad_keys)
        grad_own[rows, :] = own
        grad_other[rows, :] = other.astype(bf16)
        own, other = key_halves(core, *grad_values)
        grad_own[value_rows, :] = own
        grad_other[value_rows, :] = other.astype(bf16)


def attention_specs(groups, width, half):
    return dict(
        q=pl.BlockSpec((width, half), lambda g, info: (g, 0)),
        kv=pl.BlockSpec((2 * width, half), lambda g, info: (g, 0)),
        log=pl.BlockSpec((1, 8, half), lambda g, info: (g, 0, 0)),
    )


def attend_forward(info, queries, kv_own, kv_other, groups):
    features, half = queries.shape
    width = features // groups
    specs = attention_specs(groups, width, half)
    return pl.pallas_call(
        attend_forward_kernel,
        grid_spec=pltpu.PrefetchScalarGridSpec(
            num_scalar_prefetch=1,
            grid=(groups,),
            in_specs=[specs["q"], specs["kv"], specs["kv"]],
            out_specs=[specs["q"], specs["log"]],
        ),
        out_shape=[
            jax.ShapeDtypeStruct((features, half), bf16),
            jax.ShapeDtypeStruct((groups, 8, half), f32),
        ],
        compiler_params=pltpu.CompilerParams(vmem_limit_bytes=40 << 20),
        cost_estimate=kernel_cost(14e-6),
        name="attend_forward",
    )(info, queries, kv_own, kv_other)


def attend_backward(info, queries, kv_own, kv_other, mixed, log_total, grad_mixed, groups):
    features, half = queries.shape
    width = features // groups
    specs = attention_specs(groups, width, half)
    return pl.pallas_call(
        attend_backward_kernel,
        grid_spec=pltpu.PrefetchScalarGridSpec(
            num_scalar_prefetch=1,
            grid=(groups,),
            in_specs=[specs["q"], specs["kv"], specs["kv"], specs["q"], specs["log"], specs["q"]],
            out_specs=[specs["q"], specs["kv"], specs["kv"]],
        ),
        out_shape=[
            jax.ShapeDtypeStruct((features, half), bf16),
            jax.ShapeDtypeStruct((2 * features, half), f32),
            jax.ShapeDtypeStruct((2 * features, half), bf16),
        ],
        compiler_params=pltpu.CompilerParams(vmem_limit_bytes=40 << 20),
        cost_estimate=kernel_cost(21e-6),
        name="attend_backward",
    )(info, queries, kv_own, kv_other, mixed, log_total, grad_mixed)


def stream_pieces(pieces, buffer, arrived):
    step = pl.program_id(0)
    rows = buffer.shape[1]

    def copy(index):
        source, offset = pieces[index]
        return pltpu.make_async_copy(
            source.at[pl.ds(offset, rows), :], buffer.at[index % 2], arrived.at[index % 2]
        )

    @pl.when(step == 0)
    def _():
        copy(0).start()

    for index in range(len(pieces) - 1):

        @pl.when(step == index)
        def _(index=index):
            copy(index + 1).start()

    for index in range(len(pieces)):

        @pl.when(step == index)
        def _(index=index):
            copy(index).wait()

    return lax.rem(step, 2)


def list_pieces(refs, rows):
    return [(ref, start) for ref in refs for start in range(0, ref.shape[0], rows)]


def units_forward_kernel(count, rows, normed, middle, unit_bias, down_bias, *refs):
    weights = refs[:count]
    activated, slopes, result, buffer, arrived = refs[count:]
    slot = stream_pieces(list_pieces(weights, rows), buffer, arrived)
    width = normed.shape[1]

    @pl.when(pl.program_id(0) == 0)
    def _():
        result[...] = middle[...] + down_bias[...]

    size = normed.shape[0] // 2
    for start in range(0, 2 * size, size):
        part = slice(start, start + size)
        pre = dot(normed[part, :], buffer[slot, :, :width], (1, 1)) + unit_bias[0]
        act, slope = gelu_pair(pre)
        act = act.astype(bf16)
        activated[part, :] = act
        slopes[part, :] = slope.astype(bf16)
        result[part, :] += dot(act, buffer[slot, :, width:], (1, 0))


def units_forward(normed, middle, unit_bias, down_bias, weights):
    tokens, width = normed.shape
    rows = unit_bias.shape[1]
    steps = unit_bias.shape[0]
    units = rows * steps
    whole = pl.BlockSpec((tokens, width), lambda i: (0, 0))
    block = pl.BlockSpec((tokens, rows), lambda i: (0, i))
    return pl.pallas_call(
        functools.partial(units_forward_kernel, len(weights), rows),
        grid=(steps,),
        in_specs=[
            whole,
            whole,
            pl.BlockSpec((1, 1, rows), lambda i: (i, 0, 0)),
            pl.BlockSpec((1, width), lambda i: (0, 0)),
        ]
        + [pl.BlockSpec(memory_space=pl.ANY)] * len(weights),
        out_specs=[block, block, whole],
        out_shape=[
            jax.ShapeDtypeStruct((tokens, units), bf16),
            jax.ShapeDtypeStruct((tokens, units), bf16),
            jax.ShapeDtypeStruct((tokens, width), f32),
        ],
        scratch_shapes=[
            pltpu.VMEM((2, rows, 2 * width), bf16),
            pltpu.SemaphoreType.DMA((2,)),
        ],
        compiler_params=pltpu.CompilerParams(vmem_limit_bytes=40 << 20),
        cost_estimate=kernel_cost(17e-6),
        name="units_forward",
    )(normed, middle, unit_bias[:, None, :], down_bias, *weights)


def stream_blocks(place, source, buffer, arrived):
    step = pl.program_id(0)
    rows = buffer.shape[1]

    def copy(index):
        offset = pl.multiple_of(place[index] * rows, rows)
        slot = lax.rem(index, 2)
        return pltpu.make_async_copy(
            source.at[pl.ds(offset, rows), :], buffer.at[slot], arrived.at[slot]
        )

    @pl.when(step == 0)
    def _():
        copy(0).start()

    @pl.when(step + 1 < pl.num_programs(0))
    def _():
        copy(step + 1).start()

    copy(step).wait()
    return lax.rem(step, 2)


def units_backward_kernel(count, rows, place, grad_down, normed, activated, slopes, *refs):
    weights = refs[:count]
    sent, kept, grad_normed, bias_grad, buffer, arrived = refs[count:]
    step = pl.program_id(0)
    if count == 1:
        slot = stream_blocks(place, weights[0], buffer, arrived)
    else:
        slot = stream_pieces(list_pieces(weights, rows), buffer, arrived)
    width = normed.shape[1]
    grad_act = dot(grad_down[...], buffer[slot, :, width:], (1, 1))
    grad_hidden = grad_act * slopes[...].astype(f32)
    bias_grad[0] = jnp.sum(grad_hidden, axis=0, keepdims=True)
    grad_hidden = grad_hidden.astype(bf16)

    @pl.when(step == 0)
    def _():
        grad_normed[...] = jnp.zeros_like(grad_normed)

    grad_normed[...] += dot(grad_hidden, buffer[slot, :, :width], (1, 0))
    up = dot(grad_hidden, normed[...], (0, 0)).astype(bf16)
    down = dot(activated[...], grad_down[...], (0, 0)).astype(bf16)

    def store(target):
        target[:, :width] = up
        target[:, width:] = down

    half = pl.num_programs(0) // 2
    pl.when(step < half)(lambda: store(sent))
    pl.when(step >= half)(lambda: store(kept))


def units_backward(place, grad_down, normed, activated, slopes, weights, rows):
    tokens, width = normed.shape
    units = activated.shape[1]
    steps = units // rows
    half = steps // 2
    whole = pl.BlockSpec((tokens, width), lambda i, place: (0, 0))
    block = pl.BlockSpec((tokens, rows), lambda i, place: (0, place[i]))
    return pl.pallas_call(
        functools.partial(units_backward_kernel, len(weights), rows),
        grid_spec=pltpu.PrefetchScalarGridSpec(
            num_scalar_prefetch=1,
            grid=(steps,),
            in_specs=[whole, whole, block, block]
            + [pl.BlockSpec(memory_space=pl.ANY)] * len(weights),
            out_specs=[
                pl.BlockSpec((rows, 2 * width), lambda i, place: (jnp.minimum(i, half - 1), 0)),
                pl.BlockSpec((rows, 2 * width), lambda i, place: (jnp.maximum(i - half, 0), 0)),
                whole,
                pl.BlockSpec((1, 1, rows), lambda i, place: (place[i], 0, 0)),
            ],
            scratch_shapes=[
                pltpu.VMEM((2, rows, 2 * width), bf16),
                pltpu.SemaphoreType.DMA((2,)),
            ],
        ),
        out_shape=[jax.ShapeDtypeStruct((units // 2, 2 * width), bf16)] * 2
        + [
            jax.ShapeDtypeStruct((tokens, width), f32),
            jax.ShapeDtypeStruct((steps, 1, rows), f32),
        ],
        compiler_params=pltpu.CompilerParams(vmem_limit_bytes=40 << 20),
        cost_estimate=kernel_cost(20e-6),
        name="units_backward",
    )(place, grad_down, normed, activated, slopes, *weights)


def norm_backward_kernel(last, values, grad, kept, gain, *refs):
    if last:
        earlier, others, result, packed, sums = refs[:3], refs[3], *refs[4:]
    else:
        result, low, sums = refs
    step = pl.program_id(0)
    block = values[...]
    average = jnp.mean(block, axis=-1, keepdims=True)
    centred = block - average
    scale = lax.rsqrt(jnp.mean(centred * centred, axis=-1, keepdims=True) + epsilon)
    unit = centred * scale
    down = grad[...]
    inner = down * gain[...]
    total = kept[...] + scale * (
        inner
        - jnp.mean(inner, axis=-1, keepdims=True)
        - unit * jnp.mean(inner * unit, axis=-1, keepdims=True)
    )
    result[...] = total

    @pl.when(step == 0)
    def _():
        sums[...] = jnp.zeros_like(sums)

    sums[0:1, :] += jnp.sum(down * unit, axis=0, keepdims=True)
    sums[1:2, :] += jnp.sum(down, axis=0, keepdims=True)
    if not last:
        rounded = total.astype(bf16)
        low[...] = rounded
        sums[2:3, :] += jnp.sum(rounded.astype(f32), axis=0, keepdims=True)
    else:

        @pl.when(step == pl.num_programs(0) - 1)
        def _():
            rows = [sums[0:1, :], earlier[2][0:1, :], earlier[1][0:1, :], earlier[0][0:1, :]]
            rows += [sums[1:2, :], earlier[2][1:2, :], earlier[1][1:2, :], earlier[0][1:2, :]]
            rows += [earlier[2][2:3, :], earlier[0][2:3, :], earlier[1][2:3, :]]
            rows += [others[0:1, :], others[7:11, :], others[1:5, :]]
            rows = jnp.concatenate(rows + [others[11:13, :], others[5:7, :]])
            high = rows.astype(bf16)
            packed[0 : rows.shape[0], :] = high
            packed[rows.shape[0] :, :] = (rows - high.astype(f32)).astype(bf16)


def norm_backward(values, grad, kept, gain, *rows):
    tokens, width = values.shape
    steps = 4
    block = pl.BlockSpec((tokens // steps, width), lambda i: (i, 0))

    def whole(count):
        return pl.BlockSpec((count, width), lambda i: (0, 0))

    last = bool(rows)
    if last:
        count = 2 * (11 + rows[-1].shape[0])
        out_specs = [block, whole(count)]
        out_shape = [
            jax.ShapeDtypeStruct((tokens, width), f32),
            jax.ShapeDtypeStruct((count, width), bf16),
        ]
        scratch = [pltpu.VMEM((8, width), f32)]
    else:
        out_specs = [block, block, whole(8)]
        out_shape = [
            jax.ShapeDtypeStruct((tokens, width), f32),
            jax.ShapeDtypeStruct((tokens, width), bf16),
            jax.ShapeDtypeStruct((8, width), f32),
        ]
        scratch = []
    return pl.pallas_call(
        functools.partial(norm_backward_kernel, last),
        grid=(steps,),
        in_specs=[block, block, block, whole(1)] + [whole(row.shape[0]) for row in rows],
        out_specs=out_specs,
        out_shape=out_shape,
        scratch_shapes=scratch,
        compiler_params=pltpu.CompilerParams(vmem_limit_bytes=24 << 20),
        cost_estimate=kernel_cost(3e-6),
        name="norm_backward",
    )(values, grad, kept, gain, *rows)


def unit_results_kernel(grads, *refs):
    up, down = refs[-2:]
    width = down.shape[2]
    up[0] = grads[:, :width].astype(f32).T
    down[0] = grads[:, width:].astype(f32)


def unit_results(layer, grads, *started):
    units, double = grads.shape
    width = double // 2
    steps = 3
    rows = units // steps
    return pl.pallas_call(
        unit_results_kernel,
        grid=(steps,),
        in_specs=[pl.BlockSpec((rows, double), lambda i: (i, 0))]
        + [pl.BlockSpec(memory_space=pl.ANY)] * len(started),
        out_specs=[
            pl.BlockSpec((1, width, rows), lambda i: (layer, 0, i)),
            pl.BlockSpec((1, rows, width), lambda i: (layer, i, 0)),
        ],
        out_shape=[
            jax.ShapeDtypeStruct((2, width, units), f32),
            jax.ShapeDtypeStruct((2, units, width), f32),
        ],
        input_output_aliases={1 + k: k for k in range(len(started))},
        compiler_params=pltpu.CompilerParams(vmem_limit_bytes=24 << 20),
        cost_estimate=kernel_cost(3e-6),
        name="unit_results",
    )(grads, *started)


flip_pair = [(0, 1), (1, 0)]


def over(axis, array):
    return lax.ppermute(array, axis, flip_pair)


def z_send(array, pairs):
    return lax.ppermute(array, "z", pairs)


def z_pairs(step):
    return [(z, z ^ step) for z in range(4)]


def z_three(blocks):
    return [lax.ppermute(block, "z", z_pairs(step + 1)) for step, block in enumerate(blocks)]


def yx_three(blocks):
    across = [(place, 3 - place) for place in range(4)]
    return [
        over("x", blocks[0]),
        over("y", blocks[1]),
        lax.ppermute(blocks[2], ("y", "x"), across),
    ]


def add_low(*terms):
    total = terms[0].astype(f32)
    for term in terms[1:]:
        total = total + term.astype(f32)
    return total.astype(bf16)


def together(*arrays):
    return lax.optimization_barrier(arrays)


def tie(array, *after):
    return lax.optimization_barrier((array, after))[0]


def flip_if(bit, array, axis):
    return jnp.where(bit == 1, jnp.flip(array, axis), array)


def paired(bit, own, received, axis):
    return jnp.stack(
        [jnp.where(bit == 0, own, received), jnp.where(bit == 0, received, own)], axis=axis
    )


def local(
    stream_in,
    patch_size,
    norm_gain,
    norm_bias,
    input_weight,
    input_bias,
    output_weight,
    output_bias,
    up_weight,
    up_bias,
    down_weight,
    down_bias,
    cotangent,
):
    half, width_all = stream_in.shape
    layer_count = input_weight.shape[0]
    shard = input_weight.shape[-1]
    unit_shard = up_weight.shape[-1]
    unit_slice = unit_shard // 8
    groups = lax.axis_size("z")
    outer = lax.axis_size("o")
    core, x_bit, y_bit = lax.axis_index("c"), lax.axis_index("x"), lax.axis_index("y")
    z_place = lax.axis_index("z")
    z_low, z_high = z_place % 2, z_place // 2

    swap = []
    for c in range(2):
        for z in range(groups):
            if c != z % 2:
                swap.append((c * groups + z, (z % 2) * groups + (z - z % 2 + c)))

    def swap_rows(array):
        return jnp.where(z_low == core, array, lax.ppermute(array, ("c", "z"), swap))

    other_patch = over("c", patch_size)
    patch = jnp.where(z_low == core, patch_size, other_patch)
    patch = jnp.where(z_high == 0, patch[0], patch[1])
    grid_side = IMAGE // patch
    valid = grid_side * grid_side
    info = jnp.stack([core, valid]).astype(jnp.int32)

    stream_rows = swap_rows(stream_in)

    def z_order(array):
        pairs = array.reshape((2, 2) + array.shape[1:])
        pairs = flip_if(z_high, flip_if(z_low, pairs, 1), 0)
        return pairs.reshape(array.shape)

    def unit_flip(cut):
        cut = flip_if(z_high, flip_if(z_low, cut, 1), 0)
        return flip_if(y_bit, flip_if(x_bit, flip_if(core, cut, 4), 3), 2)

    def own_order(rows):
        cut = unit_flip(rows.reshape(2, 2, 2, 2, 2, unit_slice))
        cut = jnp.stack([cut[0].transpose(3, 1, 2, 0, 4), cut[1].transpose(3, 2, 1, 0, 4)], axis=1)
        return cut[::-1].reshape(8, unit_shard // 2)

    def own_order_back(pieces):
        cut = pieces.reshape(2, 2, 2, 2, 2, unit_slice)[::-1]
        cut = jnp.stack([cut[:, 0].transpose(3, 1, 2, 0, 4), cut[:, 1].transpose(3, 2, 1, 0, 4)])
        return unit_flip(cut).reshape(groups, unit_shard)

    def even_order(rows):
        cut = rows.reshape(groups, 8, unit_slice).transpose(1, 0, 2)
        return cut.reshape(8, unit_shard // 2)

    def even_order_back(pieces):
        cut = pieces.reshape(8, groups, unit_slice).transpose(1, 0, 2)
        return cut.reshape(groups, unit_shard)

    slice_index = (y_bit * 2 + x_bit) * 2 + core

    part = shard // 2

    def attention_slice(layer_idx):
        first = jnp.where(core == 0, input_weight[layer_idx, 1], input_weight[layer_idx, 0]).T
        second = jnp.where(core == 0, input_weight[layer_idx, 2].T, output_weight[layer_idx])
        return jnp.concatenate(
            [
                lax.dynamic_slice_in_dim(first, x_bit * part, part, axis=0),
                lax.dynamic_slice_in_dim(second, y_bit * part, part, axis=0),
            ]
        )

    def attention_halves(blocks):
        return (
            jnp.stack([block[:part] for block in blocks]),
            jnp.stack([block[part : 2 * part] for block in blocks]),
        )

    def attention_own(first, second, received):
        first = paired(x_bit, first, received[0], 1).reshape(groups, shard, width_all)
        second = paired(y_bit, second, received[1], 1).reshape(groups, shard, width_all)
        return jnp.stack([first, second], axis=1)

    def attention_whole(own):
        received = over("c", own)
        kv = jnp.where(core == 0, own, received)
        qo = jnp.where(core == 0, received, own)
        return (
            kv.reshape(2 * groups * shard, width_all),
            qo[:, 0].reshape(groups * shard, width_all),
            qo[:, 1].reshape(groups * shard, width_all),
        )

    def unit_block(layer_idx):
        up = lax.dynamic_slice_in_dim(
            up_weight[layer_idx], slice_index * unit_slice, unit_slice, axis=1
        )
        down = lax.dynamic_slice_in_dim(
            down_weight[layer_idx], slice_index * unit_slice, unit_slice, axis=0
        )
        return jnp.concatenate([up.T, down], axis=1)

    small_bias = input_bias.reshape(-1, unit_shard)
    bias_count = layer_count + small_bias.shape[0]
    bias_rows = jnp.pad(up_bias, ((0, 16 - layer_count), (0, 0))) + jnp.pad(
        small_bias, ((layer_count, 16 - bias_count), (0, 0))
    )
    everyone = ("y", "x", "c", "z")
    block = jnp.concatenate([attention_slice(0), bias_rows])
    first_blocks = z_three([block] * 3)
    blocks = [block] + first_blocks
    biases = jnp.stack([block[2 * part :] for block in blocks]).astype(f32)
    first, second = attention_halves(blocks)
    own_attention = attention_own(first, second, [over("x", first), over("y", second)])
    block = tie(unit_block(0), first, second)
    unit_blocks = z_three([block] * 3)
    first_weights = attention_whole(own_attention)
    one = tie(jnp.concatenate([block, unit_blocks[0]]), first_weights[0])
    two = tie(jnp.concatenate(unit_blocks[1:]), first_weights[0])
    one = jnp.concatenate([one, over("x", one)])
    two = jnp.concatenate([two, over("y", two)])
    near_units = [over("y", one), over("x", two)]
    even_units = lax.all_gather(
        tie(unit_block(1), *first_blocks), everyone, axis=0, tiled=True
    )
    attention_weights = [first_weights, None]
    unit_weights = [None, [even_units]]
    up_bias_all = z_order(biases[:, :layer_count])
    input_bias_all = biases[:, layer_count : layer_count + input_bias.size // unit_shard].reshape(
        groups, layer_count, 2, shard
    )
    gains = norm_gain.astype(f32)
    shifts = norm_bias.astype(f32)

    stream = stream_rows.astype(f32)
    saved = []
    for layer_idx in range(layer_count):
        if layer_idx == 1:
            attention_weights[1] = attention_whole(own_attention)
        weight_kv, weight_q, weight_o = attention_weights[layer_idx]
        layer_input = stream
        normed = normalize(stream, gains[layer_idx, 0], shifts[layer_idx, 0]).astype(bf16)
        value_bias = input_bias_all[:, layer_idx, 1]
        kv_bias = jnp.stack([jnp.zeros_like(value_bias), value_bias], axis=1).reshape(-1, 1)
        kv_own = (dot(weight_kv, normed, (1, 1)) + kv_bias).astype(bf16)
        if layer_idx == 0:
            later_block = tie(attention_slice(1), kv_own)
            later_blocks = z_three([later_block] * 3)
        kv_other = over("c", kv_own)
        query_bias = input_bias_all[:, layer_idx, 0].reshape(-1, 1)
        queries = (dot(weight_q, normed, (1, 1)) + query_bias).astype(bf16)
        mixed, log_total = attend_forward(info, queries, kv_own, kv_other, groups)
        if layer_idx == 0:
            mixed, log_total, near_units, later_blocks = together(
                mixed, log_total, near_units, later_blocks
            )
            pieces = [one, near_units[0], two, near_units[1]]
            unit_weights[0] = [over("c", piece) for piece in pieces] + pieces
            first, second = attention_halves([later_block, *later_blocks])
        middle = stream + (
            dot(mixed, weight_o, (0, 0)) + output_bias[layer_idx].astype(f32)
        )
        normed_two = normalize(middle, gains[layer_idx, 1], shifts[layer_idx, 1]).astype(bf16)
        order = own_order if layer_idx == 0 else even_order
        if layer_idx == 0:
            unit_weights[0], normed_two, first, second = together(
                unit_weights[0], normed_two, first, second
            )
            received = [over("x", first), over("y", second)]
            cotangent_rows = swap_rows(tie(cotangent, first, second))
        activated, slopes, stream = units_forward(
            normed_two,
            middle,
            order(up_bias_all[:, layer_idx]),
            down_bias[layer_idx].astype(f32)[None, :],
            unit_weights[layer_idx],
        )
        if layer_idx == 0:
            activated, slopes, stream, received, cotangent_rows = together(
                activated, slopes, stream, received, cotangent_rows
            )
            own_attention = attention_own(first, second, received)
        saved.append(
            (
                layer_input,
                middle,
                normed,
                queries,
                kv_own,
                kv_other,
                log_total,
                mixed,
                normed_two,
                slopes,
                activated,
            )
        )
    layer_rows = stream.astype(bf16)

    row_place = core * half + jnp.arange(half, dtype=jnp.int32)
    row_mask = (row_place < valid).astype(f32)[:, None]
    grad_stream = cotangent_rows.astype(f32) * row_mask

    slab = (4, unit_shard // 2, 2 * width_all)
    strip = unit_shard // 4
    thin = (2, unit_slice, 2 * width_all)

    def own_first(kept, received):
        kept, received = kept.reshape(slab), received.reshape(slab)
        parts = [add_low(kept[k], received[k]) for k in range(4)]
        return [parts[0], parts[2]], [parts[1], parts[3]]

    def even_first(kept, received):
        kept, received = kept.reshape(slab), received.reshape(slab)

        def part(rows, blocks):
            return add_low(
                jnp.concatenate([kept[k, rows] for k in blocks]),
                jnp.concatenate([received[k, rows] for k in blocks]),
            )

        one, two = slice(0, strip), slice(strip, 2 * strip)
        return [part(one, (0, 1)), part(two, (0, 2))], [part(one, (2, 3)), part(two, (1, 3))]

    def unit_second(parts, received):
        kept, sent = [], []
        for part, other in zip(parts, received):
            kept.append(add_low(part[:strip], other[:strip]).reshape(thin))
            sent.append(add_low(part[strip:], other[strip:]).reshape(thin))
        return kept, sent

    def own_third(parts, received):
        one, two = [add_low(*pair) for pair in zip(parts, received)]
        return [one[0], one[1], two[0], two[1]]

    def even_third(parts, received):
        total = jnp.concatenate([add_low(*pair) for pair in zip(parts, received)])
        return [
            lax.dynamic_index_in_dim(total, z_place ^ step, axis=0, keepdims=False)
            for step in range(4)
        ]

    def over_outer(total):
        return lax.psum(total, "o") if outer > 1 else total

    def gather_shard(total):
        return lax.all_gather(total, everyone[:3], axis=0, tiled=True)

    def attention_parts(grad_kv, grad_q, grad_o):
        kv = grad_kv.reshape(groups, 2, shard, width_all)
        qo = jnp.stack(
            [
                grad_q.reshape(groups, shard, width_all),
                grad_o.reshape(groups, shard, width_all),
            ],
            axis=1,
        )
        sent = jnp.where(core == 0, qo, kv)
        kept = jnp.where(core == 0, kv, qo)
        return sent, kept

    quarter = shard // 4
    rest = 2 * quarter

    def attention_first(total):
        cut = total.reshape(groups, 2, 2, 2, quarter, width_all)
        one, two = cut[:, 0], cut[:, 1]

        def pick(array, index, axis):
            return lax.dynamic_index_in_dim(array, index, axis, keepdims=False)

        kept = [pick(one, y_bit, 1), pick(two, x_bit, 2)]
        return kept, [pick(one, 1 - y_bit, 1), pick(two, 1 - x_bit, 2)]

    def attention_second(parts, received):
        kept, sent = [], []
        for part, other, bit in zip(parts, received, (x_bit, y_bit)):
            total = add_low(part, other)
            kept.append(lax.dynamic_index_in_dim(total, bit, 1, keepdims=False))
            sent.append(lax.dynamic_index_in_dim(total, 1 - bit, 1, keepdims=False))
        return kept, sent

    def attention_third(parts, received):
        total = jnp.concatenate([add_low(*pair) for pair in zip(parts, received)], axis=1)
        return [total[step] for step in range(4)]

    def attention_gathered(rows):
        cut = rows.reshape(4, 2, 2, quarter, width_all).transpose(1, 2, 0, 3, 4).astype(f32)
        cut = cut.reshape(2, 2, shard, width_all)
        weight_in = jnp.stack([cut[1, 0], cut[0, 0], cut[0, 1]])
        return jnp.swapaxes(weight_in, 1, 2), cut[1, 1]

    def attention_out(whole, received):
        cut = (2, shard, width_all)
        total = paired(core, whole.reshape(cut), received.reshape(cut), 0).astype(f32)
        weight_in = jnp.stack([total[1, 0], total[0, 0], total[0, 1]])
        return jnp.swapaxes(weight_in, 1, 2), total[1, 1]

    def attention_cuts(kept, received):
        place = y_bit * 2 + x_bit

        def cut(array, step):
            return lax.dynamic_slice_in_dim(array, (place ^ step) * quarter, quarter, axis=2)

        return [add_low(cut(kept, step), cut(received, step)) for step in range(4)]

    def attention_sum(cuts, received):
        return add_low(cuts[0], *received).reshape(4, rest, width_all)

    def attention_join(blocks):
        whole = jnp.stack(blocks).reshape(2, 2, 2, quarter, width_all)
        whole = flip_if(y_bit, flip_if(x_bit, whole, 1), 0)
        return whole.transpose(2, 0, 1, 3, 4).reshape(2 * shard, width_all)

    def pack(rows):
        high = rows.astype(bf16)
        low = (rows - lax.optimization_barrier(high).astype(f32)).astype(bf16)
        return lax.optimization_barrier(jnp.concatenate([high, low]))

    def unpack(rows):
        count = rows.shape[0] // 2
        return rows[:count].astype(f32) + rows[count:].astype(f32)

    def four(own, received):
        one, two, three = received
        return (unpack(own) + unpack(one)) + (unpack(two) + unpack(three))

    grad_down = grad_stream.astype(bf16)
    other_rows = [jnp.sum(grad_down.astype(f32), axis=0, keepdims=True)]
    sum_rows = []
    for layer_idx in reversed(range(layer_count)):
        (
            layer_input,
            middle,
            normed,
            queries,
            kv_own,
            kv_other,
            log_total,
            mixed,
            normed_two,
            slopes,
            activated,
        ) = saved[layer_idx]
        weight_kv, weight_q, weight_o = attention_weights[layer_idx]
        first = layer_idx == 0
        steps = jnp.arange(8, dtype=jnp.int32)
        if first:
            place = steps
            later, later_sent = attention_first(add_low(attention_kept, attention_received))
            even_cuts = even_third(unit_parts, unit_received)
            grad_down, later, later_sent, even_cuts = together(
                grad_down, later, later_sent, even_cuts
            )
            later_received = [over("y", later_sent[0]), over("x", later_sent[1])]
            even_received = z_three(even_cuts[1:])
        else:
            place = slice_index ^ ((steps % 4) * 2 + (1 - steps // 4))
        grads = units_backward(
            place,
            grad_down,
            normed_two,
            activated,
            slopes,
            unit_weights[layer_idx],
            unit_shard // 2,
        )
        if first:
            grads, later_received, even_received = together(grads, later_received, even_received)
            later, later_sent = attention_second(later, later_received)
            even_total = over_outer(add_low(even_cuts[0], *even_received))
            grads, later, later_sent, even_total = together(grads, later, later_sent, even_total)
            later_received = [over("x", later_sent[0]), over("y", later_sent[1])]
            even_grads = gather_shard(even_total)
        unit_sent, unit_kept, grad_normed_two, up_bias_grad = grads
        unit_received = over("c", unit_sent)
        order_back = own_order_back if first else even_order_back
        other_rows.append(order_back(up_bias_grad))
        grad_middle, grad_branch, rows = norm_backward(
            middle, grad_normed_two, grad_stream, gains[layer_idx, 1][None, :]
        )
        sum_rows.append(rows)
        grad_o = dot(mixed, grad_branch, (1, 0)).astype(bf16)
        grad_mixed = dot(weight_o, grad_branch, (1, 1)).astype(bf16)
        grad_mixed, grad_o, unit_received = together(grad_mixed, grad_o, unit_received)
        unit_parts, unit_sent = (own_first if first else even_first)(unit_kept, unit_received)
        if first:
            later_received = tie(later_received, grad_mixed)
            later_cuts = attention_third(later, later_received)
            grad_mixed, unit_parts, unit_sent, later_cuts = together(
                grad_mixed, unit_parts, unit_sent, later_cuts
            )
            later_received = z_three(later_cuts[1:])
        else:
            grad_mixed, unit_parts, unit_sent, layer_rows = together(
                grad_mixed, unit_parts, unit_sent, layer_rows
            )
            layer_out = swap_rows(layer_rows)
        unit_received = [over("y", unit_sent[0]), over("x", unit_sent[1])]
        outs = attend_backward(
            info, queries, kv_own, kv_other, mixed, log_total, grad_mixed, groups
        )
        kv_received = over("c", outs[2])
        outs, unit_received = together(outs[:2], unit_received)
        unit_parts, unit_sent = unit_second(unit_parts, unit_received)
        if first:
            later_received = tie(later_received, outs[0])
            later_total = over_outer(add_low(later_cuts[0], *later_received))
            outs, unit_parts, unit_sent, later_total = together(
                outs, unit_parts, unit_sent, later_total
            )
            later_grads = gather_shard(later_total)
        else:
            outs, unit_parts, unit_sent, layer_out = together(
                outs, unit_parts, unit_sent, layer_out
            )
        unit_received = [over("x", unit_sent[0]), over("y", unit_sent[1])]
        grad_queries, grad_kv_own = outs
        grad_kv = add_low(grad_kv_own, kv_received)
        grad_q = dot(grad_queries, normed, (1, 0)).astype(bf16)
        grad_kv_weight = dot(grad_kv, normed, (1, 0)).astype(bf16)
        attention_sent, attention_kept = attention_parts(grad_kv_weight, grad_q, grad_o)
        attention_received = over("c", attention_sent)
        query_bias_grad = jnp.sum(grad_queries.astype(f32), axis=1)
        value_bias_grad = jnp.sum(
            grad_kv.reshape(groups, 2, shard, half)[:, 1].astype(f32), axis=-1
        )
        other_rows.append(z_order(query_bias_grad.reshape(groups, shard)).reshape(1, -1))
        other_rows.append(z_order(value_bias_grad).reshape(1, -1))
        grad_normed = dot(grad_queries, weight_q, (0, 0)) + dot(grad_kv, weight_kv, (0, 0))
        if first:
            other_rows = jnp.concatenate(other_rows)
            grad_normed, attention_received, unit_received, other_rows = together(
                grad_normed, attention_received, unit_received, other_rows
            )
            cuts = attention_cuts(attention_kept, attention_received)
            unit_cuts = own_third(unit_parts, unit_received)
            grad_normed, cuts, unit_cuts = together(grad_normed, cuts, unit_cuts)
            received = yx_three(cuts[1:])
            unit_received = z_three(unit_cuts[1:])
            grad_stream, small = norm_backward(
                layer_input,
                grad_normed,
                grad_middle,
                gains[layer_idx, 0][None, :],
                *sum_rows,
                other_rows,
            )
        else:
            grad_stream, grad_down, rows = norm_backward(
                layer_input, grad_normed, grad_middle, gains[layer_idx, 0][None, :]
            )
            sum_rows.append(rows)
            grad_stream, grad_down, attention_received, unit_received = together(
                grad_stream, grad_down, attention_received, unit_received
            )
    width = width_all
    small = pack(unpack(small) + unpack(over("c", small)))
    grad_stream, small, received, unit_received = together(
        grad_stream, small, received, unit_received
    )
    last = attention_sum(cuts, received)
    unit_total = over_outer(add_low(unit_cuts[0], *unit_received))
    sent = [jnp.concatenate([last[k], small]) for k in (1, 2, 3)]
    sent, last, unit_total, grad_stream, even_grads, later_grads = together(
        sent, last, unit_total, grad_stream, even_grads, later_grads
    )
    received = z_three(sent)
    own_grads = gather_shard(unit_total)
    grad_in = swap_rows(grad_stream)
    later_grads = attention_gathered(later_grads)
    received, later_grads = together(received, later_grads)
    last = over_outer(add_low(last[0], *[block[:rest] for block in received]))
    small = pack(over_outer(four(small, [block[rest:] for block in received])))
    sent = jnp.concatenate([last, small])
    sent, even_grads = together(sent, even_grads)
    received = yx_three([sent] * 3)
    results = unit_results(1, even_grads)
    received, grad_in, results = together(received, grad_in, results)
    last = attention_join([last] + [block[:rest] for block in received])
    small_received = [block[rest:] for block in received]
    last, own_grads, small_received, results = together(last, own_grads, small_received, results)
    received = over("c", last)
    up_grads, down_grads = unit_results(0, own_grads, *results)
    small = four(small, small_received)
    received, up_grads, down_grads, small = together(received, up_grads, down_grads, small)
    first_grads = attention_out(last, received)

    gain_grads = small[0:4].reshape(layer_count, 2, width)
    shift_grads = small[4:8].reshape(layer_count, 2, width)
    output_bias_grads, down_bias_grads = small[8:10], small[10:12]
    up_bias_rows = small[12:20].reshape(layer_count, -1)
    input_bias_rows = small[20:24].reshape(layer_count, 2, width)

    def z_part(array, size):
        return lax.dynamic_slice_in_dim(array, z_place * size, size, axis=-1)

    return (
        layer_out,
        grad_in,
        gain_grads,
        shift_grads,
        jnp.stack([first_grads[0], later_grads[0]]),
        z_part(input_bias_rows, shard),
        jnp.stack([first_grads[1], later_grads[1]]),
        output_bias_grads,
        up_grads,
        z_part(up_bias_rows, unit_shard),
        down_grads,
        down_bias_grads,
    )


def solution(mesh):
    split = mesh.shape["dp"] // 8
    fine = Mesh(
        mesh.devices.reshape(split, 2, 2, 2, mesh.shape["tensor"]), ("o", "y", "x", "c", "z")
    )
    rows = P(("o", "y", "x", "c", "z"), None)
    placed = (
        rows,
        P(("o", "y", "x", "c")),
        P(),
        P(),
        P(None, None, None, "z"),
        P(None, None, "z"),
        P(None, "z", None),
        P(),
        P(None, None, "z"),
        P(None, "z"),
        P(None, "z", None),
        P(),
        rows,
    )
    return jax.shard_map(
        local,
        mesh=fine,
        in_specs=placed,
        out_specs=(rows, rows) + placed[2:12],
        check_vma=False,
    )
```

```python
import functools

import jax
import jax.numpy as jnp
from jax import lax
from jax.experimental import pallas as pl
from jax.experimental.pallas import tpu as pltpu
from jax.sharding import Mesh, PartitionSpec as P

HD = 64
ROWS = 1024
IMAGE = 240

epsilon = 1e-06
masked_score = -1e30
bf16 = jnp.bfloat16
f32 = jnp.float32


def dot(left, right, contract):
    return lax.dot_general(
        left, right, ((contract[:1], contract[1:]), ((), ())), preferred_element_type=f32
    )


def kernel_cost(seconds):
    return pl.CostEstimate(
        flops=int(1.1535e15 * seconds), bytes_accessed=int(3.69e12 * seconds), transcendentals=0
    )


def normalize(values, gain_row, bias_row):
    average = jnp.mean(values, axis=-1, keepdims=True)
    centred = values - average
    variance = jnp.mean(centred * centred, axis=-1, keepdims=True)
    return centred * lax.rsqrt(variance + epsilon) * gain_row + bias_row


def gelu_pair(values):
    size = jnp.abs(values)
    knot = 1.0 / (1.0 + (0.3275911 * 0.5**0.5) * size)
    bell = jnp.exp(values * values * -0.5)
    series = knot * (
        0.127414796
        + knot * (-0.142248368 + knot * (0.7107068705 + knot * (-0.7265760135 + knot * 0.5307027145)))
    )
    tail = series * bell
    normal = jnp.where(values > 0, 1.0 - tail, tail)
    return values * normal, normal + values * bell * 0.3989422804014327


def key_halves(core, own, received):
    first = jnp.where(core == 0, own, received)
    second = jnp.where(core == 0, received, own)
    return first, second


def attend_forward_kernel(info, queries, kv_own, kv_other, mixed, log_total):
    core, valid = info[0], info[1]
    width = queries.shape[0]
    half = kv_own.shape[1]
    key_place = lax.broadcasted_iota(jnp.int32, (half, 1), 0) + half
    key_bias = jnp.where(key_place < valid, 0.0, masked_score).astype(f32)
    for head in range(width // HD):
        rows = slice(head * HD, (head + 1) * HD)
        value_rows = slice(width + head * HD, width + (head + 1) * HD)
        query = queries[rows, :] * jnp.asarray(HD**-0.5, bf16)
        key_one, key_two = key_halves(core, kv_own[rows, :], kv_other[rows, :])
        value_one, value_two = key_halves(core, kv_own[value_rows, :], kv_other[value_rows, :])
        score_one = dot(key_one, query, (0, 0))
        score_two = dot(key_two, query, (0, 0)) + key_bias
        top = jnp.maximum(
            jnp.max(score_one, axis=0, keepdims=True), jnp.max(score_two, axis=0, keepdims=True)
        )
        weight_one = jnp.exp(score_one - top)
        weight_two = jnp.exp(score_two - top)
        total = jnp.sum(weight_one, axis=0, keepdims=True) + jnp.sum(
            weight_two, axis=0, keepdims=True
        )
        out = dot(value_one, weight_one.astype(bf16), (1, 0)) + dot(
            value_two, weight_two.astype(bf16), (1, 0)
        )
        mixed[rows, :] = (out / total).astype(bf16)
        log_total[0, head : head + 1, :] = top + jnp.log(total)


def attend_backward_kernel(
    info, queries, kv_own, kv_other, mixed, log_total, grad_mixed, grad_q, grad_own, grad_other
):
    core, valid = info[0], info[1]
    width = queries.shape[0]
    half = kv_own.shape[1]
    scale = HD**-0.5
    key_place = lax.broadcasted_iota(jnp.int32, (half, 1), 0) + half
    key_bias = jnp.where(key_place < valid, 0.0, masked_score).astype(f32)
    for head in range(width // HD):
        rows = slice(head * HD, (head + 1) * HD)
        value_rows = slice(width + head * HD, width + (head + 1) * HD)
        query = queries[rows, :] * jnp.asarray(scale, bf16)
        grad_out = grad_mixed[rows, :]
        delta = jnp.sum(
            grad_out.astype(f32) * mixed[rows, :].astype(f32), axis=0, keepdims=True
        )
        log_row = log_total[0, head : head + 1, :]
        keys = key_halves(core, kv_own[rows, :], kv_other[rows, :])
        values = key_halves(core, kv_own[value_rows, :], kv_other[value_rows, :])
        grad_query = None
        grad_keys = []
        grad_values = []
        for part in range(2):
            score = dot(keys[part], query, (0, 0))
            if part == 1:
                score = score + key_bias
            probs = jnp.exp(score - log_row)
            grad_values.append(dot(grad_out, probs.astype(bf16), (1, 1)))
            grad_probs = dot(values[part], grad_out, (0, 0))
            grad_score = (probs * (grad_probs - delta)).astype(bf16)
            term = dot(keys[part], grad_score, (1, 0))
            grad_query = term if grad_query is None else grad_query + term
            grad_keys.append(dot(query, grad_score, (1, 1)))
        grad_q[rows, :] = (grad_query * scale).astype(bf16)
        own, other = key_halves(core, *grad_keys)
        grad_own[rows, :] = own
        grad_other[rows, :] = other.astype(bf16)
        own, other = key_halves(core, *grad_values)
        grad_own[value_rows, :] = own
        grad_other[value_rows, :] = other.astype(bf16)


def attention_specs(groups, width, half):
    return dict(
        q=pl.BlockSpec((width, half), lambda g, info: (g, 0)),
        kv=pl.BlockSpec((2 * width, half), lambda g, info: (g, 0)),
        log=pl.BlockSpec((1, 8, half), lambda g, info: (g, 0, 0)),
    )


def attend_forward(info, queries, kv_own, kv_other, groups):
    features, half = queries.shape
    width = features // groups
    specs = attention_specs(groups, width, half)
    return pl.pallas_call(
        attend_forward_kernel,
        grid_spec=pltpu.PrefetchScalarGridSpec(
            num_scalar_prefetch=1,
            grid=(groups,),
            in_specs=[specs["q"], specs["kv"], specs["kv"]],
            out_specs=[specs["q"], specs["log"]],
        ),
        out_shape=[
            jax.ShapeDtypeStruct((features, half), bf16),
            jax.ShapeDtypeStruct((groups, 8, half), f32),
        ],
        compiler_params=pltpu.CompilerParams(vmem_limit_bytes=40 << 20),
        cost_estimate=kernel_cost(14e-6),
        name="attend_forward",
    )(info, queries, kv_own, kv_other)


def attend_backward(info, queries, kv_own, kv_other, mixed, log_total, grad_mixed, groups):
    features, half = queries.shape
    width = features // groups
    specs = attention_specs(groups, width, half)
    return pl.pallas_call(
        attend_backward_kernel,
        grid_spec=pltpu.PrefetchScalarGridSpec(
            num_scalar_prefetch=1,
            grid=(groups,),
            in_specs=[specs["q"], specs["kv"], specs["kv"], specs["q"], specs["log"], specs["q"]],
            out_specs=[specs["q"], specs["kv"], specs["kv"]],
        ),
        out_shape=[
            jax.ShapeDtypeStruct((features, half), bf16),
            jax.ShapeDtypeStruct((2 * features, half), f32),
            jax.ShapeDtypeStruct((2 * features, half), bf16),
        ],
        compiler_params=pltpu.CompilerParams(vmem_limit_bytes=40 << 20),
        cost_estimate=kernel_cost(21e-6),
        name="attend_backward",
    )(info, queries, kv_own, kv_other, mixed, log_total, grad_mixed)


def stream_pieces(pieces, buffer, arrived):
    step = pl.program_id(0)
    rows = buffer.shape[1]

    def copy(index):
        source, offset = pieces[index]
        return pltpu.make_async_copy(
            source.at[pl.ds(offset, rows), :], buffer.at[index % 2], arrived.at[index % 2]
        )

    @pl.when(step == 0)
    def _():
        copy(0).start()

    for index in range(len(pieces) - 1):

        @pl.when(step == index)
        def _(index=index):
            copy(index + 1).start()

    for index in range(len(pieces)):

        @pl.when(step == index)
        def _(index=index):
            copy(index).wait()

    return lax.rem(step, 2)


def list_pieces(refs, rows):
    return [(ref, start) for ref in refs for start in range(0, ref.shape[0], rows)]


def units_forward_kernel(count, rows, normed, middle, unit_bias, down_bias, *refs):
    weights = refs[:count]
    activated, slopes, result, buffer, arrived = refs[count:]
    slot = stream_pieces(list_pieces(weights, rows), buffer, arrived)
    width = normed.shape[1]

    @pl.when(pl.program_id(0) == 0)
    def _():
        result[...] = middle[...] + down_bias[...]

    size = normed.shape[0] // 2
    for start in range(0, 2 * size, size):
        part = slice(start, start + size)
        pre = dot(normed[part, :], buffer[slot, :, :width], (1, 1)) + unit_bias[0]
        act, slope = gelu_pair(pre)
        act = act.astype(bf16)
        activated[part, :] = act
        slopes[part, :] = slope.astype(bf16)
        result[part, :] += dot(act, buffer[slot, :, width:], (1, 0))


def units_forward(normed, middle, unit_bias, down_bias, weights):
    tokens, width = normed.shape
    rows = unit_bias.shape[1]
    steps = unit_bias.shape[0]
    units = rows * steps
    whole = pl.BlockSpec((tokens, width), lambda i: (0, 0))
    block = pl.BlockSpec((tokens, rows), lambda i: (0, i))
    return pl.pallas_call(
        functools.partial(units_forward_kernel, len(weights), rows),
        grid=(steps,),
        in_specs=[
            whole,
            whole,
            pl.BlockSpec((1, 1, rows), lambda i: (i, 0, 0)),
            pl.BlockSpec((1, width), lambda i: (0, 0)),
        ]
        + [pl.BlockSpec(memory_space=pl.ANY)] * len(weights),
        out_specs=[block, block, whole],
        out_shape=[
            jax.ShapeDtypeStruct((tokens, units), bf16),
            jax.ShapeDtypeStruct((tokens, units), bf16),
            jax.ShapeDtypeStruct((tokens, width), f32),
        ],
        scratch_shapes=[
            pltpu.VMEM((2, rows, 2 * width), bf16),
            pltpu.SemaphoreType.DMA((2,)),
        ],
        compiler_params=pltpu.CompilerParams(vmem_limit_bytes=40 << 20),
        cost_estimate=kernel_cost(17e-6),
        name="units_forward",
    )(normed, middle, unit_bias[:, None, :], down_bias, *weights)


def stream_blocks(place, source, buffer, arrived):
    step = pl.program_id(0)
    rows = buffer.shape[1]

    def copy(index):
        offset = pl.multiple_of(place[index] * rows, rows)
        slot = lax.rem(index, 2)
        return pltpu.make_async_copy(
            source.at[pl.ds(offset, rows), :], buffer.at[slot], arrived.at[slot]
        )

    @pl.when(step == 0)
    def _():
        copy(0).start()

    @pl.when(step + 1 < pl.num_programs(0))
    def _():
        copy(step + 1).start()

    copy(step).wait()
    return lax.rem(step, 2)


def units_backward_kernel(count, rows, place, grad_down, normed, activated, slopes, *refs):
    weights = refs[:count]
    sent, kept, grad_normed, bias_grad, buffer, arrived = refs[count:]
    step = pl.program_id(0)
    if count == 1:
        slot = stream_blocks(place, weights[0], buffer, arrived)
    else:
        slot = stream_pieces(list_pieces(weights, rows), buffer, arrived)
    width = normed.shape[1]
    grad_act = dot(grad_down[...], buffer[slot, :, width:], (1, 1))
    grad_hidden = grad_act * slopes[...].astype(f32)
    bias_grad[0] = jnp.sum(grad_hidden, axis=0, keepdims=True)
    grad_hidden = grad_hidden.astype(bf16)

    @pl.when(step == 0)
    def _():
        grad_normed[...] = jnp.zeros_like(grad_normed)

    grad_normed[...] += dot(grad_hidden, buffer[slot, :, :width], (1, 0))
    up = dot(grad_hidden, normed[...], (0, 0)).astype(bf16)
    down = dot(activated[...], grad_down[...], (0, 0)).astype(bf16)

    def store(target):
        target[:, :width] = up
        target[:, width:] = down

    half = pl.num_programs(0) // 2
    pl.when(step < half)(lambda: store(sent))
    pl.when(step >= half)(lambda: store(kept))


def units_backward(place, grad_down, normed, activated, slopes, weights, rows):
    tokens, width = normed.shape
    units = activated.shape[1]
    steps = units // rows
    half = steps // 2
    whole = pl.BlockSpec((tokens, width), lambda i, place: (0, 0))
    block = pl.BlockSpec((tokens, rows), lambda i, place: (0, place[i]))
    return pl.pallas_call(
        functools.partial(units_backward_kernel, len(weights), rows),
        grid_spec=pltpu.PrefetchScalarGridSpec(
            num_scalar_prefetch=1,
            grid=(steps,),
            in_specs=[whole, whole, block, block]
            + [pl.BlockSpec(memory_space=pl.ANY)] * len(weights),
            out_specs=[
                pl.BlockSpec((rows, 2 * width), lambda i, place: (jnp.minimum(i, half - 1), 0)),
                pl.BlockSpec((rows, 2 * width), lambda i, place: (jnp.maximum(i - half, 0), 0)),
                whole,
                pl.BlockSpec((1, 1, rows), lambda i, place: (place[i], 0, 0)),
            ],
            scratch_shapes=[
                pltpu.VMEM((2, rows, 2 * width), bf16),
                pltpu.SemaphoreType.DMA((2,)),
            ],
        ),
        out_shape=[jax.ShapeDtypeStruct((units // 2, 2 * width), bf16)] * 2
        + [
            jax.ShapeDtypeStruct((tokens, width), f32),
            jax.ShapeDtypeStruct((steps, 1, rows), f32),
        ],
        compiler_params=pltpu.CompilerParams(vmem_limit_bytes=40 << 20),
        cost_estimate=kernel_cost(20e-6),
        name="units_backward",
    )(place, grad_down, normed, activated, slopes, *weights)


def norm_backward_kernel(last, values, grad, kept, gain, *refs):
    if last:
        earlier, others, result, packed, sums = refs[:3], refs[3], *refs[4:]
    else:
        result, low, sums = refs
    step = pl.program_id(0)
    block = values[...]
    average = jnp.mean(block, axis=-1, keepdims=True)
    centred = block - average
    scale = lax.rsqrt(jnp.mean(centred * centred, axis=-1, keepdims=True) + epsilon)
    unit = centred * scale
    down = grad[...]
    inner = down * gain[...]
    total = kept[...] + scale * (
        inner
        - jnp.mean(inner, axis=-1, keepdims=True)
        - unit * jnp.mean(inner * unit, axis=-1, keepdims=True)
    )
    result[...] = total

    @pl.when(step == 0)
    def _():
        sums[...] = jnp.zeros_like(sums)

    sums[0:1, :] += jnp.sum(down * unit, axis=0, keepdims=True)
    sums[1:2, :] += jnp.sum(down, axis=0, keepdims=True)
    if not last:
        rounded = total.astype(bf16)
        low[...] = rounded
        sums[2:3, :] += jnp.sum(rounded.astype(f32), axis=0, keepdims=True)
    else:

        @pl.when(step == pl.num_programs(0) - 1)
        def _():
            rows = [sums[0:1, :], earlier[2][0:1, :], earlier[1][0:1, :], earlier[0][0:1, :]]
            rows += [sums[1:2, :], earlier[2][1:2, :], earlier[1][1:2, :], earlier[0][1:2, :]]
            rows += [earlier[2][2:3, :], earlier[0][2:3, :], earlier[1][2:3, :]]
            rows += [others[0:1, :], others[7:11, :], others[1:5, :]]
            rows = jnp.concatenate(rows + [others[11:13, :], others[5:7, :]])
            high = rows.astype(bf16)
            packed[0 : rows.shape[0], :] = high
            packed[rows.shape[0] :, :] = (rows - high.astype(f32)).astype(bf16)


def norm_backward(values, grad, kept, gain, *rows):
    tokens, width = values.shape
    steps = 4
    block = pl.BlockSpec((tokens // steps, width), lambda i: (i, 0))

    def whole(count):
        return pl.BlockSpec((count, width), lambda i: (0, 0))

    last = bool(rows)
    if last:
        count = 2 * (11 + rows[-1].shape[0])
        out_specs = [block, whole(count)]
        out_shape = [
            jax.ShapeDtypeStruct((tokens, width), f32),
            jax.ShapeDtypeStruct((count, width), bf16),
        ]
        scratch = [pltpu.VMEM((8, width), f32)]
    else:
        out_specs = [block, block, whole(8)]
        out_shape = [
            jax.ShapeDtypeStruct((tokens, width), f32),
            jax.ShapeDtypeStruct((tokens, width), bf16),
            jax.ShapeDtypeStruct((8, width), f32),
        ]
        scratch = []
    return pl.pallas_call(
        functools.partial(norm_backward_kernel, last),
        grid=(steps,),
        in_specs=[block, block, block, whole(1)] + [whole(row.shape[0]) for row in rows],
        out_specs=out_specs,
        out_shape=out_shape,
        scratch_shapes=scratch,
        compiler_params=pltpu.CompilerParams(vmem_limit_bytes=24 << 20),
        cost_estimate=kernel_cost(3e-6),
        name="norm_backward",
    )(values, grad, kept, gain, *rows)


def unit_results_kernel(grads, *refs):
    up, down = refs[-2:]
    width = down.shape[2]
    up[0] = grads[:, :width].astype(f32).T
    down[0] = grads[:, width:].astype(f32)


def unit_results(layer, grads, *started):
    units, double = grads.shape
    width = double // 2
    steps = 3
    rows = units // steps
    return pl.pallas_call(
        unit_results_kernel,
        grid=(steps,),
        in_specs=[pl.BlockSpec((rows, double), lambda i: (i, 0))]
        + [pl.BlockSpec(memory_space=pl.ANY)] * len(started),
        out_specs=[
            pl.BlockSpec((1, width, rows), lambda i: (layer, 0, i)),
            pl.BlockSpec((1, rows, width), lambda i: (layer, i, 0)),
        ],
        out_shape=[
            jax.ShapeDtypeStruct((2, width, units), f32),
            jax.ShapeDtypeStruct((2, units, width), f32),
        ],
        input_output_aliases={1 + k: k for k in range(len(started))},
        compiler_params=pltpu.CompilerParams(vmem_limit_bytes=24 << 20),
        cost_estimate=kernel_cost(3e-6),
        name="unit_results",
    )(grads, *started)


flip_pair = [(0, 1), (1, 0)]


def over(axis, array):
    return lax.ppermute(array, axis, flip_pair)


def z_send(array, pairs):
    return lax.ppermute(array, "z", pairs)


def z_pairs(step):
    return [(z, z ^ step) for z in range(4)]


def z_three(blocks):
    return [lax.ppermute(block, "z", z_pairs(step + 1)) for step, block in enumerate(blocks)]


def yx_three(blocks):
    across = [(place, 3 - place) for place in range(4)]
    return [
        over("x", blocks[0]),
        over("y", blocks[1]),
        lax.ppermute(blocks[2], ("y", "x"), across),
    ]


def add_low(*terms):
    total = terms[0].astype(f32)
    for term in terms[1:]:
        total = total + term.astype(f32)
    return total.astype(bf16)


def together(*arrays):
    return lax.optimization_barrier(arrays)


def tie(array, *after):
    return lax.optimization_barrier((array, after))[0]


def flip_if(bit, array, axis):
    return jnp.where(bit == 1, jnp.flip(array, axis), array)


def paired(bit, own, received, axis):
    return jnp.stack(
        [jnp.where(bit == 0, own, received), jnp.where(bit == 0, received, own)], axis=axis
    )


def local(
    stream_in,
    patch_size,
    norm_gain,
    norm_bias,
    input_weight,
    input_bias,
    output_weight,
    output_bias,
    up_weight,
    up_bias,
    down_weight,
    down_bias,
    cotangent,
):
    half, width_all = stream_in.shape
    layer_count = input_weight.shape[0]
    shard = input_weight.shape[-1]
    unit_shard = up_weight.shape[-1]
    unit_slice = unit_shard // 8
    groups = lax.axis_size("z")
    outer = lax.axis_size("o")
    core, x_bit, y_bit = lax.axis_index("c"), lax.axis_index("x"), lax.axis_index("y")
    z_place = lax.axis_index("z")
    z_low, z_high = z_place % 2, z_place // 2

    swap = []
    for c in range(2):
        for z in range(groups):
            if c != z % 2:
                swap.append((c * groups + z, (z % 2) * groups + (z - z % 2 + c)))

    def swap_rows(array):
        return jnp.where(z_low == core, array, lax.ppermute(array, ("c", "z"), swap))

    other_patch = over("c", patch_size)
    patch = jnp.where(z_low == core, patch_size, other_patch)
    patch = jnp.where(z_high == 0, patch[0], patch[1])
    grid_side = IMAGE // patch
    valid = grid_side * grid_side
    info = jnp.stack([core, valid]).astype(jnp.int32)

    stream_rows = swap_rows(stream_in)

    def z_order(array):
        pairs = array.reshape((2, 2) + array.shape[1:])
        pairs = flip_if(z_high, flip_if(z_low, pairs, 1), 0)
        return pairs.reshape(array.shape)

    def unit_flip(cut):
        cut = flip_if(z_high, flip_if(z_low, cut, 1), 0)
        return flip_if(y_bit, flip_if(x_bit, flip_if(core, cut, 4), 3), 2)

    def own_order(rows):
        cut = unit_flip(rows.reshape(2, 2, 2, 2, 2, unit_slice))
        cut = jnp.stack([cut[0].transpose(3, 1, 2, 0, 4), cut[1].transpose(3, 2, 1, 0, 4)], axis=1)
        return cut[::-1].reshape(8, unit_shard // 2)

    def own_order_back(pieces):
        cut = pieces.reshape(2, 2, 2, 2, 2, unit_slice)[::-1]
        cut = jnp.stack([cut[:, 0].transpose(3, 1, 2, 0, 4), cut[:, 1].transpose(3, 2, 1, 0, 4)])
        return unit_flip(cut).reshape(groups, unit_shard)

    def even_order(rows):
        cut = rows.reshape(groups, 8, unit_slice).transpose(1, 0, 2)
        return cut.reshape(8, unit_shard // 2)

    def even_order_back(pieces):
        cut = pieces.reshape(8, groups, unit_slice).transpose(1, 0, 2)
        return cut.reshape(groups, unit_shard)

    slice_index = (y_bit * 2 + x_bit) * 2 + core

    part = shard // 2

    def attention_slice(layer_idx):
        first = jnp.where(core == 0, input_weight[layer_idx, 1], input_weight[layer_idx, 0]).T
        second = jnp.where(core == 0, input_weight[layer_idx, 2].T, output_weight[layer_idx])
        return jnp.concatenate(
            [
                lax.dynamic_slice_in_dim(first, x_bit * part, part, axis=0),
                lax.dynamic_slice_in_dim(second, y_bit * part, part, axis=0),
            ]
        )

    def attention_halves(blocks):
        return (
            jnp.stack([block[:part] for block in blocks]),
            jnp.stack([block[part : 2 * part] for block in blocks]),
        )

    def attention_own(first, second, received):
        first = paired(x_bit, first, received[0], 1).reshape(groups, shard, width_all)
        second = paired(y_bit, second, received[1], 1).reshape(groups, shard, width_all)
        return jnp.stack([first, second], axis=1)

    def attention_whole(own):
        received = over("c", own)
        kv = jnp.where(core == 0, own, received)
        qo = jnp.where(core == 0, received, own)
        return (
            kv.reshape(2 * groups * shard, width_all),
            qo[:, 0].reshape(groups * shard, width_all),
            qo[:, 1].reshape(groups * shard, width_all),
        )

    def unit_block(layer_idx):
        up = lax.dynamic_slice_in_dim(
            up_weight[layer_idx], slice_index * unit_slice, unit_slice, axis=1
        )
        down = lax.dynamic_slice_in_dim(
            down_weight[layer_idx], slice_index * unit_slice, unit_slice, axis=0
        )
        return jnp.concatenate([up.T, down], axis=1)

    small_bias = input_bias.reshape(-1, unit_shard)
    bias_count = layer_count + small_bias.shape[0]
    bias_rows = jnp.pad(up_bias, ((0, 16 - layer_count), (0, 0))) + jnp.pad(
        small_bias, ((layer_count, 16 - bias_count), (0, 0))
    )
    everyone = ("y", "x", "c", "z")
    block = jnp.concatenate([attention_slice(0), bias_rows])
    first_blocks = z_three([block] * 3)
    blocks = [block] + first_blocks
    biases = jnp.stack([block[2 * part :] for block in blocks]).astype(f32)
    first, second = attention_halves(blocks)
    own_attention = attention_own(first, second, [over("x", first), over("y", second)])
    block = tie(unit_block(0), first, second)
    unit_blocks = z_three([block] * 3)
    first_weights = attention_whole(own_attention)
    one = tie(jnp.concatenate([block, unit_blocks[0]]), first_weights[0])
    two = tie(jnp.concatenate(unit_blocks[1:]), first_weights[0])
    one = jnp.concatenate([one, over("x", one)])
    two = jnp.concatenate([two, over("y", two)])
    near_units = [over("y", one), over("x", two)]
    even_units = lax.all_gather(
        tie(unit_block(1), *first_blocks), everyone, axis=0, tiled=True
    )
    attention_weights = [first_weights, None]
    unit_weights = [None, [even_units]]
    up_bias_all = z_order(biases[:, :layer_count])
    input_bias_all = biases[:, layer_count : layer_count + input_bias.size // unit_shard].reshape(
        groups, layer_count, 2, shard
    )
    gains = norm_gain.astype(f32)
    shifts = norm_bias.astype(f32)

    stream = stream_rows.astype(f32)
    saved = []
    for layer_idx in range(layer_count):
        if layer_idx == 1:
            attention_weights[1] = attention_whole(own_attention)
        weight_kv, weight_q, weight_o = attention_weights[layer_idx]
        layer_input = stream
        normed = normalize(stream, gains[layer_idx, 0], shifts[layer_idx, 0]).astype(bf16)
        value_bias = input_bias_all[:, layer_idx, 1]
        kv_bias = jnp.stack([jnp.zeros_like(value_bias), value_bias], axis=1).reshape(-1, 1)
        kv_own = (dot(weight_kv, normed, (1, 1)) + kv_bias).astype(bf16)
        if layer_idx == 0:
            later_block = tie(attention_slice(1), kv_own)
            later_blocks = z_three([later_block] * 3)
        kv_other = over("c", kv_own)
        query_bias = input_bias_all[:, layer_idx, 0].reshape(-1, 1)
        queries = (dot(weight_q, normed, (1, 1)) + query_bias).astype(bf16)
        mixed, log_total = attend_forward(info, queries, kv_own, kv_other, groups)
        if layer_idx == 0:
            mixed, log_total, near_units, later_blocks = together(
                mixed, log_total, near_units, later_blocks
            )
            pieces = [one, near_units[0], two, near_units[1]]
            unit_weights[0] = [over("c", piece) for piece in pieces] + pieces
            first, second = attention_halves([later_block, *later_blocks])
        middle = stream + (
            dot(mixed, weight_o, (0, 0)) + output_bias[layer_idx].astype(f32)
        )
        normed_two = normalize(middle, gains[layer_idx, 1], shifts[layer_idx, 1]).astype(bf16)
        order = own_order if layer_idx == 0 else even_order
        if layer_idx == 0:
            unit_weights[0], normed_two, first, second = together(
                unit_weights[0], normed_two, first, second
            )
            received = [over("x", first), over("y", second)]
            cotangent_rows = swap_rows(tie(cotangent, first, second))
        activated, slopes, stream = units_forward(
            normed_two,
            middle,
            order(up_bias_all[:, layer_idx]).reshape(8 if layer_idx == 0 else 4, -1),
            down_bias[layer_idx].astype(f32)[None, :],
            unit_weights[layer_idx],
        )
        if layer_idx == 0:
            activated, slopes, stream, received, cotangent_rows = together(
                activated, slopes, stream, received, cotangent_rows
            )
            own_attention = attention_own(first, second, received)
        saved.append(
            (
                layer_input,
                middle,
                normed,
                queries,
                kv_own,
                kv_other,
                log_total,
                mixed,
                normed_two,
                slopes,
                activated,
            )
        )
    layer_rows = stream.astype(bf16)

    row_place = core * half + jnp.arange(half, dtype=jnp.int32)
    row_mask = (row_place < valid).astype(f32)[:, None]
    grad_stream = cotangent_rows.astype(f32) * row_mask

    slab = (4, unit_shard // 2, 2 * width_all)
    strip = unit_shard // 4
    thin = (2, unit_slice, 2 * width_all)

    def own_first(kept, received):
        kept, received = kept.reshape(slab), received.reshape(slab)
        parts = [add_low(kept[k], received[k]) for k in range(4)]
        return [parts[0], parts[2]], [parts[1], parts[3]]

    def even_first(kept, received):
        kept, received = kept.reshape(slab), received.reshape(slab)

        def part(rows, blocks):
            return add_low(
                jnp.concatenate([kept[k, rows] for k in blocks]),
                jnp.concatenate([received[k, rows] for k in blocks]),
            )

        one, two = slice(0, strip), slice(strip, 2 * strip)
        return [part(one, (0, 1)), part(two, (0, 2))], [part(one, (2, 3)), part(two, (1, 3))]

    def unit_second(parts, received):
        kept, sent = [], []
        for part, other in zip(parts, received):
            kept.append(add_low(part[:strip], other[:strip]).reshape(thin))
            sent.append(add_low(part[strip:], other[strip:]).reshape(thin))
        return kept, sent

    def own_third(parts, received):
        one, two = [add_low(*pair) for pair in zip(parts, received)]
        return [one[0], one[1], two[0], two[1]]

    def even_third(parts, received):
        total = jnp.concatenate([add_low(*pair) for pair in zip(parts, received)])
        return [
            lax.dynamic_index_in_dim(total, z_place ^ step, axis=0, keepdims=False)
            for step in range(4)
        ]

    def over_outer(total):
        return lax.psum(total, "o") if outer > 1 else total

    def gather_shard(total):
        return lax.all_gather(total, everyone[:3], axis=0, tiled=True)

    def attention_parts(grad_kv, grad_q, grad_o):
        kv = grad_kv.reshape(groups, 2, shard, width_all)
        qo = jnp.stack(
            [
                grad_q.reshape(groups, shard, width_all),
                grad_o.reshape(groups, shard, width_all),
            ],
            axis=1,
        )
        sent = jnp.where(core == 0, qo, kv)
        kept = jnp.where(core == 0, kv, qo)
        return sent, kept

    quarter = shard // 4
    rest = 2 * quarter

    def attention_first(total):
        cut = total.reshape(groups, 2, 2, 2, quarter, width_all)
        one, two = cut[:, 0], cut[:, 1]

        def pick(array, index, axis):
            return lax.dynamic_index_in_dim(array, index, axis, keepdims=False)

        kept = [pick(one, y_bit, 1), pick(two, x_bit, 2)]
        return kept, [pick(one, 1 - y_bit, 1), pick(two, 1 - x_bit, 2)]

    def attention_second(parts, received):
        kept, sent = [], []
        for part, other, bit in zip(parts, received, (x_bit, y_bit)):
            total = add_low(part, other)
            kept.append(lax.dynamic_index_in_dim(total, bit, 1, keepdims=False))
            sent.append(lax.dynamic_index_in_dim(total, 1 - bit, 1, keepdims=False))
        return kept, sent

    def attention_third(parts, received):
        total = jnp.concatenate([add_low(*pair) for pair in zip(parts, received)], axis=1)
        return [total[step] for step in range(4)]

    def attention_gathered(rows):
        cut = rows.reshape(4, 2, 2, quarter, width_all).transpose(1, 2, 0, 3, 4).astype(f32)
        cut = cut.reshape(2, 2, shard, width_all)
        weight_in = jnp.stack([cut[1, 0], cut[0, 0], cut[0, 1]])
        return jnp.swapaxes(weight_in, 1, 2), cut[1, 1]

    def attention_out(whole, received):
        cut = (2, shard, width_all)
        total = paired(core, whole.reshape(cut), received.reshape(cut), 0).astype(f32)
        weight_in = jnp.stack([total[1, 0], total[0, 0], total[0, 1]])
        return jnp.swapaxes(weight_in, 1, 2), total[1, 1]

    def attention_cuts(kept, received):
        place = y_bit * 2 + x_bit

        def cut(array, step):
            return lax.dynamic_slice_in_dim(array, (place ^ step) * quarter, quarter, axis=2)

        return [add_low(cut(kept, step), cut(received, step)) for step in range(4)]

    def attention_sum(cuts, received):
        return add_low(cuts[0], *received).reshape(4, rest, width_all)

    def attention_join(blocks):
        whole = jnp.stack(blocks).reshape(2, 2, 2, quarter, width_all)
        whole = flip_if(y_bit, flip_if(x_bit, whole, 1), 0)
        return whole.transpose(2, 0, 1, 3, 4).reshape(2 * shard, width_all)

    def pack(rows):
        high = rows.astype(bf16)
        low = (rows - lax.optimization_barrier(high).astype(f32)).astype(bf16)
        return lax.optimization_barrier(jnp.concatenate([high, low]))

    def unpack(rows):
        count = rows.shape[0] // 2
        return rows[:count].astype(f32) + rows[count:].astype(f32)

    def four(own, received):
        one, two, three = received
        return (unpack(own) + unpack(one)) + (unpack(two) + unpack(three))

    grad_down = grad_stream.astype(bf16)
    other_rows = [jnp.sum(grad_down.astype(f32), axis=0, keepdims=True)]
    sum_rows = []
    for layer_idx in reversed(range(layer_count)):
        (
            layer_input,
            middle,
            normed,
            queries,
            kv_own,
            kv_other,
            log_total,
            mixed,
            normed_two,
            slopes,
            activated,
        ) = saved[layer_idx]
        weight_kv, weight_q, weight_o = attention_weights[layer_idx]
        first = layer_idx == 0
        steps = jnp.arange(8, dtype=jnp.int32)
        if first:
            place = steps
            later, later_sent = attention_first(add_low(attention_kept, attention_received))
            even_cuts = even_third(unit_parts, unit_received)
            grad_down, later, later_sent, even_cuts = together(
                grad_down, later, later_sent, even_cuts
            )
            later_received = [over("y", later_sent[0]), over("x", later_sent[1])]
            even_received = z_three(even_cuts[1:])
        else:
            place = slice_index ^ ((steps % 4) * 2 + (1 - steps // 4))
        grads = units_backward(
            place,
            grad_down,
            normed_two,
            activated,
            slopes,
            unit_weights[layer_idx],
            unit_shard // 2,
        )
        if first:
            grads, later_received, even_received = together(grads, later_received, even_received)
            later, later_sent = attention_second(later, later_received)
            even_total = over_outer(add_low(even_cuts[0], *even_received))
            grads, later, later_sent, even_total = together(grads, later, later_sent, even_total)
            later_received = [over("x", later_sent[0]), over("y", later_sent[1])]
            even_grads = gather_shard(even_total)
        unit_sent, unit_kept, grad_normed_two, up_bias_grad = grads
        unit_received = over("c", unit_sent)
        order_back = own_order_back if first else even_order_back
        other_rows.append(order_back(up_bias_grad))
        grad_middle, grad_branch, rows = norm_backward(
            middle, grad_normed_two, grad_stream, gains[layer_idx, 1][None, :]
        )
        sum_rows.append(rows)
        grad_o = dot(mixed, grad_branch, (1, 0)).astype(bf16)
        grad_mixed = dot(weight_o, grad_branch, (1, 1)).astype(bf16)
        grad_mixed, grad_o, unit_received = together(grad_mixed, grad_o, unit_received)
        unit_parts, unit_sent = (own_first if first else even_first)(unit_kept, unit_received)
        if first:
            later_received = tie(later_received, grad_mixed)
            later_cuts = attention_third(later, later_received)
            grad_mixed, unit_parts, unit_sent, later_cuts = together(
                grad_mixed, unit_parts, unit_sent, later_cuts
            )
            later_received = z_three(later_cuts[1:])
        else:
            grad_mixed, unit_parts, unit_sent, layer_rows = together(
                grad_mixed, unit_parts, unit_sent, layer_rows
            )
            layer_out = swap_rows(layer_rows)
        unit_received = [over("y", unit_sent[0]), over("x", unit_sent[1])]
        outs = attend_backward(
            info, queries, kv_own, kv_other, mixed, log_total, grad_mixed, groups
        )
        kv_received = over("c", outs[2])
        outs, unit_received = together(outs[:2], unit_received)
        unit_parts, unit_sent = unit_second(unit_parts, unit_received)
        if first:
            later_received = tie(later_received, outs[0])
            later_total = over_outer(add_low(later_cuts[0], *later_received))
            outs, unit_parts, unit_sent, later_total = together(
                outs, unit_parts, unit_sent, later_total
            )
            later_grads = gather_shard(later_total)
        else:
            outs, unit_parts, unit_sent, layer_out = together(
                outs, unit_parts, unit_sent, layer_out
            )
        unit_received = [over("x", unit_sent[0]), over("y", unit_sent[1])]
        grad_queries, grad_kv_own = outs
        grad_kv = add_low(grad_kv_own, kv_received)
        grad_q = dot(grad_queries, normed, (1, 0)).astype(bf16)
        grad_kv_weight = dot(grad_kv, normed, (1, 0)).astype(bf16)
        attention_sent, attention_kept = attention_parts(grad_kv_weight, grad_q, grad_o)
        attention_received = over("c", attention_sent)
        query_bias_grad = jnp.sum(grad_queries.astype(f32), axis=1)
        value_bias_grad = jnp.sum(
            grad_kv.reshape(groups, 2, shard, half)[:, 1].astype(f32), axis=-1
        )
        other_rows.append(z_order(query_bias_grad.reshape(groups, shard)).reshape(1, -1))
        other_rows.append(z_order(value_bias_grad).reshape(1, -1))
        grad_normed = dot(grad_queries, weight_q, (0, 0)) + dot(grad_kv, weight_kv, (0, 0))
        if first:
            other_rows = jnp.concatenate(other_rows)
            grad_normed, attention_received, unit_received, other_rows = together(
                grad_normed, attention_received, unit_received, other_rows
            )
            cuts = attention_cuts(attention_kept, attention_received)
            unit_cuts = own_third(unit_parts, unit_received)
            grad_normed, cuts, unit_cuts = together(grad_normed, cuts, unit_cuts)
            received = yx_three(cuts[1:])
            unit_received = z_three(unit_cuts[1:])
            grad_stream, small = norm_backward(
                layer_input,
                grad_normed,
                grad_middle,
                gains[layer_idx, 0][None, :],
                *sum_rows,
                other_rows,
            )
        else:
            grad_stream, grad_down, rows = norm_backward(
                layer_input, grad_normed, grad_middle, gains[layer_idx, 0][None, :]
            )
            sum_rows.append(rows)
            grad_stream, grad_down, attention_received, unit_received = together(
                grad_stream, grad_down, attention_received, unit_received
            )
    width = width_all
    small = pack(unpack(small) + unpack(over("c", small)))
    grad_stream, small, received, unit_received = together(
        grad_stream, small, received, unit_received
    )
    last = attention_sum(cuts, received)
    unit_total = over_outer(add_low(unit_cuts[0], *unit_received))
    sent = [jnp.concatenate([last[k], small]) for k in (1, 2, 3)]
    sent, last, unit_total, grad_stream, even_grads, later_grads = together(
        sent, last, unit_total, grad_stream, even_grads, later_grads
    )
    received = z_three(sent)
    own_grads = gather_shard(unit_total)
    grad_in = swap_rows(grad_stream)
    later_grads = attention_gathered(later_grads)
    received, later_grads = together(received, later_grads)
    last = over_outer(add_low(last[0], *[block[:rest] for block in received]))
    small = pack(over_outer(four(small, [block[rest:] for block in received])))
    sent = jnp.concatenate([last, small])
    sent, even_grads = together(sent, even_grads)
    received = yx_three([sent] * 3)
    results = unit_results(1, even_grads)
    received, grad_in, results = together(received, grad_in, results)
    last = attention_join([last] + [block[:rest] for block in received])
    small_received = [block[rest:] for block in received]
    last, own_grads, small_received, results = together(last, own_grads, small_received, results)
    received = over("c", last)
    up_grads, down_grads = unit_results(0, own_grads, *results)
    small = four(small, small_received)
    received, up_grads, down_grads, small = together(received, up_grads, down_grads, small)
    first_grads = attention_out(last, received)

    gain_grads = small[0:4].reshape(layer_count, 2, width)
    shift_grads = small[4:8].reshape(layer_count, 2, width)
    output_bias_grads, down_bias_grads = small[8:10], small[10:12]
    up_bias_rows = small[12:20].reshape(layer_count, -1)
    input_bias_rows = small[20:24].reshape(layer_count, 2, width)

    def z_part(array, size):
        return lax.dynamic_slice_in_dim(array, z_place * size, size, axis=-1)

    return (
        layer_out,
        grad_in,
        gain_grads,
        shift_grads,
        jnp.stack([first_grads[0], later_grads[0]]),
        z_part(input_bias_rows, shard),
        jnp.stack([first_grads[1], later_grads[1]]),
        output_bias_grads,
        up_grads,
        z_part(up_bias_rows, unit_shard),
        down_grads,
        down_bias_grads,
    )


def solution(mesh):
    split = mesh.shape["dp"] // 8
    fine = Mesh(
        mesh.devices.reshape(split, 2, 2, 2, mesh.shape["tensor"]), ("o", "y", "x", "c", "z")
    )
    rows = P(("o", "y", "x", "c", "z"), None)
    placed = (
        rows,
        P(("o", "y", "x", "c")),
        P(),
        P(),
        P(None, None, None, "z"),
        P(None, None, "z"),
        P(None, "z", None),
        P(),
        P(None, None, "z"),
        P(None, "z"),
        P(None, "z", None),
        P(),
        rows,
    )
    return jax.shard_map(
        local,
        mesh=fine,
        in_specs=placed,
        out_specs=(rows, rows) + placed[2:12],
        check_vma=False,
    )
```
